32 devices in a mesh: section: 8 (over y, x, core), tp: 4 (over z).
Axes of the slice: x: 2, y: 2, z: 4, core: 2. Of those that a mesh axis runs over, the one named last changes fastest.
Arguments:
- block_weights: bfloat16 [8, 3072, 4, 2048], P(None, 'section', None, 'tp'), may hold values from -0.109375 to 0.109375
- modulation: float32 [8, 3, 3072], P('section'), may hold values from -4 to 4
- inflow: bfloat16 [8, 512, 3072], P('section', None, 'tp'), may hold values from -6 to 6
- stale_cache: bfloat16 [8, 2, 2048, 2048], P('section', None, None, 'tp'), may hold values from -120 to 120
- patch_index: int32 [8], P('section'), may hold values from 0 to 3
- assignment: int32 [8], replicated, may hold values from 0 to 7, each once
Outputs:
- outflow: bfloat16 [8, 512, 3072], P('section', None, 'tp')
The draws below stay inside these ranges and needn't reach their ends.
All inputs are finite; a program needn't handle non-finite values.
Results may differ from the reference program's by a relative error of at most 0.022.
Values may be sent and summed in bfloat16 or wider, within the bound.
No kernel may reach another device: no remote copies, remote signals or barrier semaphores. Data moves between devices by JAX's collectives and lax.ppermute only.
A program may use at most 128 MiB of HBM per device.

```python
import jax
import jax.numpy as jnp
from jax import lax

D = 3072
HD = 128
HEADS = 16
INNER = 2048
PATCH = 512
SEQ = 2048
BLOCKS = 8
N_TP = 4


def draw_stale_cache(key, part):
    key = jax.random.fold_in(key, 11)
    first_key = jax.random.fold_in(key, 0)
    dims = (BLOCKS, 2, SEQ, INNER)
    scales = jnp.array([1.6, 3.0], jnp.float32).reshape(1, 2, 1, 1)
    drawn = jnp.clip(jax.random.normal(first_key, dims, jnp.float32), -6.0, 6.0)
    return (drawn * scales).astype(jnp.bfloat16)


def place_ends(entries, stream_key, smallest, high):
    longest = entries.shape.index(max(entries.shape))
    spots = []
    for shift in (0, 1):
        where = [jax.random.randint(jax.random.fold_in(stream_key, axis), (), 0, length) for axis, length in enumerate(entries.shape)]
        where[longest] = (where[longest] + shift) % entries.shape[longest]
        spots.append(tuple(where))
    return entries.at[spots[0]].set(smallest).at[spots[1]].set(high)


def level_of(own_key, extent, shards, low, top_value):
    level, own = 1.0, jax.random.fold_in(own_key, 6)
    for position, parts in shards:
        draws = jnp.exp(jax.random.uniform(jax.random.fold_in(own, position), (parts,), jnp.float32, low / len(shards), top_value / len(shards)))
        level = level * jnp.repeat(draws, extent[position] // parts).reshape([-1 if axis == position else 1 for axis in range(len(extent))])
    return level


def gaussian(own_key, shape, scale, bound, shards=(), kind=jnp.bfloat16):
    values = jax.random.normal(own_key, shape, jnp.float32) * scale
    if len(shards) > 0:
        values = level_of(own_key, shape, shards, -0.22, 0.18) * values
    return jnp.clip(values, min=-bound, max=bound).astype(kind)


def setup_inputs(seed: int = 0) -> dict:
    key_of = jax.random.split(jax.random.key(seed), 7)
    return {
        "block_weights": gaussian(key_of[0], (BLOCKS, D, 4, INNER), D ** -0.5, 0.109375, ((1, 8), (3, 4))),
        "modulation": gaussian(key_of[1], (BLOCKS, 3, D), 0.7, 4.0, ((0, 8),), jnp.float32),
        "inflow": gaussian(key_of[2], (BLOCKS, PATCH, D), 1.0, 6.0, ((0, 8), (2, 4))),
        "stale_cache": draw_stale_cache(jax.random.fold_in(key_of[6], 71), 0),
        "patch_index": place_ends(jax.random.randint(key_of[4], (BLOCKS,), 0, SEQ // PATCH), jax.random.fold_in(key_of[4], 1), 0, (SEQ // PATCH) - 1).astype(jnp.int32),
        "assignment": jax.random.permutation(key_of[5], BLOCKS).astype(jnp.int32),
    }


def run_section(block_weights, items):
    block, modulation_row, inflow_row, cache_row, patch_row = items
    weights = lax.dynamic_index_in_dim(block_weights, block, 0, keepdims=False)
    tokens = inflow_row.astype(jnp.float32)
    center = lax.optimization_barrier(jnp.mean(tokens, axis=1, keepdims=True))
    spread = lax.optimization_barrier(jnp.mean((tokens - center) ** 2, axis=1, keepdims=True))
    normed = (tokens - center) * lax.rsqrt(spread + 1e-06)
    normed = (normed * (1.0 + modulation_row[0]) + modulation_row[1]).astype(jnp.bfloat16)
    projected = jnp.dot(normed, weights[:, :3, :].reshape(D, 3 * INNER), preferred_element_type=jnp.float32)
    projected = projected.astype(jnp.bfloat16).reshape(PATCH, 3, HEADS, HD)
    start = (patch_row * PATCH).astype(jnp.int32)
    zero_index = jnp.zeros((), jnp.int32)
    keys_all = lax.dynamic_update_slice(cache_row[0], projected[:, 1].reshape(PATCH, INNER), (start, zero_index))
    values_all = lax.dynamic_update_slice(cache_row[1], projected[:, 2].reshape(PATCH, INNER), (start, zero_index))
    query = projected[:, 0].astype(jnp.float32)
    keys_heads = keys_all.reshape(SEQ, HEADS, HD).astype(jnp.float32)
    values_heads = values_all.reshape(SEQ, HEADS, HD).astype(jnp.float32)
    scores = jnp.einsum('phd,shd->hps', query, keys_heads) / jnp.sqrt(jnp.float32(HD))
    highest = lax.optimization_barrier(jnp.max(scores, axis=2, keepdims=True))
    expo = jnp.exp(scores - highest)
    probabilities = (expo / lax.optimization_barrier(jnp.sum(expo, axis=2, keepdims=True))).astype(jnp.bfloat16)
    attended = jnp.einsum('hps,shd->phd', probabilities.astype(jnp.float32), values_heads).astype(jnp.bfloat16)
    groups = attended.reshape(PATCH, N_TP, INNER // N_TP).astype(jnp.float32)
    output_proj = weights[:, 3, :].reshape(D, N_TP, INNER // N_TP).astype(jnp.float32)
    partials = jnp.einsum('pti,dti->tpd', groups, output_proj).astype(jnp.bfloat16)
    mixed = lax.optimization_barrier(jnp.sum(partials.astype(jnp.float32), axis=0))
    return (tokens + modulation_row[2] * mixed).astype(jnp.bfloat16)

def reference(block_weights, modulation, inflow, stale_cache, patch_index, assignment):
    section_ids = jnp.arange(BLOCKS, dtype=jnp.int32)
    owner_table = (assignment[None, :] == section_ids[:, None]).astype(jnp.int32)
    inverse = lax.optimization_barrier(jnp.sum(owner_table * section_ids[None, :], axis=1)).astype(jnp.int32)
    results = lax.map(lambda items: run_section(block_weights, items), (inverse, modulation, inflow, stale_cache, patch_index))
    return jnp.roll(results, 1, axis=0)
```

```python
import functools

import jax
import jax.numpy as jnp
from jax import lax
from jax.experimental import pallas as pl
from jax.experimental.pallas import tpu as pltpu
from jax.sharding import PartitionSpec as P

HD = 128
VMEM_LIMIT = 48 * 1024 * 1024


def split_kernel(lanes, order_ref, rows_ref, *rest):
    outs, wide = rest[:4], rest[4]
    depth = outs[0].shape[1]
    period = 4 * lanes
    wide[...] = rows_ref[0].astype(jnp.float32)
    for kind in range(4):
        for lane in range(lanes):
            part = wide[pl.ds(lane * 4 + kind, depth, stride=period), :]
            outs[kind][0, :, lane * HD : (lane + 1) * HD] = part.astype(jnp.bfloat16)


def split_blocks(block_weights, order):
    blocks, depth, kinds, inner = block_weights.shape
    lanes = inner // HD
    rows = block_weights.reshape(blocks, depth, kinds, lanes, HD)
    rows = rows.transpose(0, 1, 3, 2, 4).reshape(blocks, depth * lanes * kinds, HD)
    steps = 2 if depth % 32 == 0 else 1
    step_rows = depth // steps
    out = jax.ShapeDtypeStruct((blocks, depth, inner), jnp.bfloat16)
    return pl.pallas_call(
        functools.partial(split_kernel, lanes),
        grid_spec=pltpu.PrefetchScalarGridSpec(
            num_scalar_prefetch=1,
            grid=(blocks, steps),
            in_specs=[
                pl.BlockSpec(
                    (1, step_rows * lanes * kinds, HD), lambda i, j, order: (order[i], j, 0)
                )
            ],
            out_specs=[pl.BlockSpec((1, step_rows, inner), lambda i, j, order: (i, j, 0))] * 4,
            scratch_shapes=[pltpu.VMEM((step_rows * lanes * kinds, HD), jnp.float32)],
        ),
        out_shape=[out] * 4,
        compiler_params=pltpu.CompilerParams(vmem_limit_bytes=VMEM_LIMIT),
        cost_estimate=pl.CostEstimate(
            flops=0, bytes_accessed=4 * block_weights.size, transcendentals=0
        ),
        name="split_blocks",
    )(order, rows)


def norm_kernel(tokens_ref, modulation_ref, out_ref):
    tokens = tokens_ref[...].astype(jnp.float32)
    center = jnp.mean(tokens, axis=1, keepdims=True)
    tokens = tokens - center
    spread = jnp.mean(tokens * tokens, axis=1, keepdims=True)
    normed = tokens * lax.rsqrt(spread + 1e-06)
    out_ref[...] = (normed * (1.0 + modulation_ref[0:1]) + modulation_ref[1:2]).astype(jnp.bfloat16)


def norm(tokens, modulation):
    patch, width = tokens.shape
    rows = 128
    return pl.pallas_call(
        norm_kernel,
        grid=(patch // rows,),
        in_specs=[
            pl.BlockSpec((rows, width), lambda i: (i, 0)),
            pl.BlockSpec((3, width), lambda i: (0, 0)),
        ],
        out_specs=pl.BlockSpec((rows, width), lambda i: (i, 0)),
        out_shape=jax.ShapeDtypeStruct((patch, width), jnp.bfloat16),
        compiler_params=pltpu.CompilerParams(vmem_limit_bytes=VMEM_LIMIT),
        cost_estimate=pl.CostEstimate(
            flops=10 * patch * width, bytes_accessed=4 * patch * width, transcendentals=0
        ),
        name="norm",
    )(tokens, modulation)


def attention_kernel(where_ref, q_ref, k_ref, v_ref, stale_ref, out_ref):
    patch = q_ref.shape[0]
    pieces = stale_ref.shape[1] // patch
    query = q_ref[...]
    scale = 1.0 / jnp.sqrt(jnp.float32(HD))

    def scores_of(keys):
        return lax.dot_general(
            query, keys, (((1,), (1,)), ((), ())), preferred_element_type=jnp.float32
        ) * scale

    highest, total, summed = None, None, None
    for piece in range(pieces):
        if piece < pieces - 1:
            start = pl.multiple_of(lax.rem(where_ref[0] + 1 + piece, pieces) * patch, patch)
            keys = stale_ref[0, pl.ds(start, patch), :]
            values = stale_ref[1, pl.ds(start, patch), :]
        else:
            keys, values = k_ref[...], v_ref[...]
        scores = scores_of(keys)
        top = jnp.max(scores, axis=1, keepdims=True)
        if piece > 0:
            top = jnp.maximum(highest, top)
        expo = jnp.exp(scores - top)
        row = jnp.sum(expo, axis=1, keepdims=True)
        part = jnp.dot(expo.astype(jnp.bfloat16), values, preferred_element_type=jnp.float32)
        if piece > 0:
            shrink = jnp.exp(highest - top)
            row = total * shrink + row
            part = summed * shrink + part
        highest, total, summed = top, row, part
    out_ref[...] = (summed / total).astype(jnp.bfloat16)


def attention(where, query, key, value, stale):
    patch, inner = query.shape
    seq_len = stale.shape[1]
    own = pl.BlockSpec((patch, HD), lambda h, where: (0, h))
    return pl.pallas_call(
        attention_kernel,
        grid_spec=pltpu.PrefetchScalarGridSpec(
            num_scalar_prefetch=1,
            grid=(inner // HD,),
            in_specs=[own, own, own, pl.BlockSpec((2, seq_len, HD), lambda h, where: (0, 0, h))],
            out_specs=own,
        ),
        out_shape=jax.ShapeDtypeStruct((patch, inner), jnp.bfloat16),
        compiler_params=pltpu.CompilerParams(vmem_limit_bytes=VMEM_LIMIT),
        cost_estimate=pl.CostEstimate(
            flops=4 * patch * inner * seq_len,
            bytes_accessed=4 * inner * (seq_len + 2 * patch),
            transcendentals=patch * seq_len * (inner // HD),
        ),
        name="attention",
    )(where, query, key, value, stale)


def local(block_weights, modulation, inflow, stale_cache, patch_index, assignment):
    sections = lax.axis_size("section")
    section_ids = jnp.arange(sections, dtype=jnp.int32)
    owner_table = (assignment[None, :] == section_ids[:, None]).astype(jnp.int32)
    inverse = jnp.sum(owner_table * section_ids[None, :], axis=1)
    parts = split_blocks(block_weights, inverse)
    width = modulation.shape[2]
    inner = block_weights.shape[3]

    def relay(part):
        moved = lax.all_to_all(part, "section", split_axis=0, concat_axis=0, tiled=True)
        return moved.reshape(width, inner)

    to_query, to_key, to_value, to_out = [relay(part) for part in parts]
    tokens = lax.all_gather(inflow[0], "tp", axis=1, tiled=True)
    normed = norm(tokens, modulation[0])

    def project(matrix):
        return jnp.dot(normed, matrix, preferred_element_type=jnp.float32).astype(jnp.bfloat16)

    query, key, value = project(to_query), project(to_key), project(to_value)
    attended = attention(patch_index, query, key, value, stale_cache[0])
    partial = lax.dot_general(
        attended, to_out, (((1,), (1,)), ((), ())), preferred_element_type=jnp.float32
    ).astype(jnp.bfloat16)
    mixed = lax.psum_scatter(partial, "tp", scatter_dimension=1, tiled=True).astype(jnp.float32)
    share = inflow.shape[2]
    gate = lax.dynamic_slice_in_dim(modulation[0, 2], lax.axis_index("tp") * share, share, 0)
    result = (inflow[0].astype(jnp.float32) + gate * mixed).astype(jnp.bfloat16)
    route = [((i - 1) % sections, i) for i in range(sections)]
    return lax.ppermute(result, "section", route)[None]


def solution(mesh):
    placed = (
        P(None, "section", None, "tp"),
        P("section", None, None),
        P("section", None, "tp"),
        P("section", None, None, "tp"),
        P("section"),
        P(),
    )
    return jax.shard_map(
        local, mesh=mesh, in_specs=placed, out_specs=P("section", None, "tp"), check_vma=False
    )
```

```python
import functools

import jax
import jax.numpy as jnp
import ml_dtypes
import numpy as np
from jax import lax
from jax.experimental import pallas as pl
from jax.experimental.pallas import tpu as pltpu
from jax.sharding import PartitionSpec as P

HD = 128
VMEM_LIMIT = 48 * 1024 * 1024
F32 = jnp.float32
BF16 = jnp.bfloat16
WHOLE = pl.BlockSpec(memory_space=pltpu.VMEM)
ANYWHERE = pl.BlockSpec(memory_space=pl.ANY)
SCALAR = pl.BlockSpec(memory_space=pltpu.SMEM)
PARAMS = pltpu.CompilerParams(vmem_limit_bytes=VMEM_LIMIT)


def cost(flops, size, exps=0):
    return pl.CostEstimate(flops=flops, bytes_accessed=size, transcendentals=exps)


def turned(left, right):
    return lax.dot_general(left, right, (((1,), (1,)), ((), ())), preferred_element_type=F32)


def pick_matrix(kinds, lanes, depth_step):
    period = 4 * lanes
    row = np.arange(len(kinds) * lanes * depth_step)
    kind = np.asarray(kinds)[row // (lanes * depth_step)]
    source = (row % depth_step) * period + (row // depth_step) % lanes * 4 + kind
    return np.equal.outer(source, np.arange(period * depth_step)).astype(ml_dtypes.bfloat16)


def split_kernel(lanes, plan, kinds, depth_step, order_ref, pick_ref, rows_ref, *outs):
    depth = rows_ref.shape[1] // (4 * lanes)
    chunk = depth_step * 4 * lanes

    def fill(own):
        for first in range(0, depth, depth_step):
            begin = first * 4 * lanes
            sorted_rows = jnp.dot(
                pick_ref[...], rows_ref[0, begin : begin + chunk, :], preferred_element_type=F32
            ).astype(BF16)
            for out, columns in zip(own, plan):
                for column, (kind, lane) in enumerate(columns):
                    at = (kinds.index(kind) * lanes + lane) * depth_step
                    out[first : first + depth_step, column * HD : (column + 1) * HD] = sorted_rows[
                        at : at + depth_step
                    ]

    for block in range(len(outs) // len(plan)):
        own = outs[block * len(plan) : (block + 1) * len(plan)]
        pl.when(pl.program_id(0) == block)(functools.partial(fill, own))


def split_blocks(rows, order, plan, lanes):
    depth = rows.shape[1] // (4 * lanes)
    depth_step = max(n for n in (16, 32, 64) if depth % n == 0 and n * 4 * lanes <= 256)
    kinds = sorted({kind for columns in plan for kind, _ in columns})
    pick = pick_matrix(kinds, lanes, depth_step)
    blocks = order.shape[0]
    shapes = [(depth, len(columns) * HD) for columns in plan]
    flat = pl.pallas_call(
        functools.partial(split_kernel, lanes, plan, kinds, depth_step),
        grid_spec=pltpu.PrefetchScalarGridSpec(
            num_scalar_prefetch=1,
            grid=(blocks,),
            in_specs=[
                pl.BlockSpec(pick.shape, lambda i, order: (0, 0)),
                pl.BlockSpec((1,) + rows.shape[1:], lambda i, order: (order[i], 0, 0)),
            ],
            out_specs=[pl.BlockSpec(shape, lambda i, order: (0, 0)) for shape in shapes] * blocks,
        ),
        out_shape=[jax.ShapeDtypeStruct(shape, BF16) for shape in shapes] * blocks,
        compiler_params=PARAMS,
        cost_estimate=cost(0, 3 * blocks * rows.shape[1] * HD),
        name="split_blocks",
    )(order, jnp.asarray(pick), rows)
    return [list(flat[i :: len(shapes)]) for i in range(len(shapes))]


def norm_kernel(tokens_ref, modulation_ref, out_ref):
    tokens = tokens_ref[...].astype(F32)
    center = jnp.mean(tokens, axis=1, keepdims=True)
    tokens = tokens - center
    spread = jnp.mean(tokens * tokens, axis=1, keepdims=True)
    normed = tokens * lax.rsqrt(spread + 1e-06)
    out_ref[...] = (normed * (1.0 + modulation_ref[0:1]) + modulation_ref[1:2]).astype(BF16)


def norm(tokens, modulation):
    patch, width = tokens.shape
    rows = 128
    return pl.pallas_call(
        norm_kernel,
        grid=(patch // rows,),
        in_specs=[
            pl.BlockSpec((rows, width), lambda i: (i, 0)),
            pl.BlockSpec((3, width), lambda i: (0, 0)),
        ],
        out_specs=pl.BlockSpec((rows, width), lambda i: (i, 0)),
        out_shape=jax.ShapeDtypeStruct((patch, width), BF16),
        compiler_params=PARAMS,
        cost_estimate=cost(10 * patch * width, 4 * patch * width),
        name="norm",
    )(tokens, modulation)


def gathered(pieces, sources_ref, matrix, sems):
    depth = pieces[0].shape[0]
    copies = []
    for index, piece in enumerate(pieces):
        start = pl.multiple_of(sources_ref[index] * depth, 16)
        copies.append(
            pltpu.make_async_copy(piece, matrix.at[pl.ds(start, depth), :], sems.at[index])
        )
        copies[-1].start()
    for copy in copies:
        copy.wait()


def score_kernel(count, sources_ref, where_ref, normed_ref, stale_ref, *rest):
    pieces, (expo_ref, base_ref, share_ref, both, matrix, sems) = rest[:count], rest[count:]
    heads, patch, _ = expo_ref.shape
    parts = stale_ref.shape[1] // patch
    gathered(pieces, sources_ref, matrix, sems)
    both[...] = jnp.dot(normed_ref[...], matrix[...], preferred_element_type=F32).astype(BF16)
    starts = [
        pl.multiple_of(lax.rem(where_ref[0] + 1 + part, parts) * patch, patch)
        for part in range(parts - 1)
    ]
    for head in range(heads):
        cols = slice(head * HD, (head + 1) * HD)
        query = both[:, cols]
        keys = [stale_ref[0, pl.ds(start, patch), cols] for start in starts]
        keys.append(both[:, (heads + head) * HD : (heads + head + 1) * HD])
        scores = [turned(query, key) / jnp.sqrt(F32(HD)) for key in keys]
        top = functools.reduce(jnp.maximum, scores)
        top = jnp.max(top, axis=1, keepdims=True)
        total, summed = 0.0, 0.0
        for part, score in enumerate(scores):
            expo = jnp.exp(score - top)
            total += jnp.sum(expo, axis=1, keepdims=True)
            expo = expo.astype(BF16)
            if part == parts - 1:
                expo_ref[head] = expo
                continue
            values = stale_ref[1, pl.ds(starts[part], patch), cols]
            summed += jnp.dot(expo, values, preferred_element_type=F32)
        share = 1.0 / total
        base_ref[head] = summed * share
        share_ref[head] = jnp.broadcast_to(share, (patch, HD))


def attend_kernel(count, sources_ref, normed_ref, expo_ref, base_ref, share_ref, *rest):
    pieces, (out_ref, values, matrix, sems) = rest[:count], rest[count:]
    gathered(pieces, sources_ref, matrix, sems)
    values[...] = jnp.dot(normed_ref[...], matrix[...], preferred_element_type=F32).astype(BF16)
    for spot in range(expo_ref.shape[0]):
        cols = slice(spot * HD, (spot + 1) * HD)
        new = jnp.dot(expo_ref[spot], values[:, cols], preferred_element_type=F32)
        out_ref[:, cols] = (base_ref[spot] + new * share_ref[spot]).astype(BF16)


def score(normed, pieces, sources, where, stale, group):
    patch, width = normed.shape
    heads, keys = len(group), stale.shape[1]
    columns = heads * HD
    stat = jax.ShapeDtypeStruct((heads, patch, HD), F32)
    at = lambda i: (0, 0, group[0] // heads)
    return pl.pallas_call(
        functools.partial(score_kernel, len(pieces)),
        grid=(1,),
        in_specs=[SCALAR, SCALAR, WHOLE, pl.BlockSpec((2, keys, columns), at)]
        + [ANYWHERE] * len(pieces),
        out_specs=[WHOLE] * 3,
        out_shape=[jax.ShapeDtypeStruct((heads, patch, patch), BF16), stat, stat],
        scratch_shapes=[
            pltpu.VMEM((patch, 2 * columns), BF16),
            pltpu.VMEM((width, 2 * columns), BF16),
            pltpu.SemaphoreType.DMA((len(pieces),)),
        ],
        compiler_params=PARAMS,
        cost_estimate=cost(
            4 * patch * columns * (width + keys), 4 * columns * (width + keys), patch * heads * keys
        ),
        name="score",
    )(sources, where, normed, stale, *pieces)


def attend(normed, pieces, sources, first, expo, base, share):
    patch, width = normed.shape
    columns = pieces[0].shape[1]
    count = columns // HD
    picked = lambda last: pl.BlockSpec((count, patch, last), lambda i: (first // count, 0, 0))
    return pl.pallas_call(
        functools.partial(attend_kernel, len(pieces)),
        grid=(1,),
        in_specs=[SCALAR, WHOLE, picked(patch), picked(HD), picked(HD)]
        + [ANYWHERE] * len(pieces),
        out_specs=WHOLE,
        out_shape=jax.ShapeDtypeStruct((patch, columns), BF16),
        scratch_shapes=[
            pltpu.VMEM((patch, columns), BF16),
            pltpu.VMEM((width, columns), BF16),
            pltpu.SemaphoreType.DMA((len(pieces),)),
        ],
        compiler_params=PARAMS,
        cost_estimate=cost(2 * patch * columns * (width + patch), 2 * columns * width),
        name="attend",
    )(sources, normed, expo, base, share, *pieces)


def output_kernel(tp, chunks, inflow_ref, gate_ref, *rest):
    attended, matrices, out_ref = rest[: tp * chunks], rest[tp * chunks : -1], rest[-1]
    mixed = 0.0
    for index in range(tp):
        own = attended[index * chunks : (index + 1) * chunks]
        left = jnp.concatenate([piece[...] for piece in own], axis=1)
        mixed += turned(left, matrices[index][...])
    out_ref[...] = (inflow_ref[...].astype(F32) + gate_ref[...] * mixed).astype(BF16)


def output(inflow, gate, attended, matrices):
    tp, chunks = len(attended), len(attended[0])
    patch, share = inflow.shape
    inner = matrices[0].shape[1]
    flat = [piece for own in attended for piece in own]
    return pl.pallas_call(
        functools.partial(output_kernel, tp, chunks),
        in_specs=[WHOLE] * (2 + len(flat) + tp),
        out_specs=WHOLE,
        out_shape=jax.ShapeDtypeStruct(inflow.shape, BF16),
        compiler_params=PARAMS,
        cost_estimate=cost(2 * patch * share * inner * tp, 2 * inner * tp * (share + patch)),
        name="output",
    )(inflow, gate, *flat, *matrices)


def after(block, earlier):
    return lax.optimization_barrier((block, earlier))[0]


def swapped(block, axis, distance):
    return lax.ppermute(block, axis, [(i, i ^ distance) for i in range(lax.axis_size(axis))])


def handed_on(block):
    sections = lax.axis_size("section")
    return lax.ppermute(block, "section", [(i, (i + 1) % sections) for i in range(sections)])


def relay(stages, window):
    sections = len(stages[0])
    distances = sorted(range(1, sections), key=lambda d: (d == 1, d % 2, d))
    sent, arrived = [], []
    for pieces in stages:
        received = {0: pieces[0]}
        for distance in distances:
            piece = pieces[distance]
            if len(sent) >= window:
                piece = after(piece, sent[-window])
            received[distance] = swapped(piece, "section", distance)
            sent.append(received[distance])
        arrived.append([received[d] for d in range(sections)])
    return arrived


def place_kernel(count, slots_ref, *rest):
    pieces, (out_ref, sems) = rest[:count], rest[count:]
    copies = [
        pltpu.make_async_copy(piece, out_ref.at[slots_ref[index]], sems.at[index])
        for index, piece in enumerate(pieces)
    ]
    for copy in copies:
        copy.start()
    for copy in copies:
        copy.wait()


def placed(pieces, slots):
    return pl.pallas_call(
        functools.partial(place_kernel, len(pieces)),
        in_specs=[SCALAR] + [ANYWHERE] * len(pieces),
        out_specs=ANYWHERE,
        out_shape=jax.ShapeDtypeStruct((len(pieces),) + pieces[0].shape, BF16),
        scratch_shapes=[pltpu.SemaphoreType.DMA((len(pieces),))],
        compiler_params=PARAMS,
        cost_estimate=cost(0, 4 * len(pieces) * pieces[0].size),
        name="placed",
    )(slots, *pieces)


def local(block_weights, modulation, inflow, stale_cache, patch_index, assignment):
    sections, tp = lax.axis_size("section"), lax.axis_size("tp")
    here, rank = lax.axis_index("section"), lax.axis_index("tp")
    blocks, depth, kinds, inner = block_weights.shape
    lanes = inner // HD
    share = inflow.shape[2]

    section_ids = jnp.arange(sections, dtype=jnp.int32)
    sources = here ^ section_ids

    def block_of(section):
        return jnp.sum((assignment[None] == section[:, None]) * section_ids[None], axis=1)

    rows = block_weights.reshape(blocks, depth, kinds, lanes, HD)
    rows = rows.transpose(0, 1, 3, 2, 4).reshape(blocks, depth * lanes * kinds, HD)
    tokens = lax.all_gather(inflow[0], "tp", axis=1, tiled=True)

    size = 2 if lanes % 2 == 0 else 1
    groups = [tuple(range(first, first + size)) for first in range(0, lanes, size)]
    plan, chunks = [], []
    for group in groups:
        plan.append([(kind, head) for kind in (0, 1) for head in group])
        parts = [group] if group != groups[-1] else [(head,) for head in group]
        plan += [[(2, head) for head in part] for part in parts]
        chunks.append(parts)
    to_out = split_blocks(
        rows, block_of((sources + sections - 1) % sections), [[(3, head) for head in range(lanes)]], lanes
    )
    arrived = iter(relay(to_out + split_blocks(rows, block_of(sources), plan, lanes), 4))

    per = sections // tp
    slots = ((sources // per) ^ rank) * per + sources % per
    held = placed(next(arrived), slots).reshape(tp, per * depth, inner)
    matrices = [held[0]]
    for distance in range(1, tp):
        matrices.append(swapped(after(held[distance], matrices[-1]), "tp", distance))

    normed = norm(tokens, modulation[0])
    attended = [[] for _ in range(tp)]
    for group, parts in zip(groups, chunks):
        stats = score(normed, next(arrived), sources, patch_index, stale_cache[0], group)
        for part in parts:
            own = attend(normed, next(arrived), sources, part[0] - group[0], *stats)
            moved = handed_on(own)
            for distance in range(tp):
                attended[distance].append(swapped(moved, "tp", distance) if distance else moved)
    carried = handed_on(after(inflow[0], own))
    gate = handed_on(modulation[0, 2])
    gate = lax.dynamic_slice_in_dim(gate, rank * share, share, 0)[None]
    return output(carried, gate, attended, matrices)[None]


def solution(mesh):
    spread = (
        P(None, "section", None, "tp"),
        P("section", None, None),
        P("section", None, "tp"),
        P("section", None, None, "tp"),
        P("section"),
        P(),
    )
    return jax.shard_map(
        local, mesh=mesh, in_specs=spread, out_specs=P("section", None, "tp"), check_vma=False
    )
```

```python
import functools

import jax
import jax.numpy as jnp
import ml_dtypes
import numpy as np
from jax import lax
from jax.experimental import pallas as pl
from jax.experimental.pallas import tpu as pltpu
from jax.sharding import PartitionSpec as P

HD = 128
F32 = jnp.float32
BF16 = jnp.bfloat16
WHOLE = pl.BlockSpec(memory_space=pltpu.VMEM)
ANYWHERE = pl.BlockSpec(memory_space=pl.ANY)
SCALAR = pl.BlockSpec(memory_space=pltpu.SMEM)


def params(mebibytes):
    return pltpu.CompilerParams(vmem_limit_bytes=mebibytes * 1024 * 1024)


def in_hbm(array):
    return pltpu.with_memory_space_constraint(array, pltpu.HBM)


def cost(flops, size, exps=0):
    return pl.CostEstimate(flops=flops, bytes_accessed=size, transcendentals=exps)


def turned(left, right):
    return lax.dot_general(left, right, (((1,), (1,)), ((), ())), preferred_element_type=F32)


def pick_matrix(kinds, lanes, depth_step):
    period = 4 * lanes
    row = np.arange(len(kinds) * lanes * depth_step)
    kind = np.asarray(kinds)[row // (lanes * depth_step)]
    source = (row % depth_step) * period + (row // depth_step) % lanes * 4 + kind
    return np.equal.outer(source, np.arange(period * depth_step)).astype(ml_dtypes.bfloat16)


def split_kernel(lanes, plan, kinds, depth_step, order_ref, pick_ref, rows_ref, *outs):
    depth = rows_ref.shape[1] // (4 * lanes)
    chunk = depth_step * 4 * lanes

    def fill(own):
        for first in range(0, depth, depth_step):
            begin = first * 4 * lanes
            sorted_rows = jnp.dot(
                pick_ref[...], rows_ref[0, begin : begin + chunk, :], preferred_element_type=F32
            ).astype(BF16)
            for out, columns in zip(own, plan):
                for column, (kind, lane) in enumerate(columns):
                    at = (kinds.index(kind) * lanes + lane) * depth_step
                    out[first : first + depth_step, column * HD : (column + 1) * HD] = sorted_rows[
                        at : at + depth_step
                    ]

    for block in range(len(outs) // len(plan)):
        own = outs[block * len(plan) : (block + 1) * len(plan)]
        pl.when(pl.program_id(0) == block)(functools.partial(fill, own))


def split_blocks(rows, order, plan, lanes):
    depth = rows.shape[1] // (4 * lanes)
    depth_step = max(n for n in (16, 32, 64) if depth % n == 0 and n * 4 * lanes <= 256)
    kinds = sorted({kind for columns in plan for kind, _ in columns})
    pick = pick_matrix(kinds, lanes, depth_step)
    blocks = order.shape[0]
    shapes = [(depth, len(columns) * HD) for columns in plan]
    flat = pl.pallas_call(
        functools.partial(split_kernel, lanes, plan, kinds, depth_step),
        grid_spec=pltpu.PrefetchScalarGridSpec(
            num_scalar_prefetch=1,
            grid=(blocks,),
            in_specs=[
                pl.BlockSpec(pick.shape, lambda i, order: (0, 0)),
                pl.BlockSpec((1,) + rows.shape[1:], lambda i, order: (order[i], 0, 0)),
            ],
            out_specs=[WHOLE] * (len(shapes) * blocks),
        ),
        out_shape=[jax.ShapeDtypeStruct(shape, BF16) for shape in shapes] * blocks,
        compiler_params=params(10),
        cost_estimate=cost(0, 3 * blocks * rows.shape[1] * HD),
        name="split_blocks",
    )(order, jnp.asarray(pick), in_hbm(rows))
    return [list(flat[i :: len(shapes)]) for i in range(len(shapes))]


def norm_kernel(tokens_ref, modulation_ref, out_ref):
    tokens = tokens_ref[...].astype(F32)
    center = jnp.mean(tokens, axis=1, keepdims=True)
    tokens = tokens - center
    spread = jnp.mean(tokens * tokens, axis=1, keepdims=True)
    normed = tokens * lax.rsqrt(spread + 1e-06)
    out_ref[...] = (normed * (1.0 + modulation_ref[0:1]) + modulation_ref[1:2]).astype(BF16)


def norm(tokens, modulation):
    patch, width = tokens.shape
    rows = 128
    return pl.pallas_call(
        norm_kernel,
        grid=(patch // rows,),
        in_specs=[
            pl.BlockSpec((rows, width), lambda i: (i, 0)),
            pl.BlockSpec((3, width), lambda i: (0, 0)),
        ],
        out_specs=pl.BlockSpec((rows, width), lambda i: (i, 0)),
        out_shape=jax.ShapeDtypeStruct((patch, width), BF16),
        compiler_params=params(14),
        cost_estimate=cost(10 * patch * width, 4 * patch * width),
        name="norm",
    )(in_hbm(tokens), modulation)


def fetched(pairs, pieces, first, sources_ref, matrix, sems):
    depth, columns = pieces[0].shape[0], pl.ds(first, matrix.shape[1])
    for index, piece in enumerate(pieces):
        start = pl.multiple_of(sources_ref[index] * depth, 16)
        pairs = pairs + [(piece.at[:, columns], matrix.at[pl.ds(start, depth), :])]
    copies = [
        pltpu.make_async_copy(source, target, sems.at[index])
        for index, (source, target) in enumerate(pairs)
    ]
    for copy in copies:
        copy.start()
    for copy in copies:
        copy.wait()


def score_kernel(count, cols, sources_ref, where_ref, normed, stale_hbm, *rest):
    pieces, (expo_ref, base_ref, share_ref, both, matrix, stale, sems) = (
        rest[:count], rest[count:]
    )
    heads, patch, _ = expo_ref.shape
    parts = stale.shape[1] // patch
    fetched([(stale_hbm.at[:, :, cols], stale)], pieces, 0, sources_ref, matrix, sems)
    both[...] = jnp.dot(normed[...], matrix[...], preferred_element_type=F32).astype(BF16)
    starts = [
        pl.multiple_of(lax.rem(where_ref[0] + 1 + part, parts) * patch, patch)
        for part in range(parts - 1)
    ]
    scale = F32(np.log2(np.e) / np.sqrt(HD))
    for head in range(heads):
        own = slice(head * HD, (head + 1) * HD)
        query = both[:, own]
        keys = [stale[0, pl.ds(start, patch), own] for start in starts]
        keys.append(both[:, (heads + head) * HD : (heads + head + 1) * HD])
        scores = [turned(query, key) for key in keys]
        top = functools.reduce(jnp.maximum, scores)
        top = jnp.max(top, axis=1, keepdims=True)
        total, summed = 0.0, 0.0
        for part, score in enumerate(scores):
            expo = jnp.exp2((score - top) * scale)
            total += expo
            expo = expo.astype(BF16)
            if part == parts - 1:
                expo_ref[head] = expo
                continue
            values = stale[1, pl.ds(starts[part], patch), own]
            summed += jnp.dot(expo, values, preferred_element_type=F32)
        share = 1.0 / jnp.sum(total, axis=1, keepdims=True)
        base_ref[head] = summed * share
        share_ref[head] = jnp.broadcast_to(share, (patch, HD))


def attend_kernel(count, first, sources_ref, normed, expo_ref, base_ref, share_ref, *rest):
    pieces, (out_ref, values, matrix, sems) = rest[:count], rest[count:]
    fetched([], pieces, first, sources_ref, matrix, sems)
    values[...] = jnp.dot(normed[...], matrix[...], preferred_element_type=F32).astype(BF16)
    for spot in range(expo_ref.shape[0]):
        own = slice(spot * HD, (spot + 1) * HD)
        new = jnp.dot(expo_ref[spot], values[:, own], preferred_element_type=F32)
        out_ref[:, own] = (base_ref[spot] + new * share_ref[spot]).astype(BF16)


def score(normed, pieces, sources, where, stale, group):
    patch, width = normed.shape
    heads, keys = len(group), stale.shape[1]
    columns = heads * HD
    stat = jax.ShapeDtypeStruct((heads, patch, HD), F32)
    cols = slice(group[0] * HD, group[0] * HD + columns)
    return pl.pallas_call(
        functools.partial(score_kernel, len(pieces), cols),
        in_specs=[SCALAR, SCALAR, WHOLE] + [ANYWHERE] * (1 + len(pieces)),
        out_specs=[WHOLE] * 3,
        out_shape=[jax.ShapeDtypeStruct((heads, patch, patch), BF16), stat, stat],
        scratch_shapes=[
            pltpu.VMEM((patch, 2 * columns), BF16),
            pltpu.VMEM((width, 2 * columns), BF16),
            pltpu.VMEM((2, keys, columns), BF16),
            pltpu.SemaphoreType.DMA((len(pieces) + 1,)),
        ],
        compiler_params=params(20),
        cost_estimate=cost(
            4 * patch * columns * (width + keys), 4 * columns * (width + keys), patch * heads * keys
        ),
        name="score",
    )(sources, where, normed, in_hbm(stale), *pieces)


def attend(normed, pieces, sources, first, expo, base, share):
    patch, width = normed.shape
    columns = expo.shape[0] * HD
    return pl.pallas_call(
        functools.partial(attend_kernel, len(pieces), first),
        in_specs=[SCALAR, WHOLE, WHOLE, WHOLE, WHOLE] + [ANYWHERE] * len(pieces),
        out_specs=WHOLE,
        out_shape=jax.ShapeDtypeStruct((patch, columns), BF16),
        scratch_shapes=[
            pltpu.VMEM((patch, columns), BF16),
            pltpu.VMEM((width, columns), BF16),
            pltpu.SemaphoreType.DMA((len(pieces),)),
        ],
        compiler_params=params(10),
        cost_estimate=cost(2 * patch * columns * (width + patch), 2 * columns * width),
        name="attend",
    )(sources, normed, expo, base, share, *pieces)


def output_kernel(tp, chunks, inflow_ref, gate_ref, *rest):
    attended, matrices, out_ref = rest[: tp * chunks], rest[tp * chunks : -1], rest[-1]
    mixed = 0.0
    for index in range(tp):
        own = attended[index * chunks : (index + 1) * chunks]
        left = jnp.concatenate([piece[...] for piece in own], axis=1)
        mixed += turned(left, matrices[index][...])
    out_ref[...] = (inflow_ref[...].astype(F32) + gate_ref[...] * mixed).astype(BF16)


def output(inflow, gate, attended, matrices):
    tp, chunks = len(attended), len(attended[0])
    patch, share = inflow.shape
    inner = matrices[0].shape[1]
    arrays = [inflow, gate] + [piece for own in attended for piece in own] + matrices
    return pl.pallas_call(
        functools.partial(output_kernel, tp, chunks),
        grid=(1,),
        in_specs=[pl.BlockSpec(array.shape, lambda i: (0, 0)) for array in arrays],
        out_specs=pl.BlockSpec(inflow.shape, lambda i: (0, 0)),
        out_shape=jax.ShapeDtypeStruct(inflow.shape, BF16),
        compiler_params=params(20),
        cost_estimate=cost(2 * patch * share * inner * tp, 2 * inner * tp * (share + patch)),
        name="output",
    )(*arrays)


def after(block, earlier):
    return lax.optimization_barrier((block, earlier))[0]


def swapped(block, axis, distance):
    return lax.ppermute(block, axis, [(i, i ^ distance) for i in range(lax.axis_size(axis))])


def handed_on(block):
    sections = lax.axis_size("section")
    return lax.ppermute(block, "section", [(i, (i + 1) % sections) for i in range(sections)])


class Relay:
    def __init__(self, window):
        self.window, self.sent = window, []

    def swap(self, piece, distance, *earlier):
        size = piece.size
        for other in reversed(self.sent):
            size += other.size
            if size > self.window:
                earlier += (other,)
                break
        for other in earlier:
            piece = after(piece, other)
        self.sent.append(swapped(piece, "section", distance))
        return self.sent[-1]


def place_kernel(count, slots_ref, *rest):
    pieces, (out_ref, sems) = rest[:count], rest[count:]
    copies = [
        pltpu.make_async_copy(piece, out_ref.at[slots_ref[index]], sems.at[index])
        for index, piece in enumerate(pieces)
    ]
    for copy in copies:
        copy.start()
    for copy in copies:
        copy.wait()


def placed(pieces, slots):
    return pl.pallas_call(
        functools.partial(place_kernel, len(pieces)),
        in_specs=[SCALAR] + [ANYWHERE] * len(pieces),
        out_specs=ANYWHERE,
        out_shape=jax.ShapeDtypeStruct((len(pieces),) + pieces[0].shape, BF16),
        scratch_shapes=[pltpu.SemaphoreType.DMA((len(pieces),))],
        compiler_params=params(4),
        cost_estimate=cost(0, 4 * len(pieces) * pieces[0].size),
        name="placed",
    )(slots, *pieces)


def local(block_weights, modulation, inflow, stale_cache, patch_index, assignment):
    sections, tp = lax.axis_size("section"), lax.axis_size("tp")
    here, rank = lax.axis_index("section"), lax.axis_index("tp")
    blocks, depth, kinds, inner = block_weights.shape
    lanes = inner // HD
    share = inflow.shape[2]

    section_ids = jnp.arange(sections, dtype=jnp.int32)
    sources = here ^ section_ids

    def block_of(section):
        return jnp.sum((assignment[None] == section[:, None]) * section_ids[None], axis=1)

    rows = block_weights.reshape(blocks, depth, kinds, lanes, HD)
    rows = rows.transpose(0, 1, 3, 2, 4).reshape(blocks, depth * lanes * kinds, HD)
    tokens = lax.all_gather(inflow[0], "tp", axis=1, tiled=True)

    order = sorted(range(1, sections), key=lambda d: (d == 1, d % 2, d))
    own_blocks = block_of(sources)
    before = block_of((sources + sections - 1) % sections)

    ahead = [order[:3], order[3:] + [0]]
    to_out = {}
    for some in ahead:
        blocks_now = jnp.stack([before[d] for d in some])
        (made,) = split_blocks(rows, blocks_now, [[(3, head) for head in range(lanes)]], lanes)
        to_out.update(zip(some, made))
    size = max(1, lanes // 2)
    groups = [tuple(range(first, first + size)) for first in range(0, lanes, size)]
    plan = []
    for group in groups:
        plan.append([(kind, head) for kind in (0, 1) for head in group])
        values = [(2, head) for head in group]
        if group == groups[-1]:
            plan.append(values)
        else:
            plan[-1] += values
    split = split_blocks(rows, own_blocks, plan, lanes)

    relay = Relay(4 * depth * inner)
    for distance in order:
        to_out[distance] = relay.swap(to_out[distance], distance)
    per = sections // tp
    slots = ((sources // per) ^ rank) * per + sources % per
    held = placed([to_out[d] for d in range(sections)], slots).reshape(tp, per * depth, inner)
    matrices = [held[0]]
    for distance in range(1, tp):
        matrices.append(swapped(after(held[distance], matrices[-1]), "tp", distance))
    normed = norm(tokens, modulation[0])

    def relayed(stage, *earlier, at=0):
        pieces = [split[stage][0]] * sections
        for index, distance in enumerate(order):
            wait = earlier if index == at else ()
            pieces[distance] = relay.swap(split[stage][distance], distance, *wait)
        return pieces

    attended = [[] for _ in range(tp)]

    def share_out(part):
        moved = handed_on(part)
        for distance in range(tp):
            attended[distance].append(swapped(moved, "tp", distance) if distance else moved)
        return moved

    done = (normed,)
    for stage, group in enumerate(groups[:-1]):
        pieces = relayed(stage, *done, at=sections - 2)
        stats = score(normed, pieces, sources, patch_index, stale_cache[0], group)
        own = attend(normed, pieces, sources, 2 * len(group) * HD, *stats)
        done = (own,)
        share_out(own)
    pieces = relayed(len(plan) - 2, *done, at=min(4, sections - 2))
    value_pieces = relayed(len(plan) - 1)
    stats = score(normed, pieces, sources, patch_index, stale_cache[0], groups[-1])
    own = attend(normed, value_pieces, sources, 0, *stats)
    share_out(own)
    carried = handed_on(after(inflow[0], own))
    gate = handed_on(modulation[0, 2])
    gate = lax.dynamic_slice_in_dim(gate, rank * share, share, 0)[None]
    return output(carried, gate, attended, matrices)[None]


def solution(mesh):
    spread = (
        P(None, "section", None, "tp"),
        P("section", None, None),
        P("section", None, "tp"),
        P("section", None, None, "tp"),
        P("section"),
        P(),
    )
    return jax.shard_map(
        local, mesh=mesh, in_specs=spread, out_specs=P("section", None, "tp"), check_vma=False
    )
```

```python
import functools

import jax
import jax.numpy as jnp
import numpy as np
from jax import lax
from jax.experimental import pallas as pl
from jax.experimental.pallas import tpu as pltpu
from jax.sharding import PartitionSpec as P

HD = 128
F32 = jnp.float32
BF16 = jnp.bfloat16
WHOLE = pl.BlockSpec(memory_space=pltpu.VMEM)
ANYWHERE = pl.BlockSpec(memory_space=pl.ANY)
SCALAR = pl.BlockSpec(memory_space=pltpu.SMEM)


def params(mebibytes):
    return pltpu.CompilerParams(vmem_limit_bytes=mebibytes * 1024 * 1024)


def in_hbm(array):
    return pltpu.with_memory_space_constraint(array, pltpu.HBM)


def cost(flops, size, exps=0):
    return pl.CostEstimate(flops=flops, bytes_accessed=size, transcendentals=exps)


def turned(left, right):
    return lax.dot_general(left, right, (((1,), (1,)), ((), ())), preferred_element_type=F32)


def pick_matrix(kinds, lanes, depth_step):
    period = 4 * lanes
    shape = (len(kinds) * lanes * depth_step, period * depth_step)
    row = lax.broadcasted_iota(jnp.int32, shape, 0)
    column = lax.broadcasted_iota(jnp.int32, shape, 1)
    source = row % depth_step * period + row // depth_step % lanes * 4 + kinds[0]
    source += row // (lanes * depth_step)
    return jnp.where(source == column, 1.0, 0.0).astype(BF16)


def split_kernel(lanes, plan, kinds, depth_step, order_ref, rows_ref, *rest):
    outs, pick = rest[:-1], rest[-1]
    depth = rows_ref.shape[1] // (4 * lanes)
    chunk = depth_step * 4 * lanes

    @pl.when(pl.program_id(0) == 0)
    def _():
        pick[...] = pick_matrix(kinds, lanes, depth_step)

    def fill(own):
        for first in range(0, depth, depth_step):
            begin = first * 4 * lanes
            sorted_rows = jnp.dot(
                pick[...], rows_ref[0, begin : begin + chunk, :], preferred_element_type=F32
            ).astype(BF16)
            for out, columns in zip(own, plan):
                for column, (kind, lane) in enumerate(columns):
                    at = (kinds.index(kind) * lanes + lane) * depth_step
                    out[first : first + depth_step, column * HD : (column + 1) * HD] = sorted_rows[
                        at : at + depth_step
                    ]

    for block in range(len(outs) // len(plan)):
        own = outs[block * len(plan) : (block + 1) * len(plan)]
        pl.when(pl.program_id(0) == block)(functools.partial(fill, own))


def split_blocks(rows, order, first, count, plan, lanes, early):
    depth = rows.shape[1] // (4 * lanes)
    depth_step = max(n for n in (16, 32, 64) if depth % n == 0 and n * 4 * lanes <= 256)
    kinds = sorted({kind for columns in plan for kind, _ in columns})
    shapes = [(depth, len(columns) * HD) for columns in plan] * count
    if early:
        out_specs = [WHOLE] * len(shapes)
        out_shape = [jax.ShapeDtypeStruct(shape, BF16) for shape in shapes]
    else:
        out_specs = [pl.BlockSpec(shape, lambda i, order: (0, 0)) for shape in shapes]
        out_shape = [pltpu.HBM(shape, BF16) for shape in shapes]
    flat = pl.pallas_call(
        functools.partial(split_kernel, lanes, plan, kinds, depth_step),
        grid_spec=pltpu.PrefetchScalarGridSpec(
            num_scalar_prefetch=1,
            grid=(count,),
            in_specs=[pl.BlockSpec((1,) + rows.shape[1:], lambda i, order: (order[first + i], 0, 0))],
            out_specs=out_specs,
            scratch_shapes=[
                pltpu.VMEM((len(kinds) * lanes * depth_step, depth_step * 4 * lanes), BF16)
            ],
        ),
        out_shape=out_shape,
        compiler_params=params(10 if early else 32),
        cost_estimate=cost(0, 3 * count * rows.shape[1] * HD),
        name="split_blocks",
    )(order, in_hbm(rows))
    return [list(flat[i :: len(plan)]) for i in range(len(plan))]


def norm_kernel(tokens_ref, modulation_ref, out_ref):
    tokens = tokens_ref[...].astype(F32)
    center = jnp.mean(tokens, axis=1, keepdims=True)
    tokens = tokens - center
    spread = jnp.mean(tokens * tokens, axis=1, keepdims=True)
    normed = tokens * lax.rsqrt(spread + 1e-06)
    out_ref[...] = (normed * (1.0 + modulation_ref[0:1]) + modulation_ref[1:2]).astype(BF16)


def norm(tokens, modulation):
    patch, width = tokens.shape
    rows = 128
    return pl.pallas_call(
        norm_kernel,
        grid=(patch // rows,),
        in_specs=[
            pl.BlockSpec((rows, width), lambda i: (i, 0)),
            pl.BlockSpec((3, width), lambda i: (0, 0)),
        ],
        out_specs=pl.BlockSpec((rows, width), lambda i: (i, 0)),
        out_shape=jax.ShapeDtypeStruct((patch, width), BF16),
        compiler_params=params(14),
        cost_estimate=cost(10 * patch * width, 4 * patch * width),
        name="norm",
    )(in_hbm(tokens), modulation)


def fetched(pairs, pieces, first, sources_ref, matrix, sems):
    depth, columns = pieces[0].shape[0], pl.ds(first, matrix.shape[1])
    for index, piece in enumerate(pieces):
        start = pl.multiple_of(sources_ref[index] * depth, 16)
        pairs = pairs + [(piece.at[:, columns], matrix.at[pl.ds(start, depth), :])]
    copies = [
        pltpu.make_async_copy(source, target, sems.at[index])
        for index, (source, target) in enumerate(pairs)
    ]
    for copy in copies:
        copy.start()
    for copy in copies:
        copy.wait()


def score_kernel(count, cols, sources_ref, where_ref, normed, stale_hbm, *rest):
    pieces, (expo_ref, base_ref, share_ref, both, matrix, stale, sems) = (
        rest[:count], rest[count:]
    )
    heads, patch, _ = expo_ref.shape
    parts = stale.shape[1] // patch
    fetched([(stale_hbm.at[:, :, cols], stale)], pieces, 0, sources_ref, matrix, sems)
    both[...] = jnp.dot(normed[...], matrix[...], preferred_element_type=F32).astype(BF16)
    starts = [
        pl.multiple_of(lax.rem(where_ref[0] + 1 + part, parts) * patch, patch)
        for part in range(parts - 1)
    ]
    scale = F32(np.log2(np.e) / np.sqrt(HD))
    for head in range(heads):
        own = slice(head * HD, (head + 1) * HD)
        query = both[:, own]
        keys = [stale[0, pl.ds(start, patch), own] for start in starts]
        keys.append(both[:, (heads + head) * HD : (heads + head + 1) * HD])
        scores = [turned(query, key) for key in keys]
        top = functools.reduce(jnp.maximum, scores)
        top = jnp.max(top, axis=1, keepdims=True)
        total, summed = 0.0, 0.0
        for part, score in enumerate(scores):
            expo = jnp.exp2((score - top) * scale)
            total += expo
            expo = expo.astype(BF16)
            if part == parts - 1:
                expo_ref[head] = expo
                continue
            values = stale[1, pl.ds(starts[part], patch), own]
            summed += jnp.dot(expo, values, preferred_element_type=F32)
        share = 1.0 / jnp.sum(total, axis=1, keepdims=True)
        base_ref[head] = summed * share
        share_ref[head] = jnp.broadcast_to(share, (patch, HD))


def attend_kernel(count, first, sources_ref, normed, expo_ref, base_ref, share_ref, *rest):
    pieces, (out_ref, values, matrix, sems) = rest[:count], rest[count:]
    fetched([], pieces, first, sources_ref, matrix, sems)
    values[...] = jnp.dot(normed[...], matrix[...], preferred_element_type=F32).astype(BF16)
    for spot in range(expo_ref.shape[0]):
        own = slice(spot * HD, (spot + 1) * HD)
        new = jnp.dot(expo_ref[spot], values[:, own], preferred_element_type=F32)
        out_ref[:, own] = (base_ref[spot] + new * share_ref[spot]).astype(BF16)


def score(normed, pieces, sources, where, stale, group):
    patch, width = normed.shape
    heads, keys = len(group), stale.shape[1]
    columns = heads * HD
    stat = jax.ShapeDtypeStruct((heads, patch, HD), F32)
    cols = slice(group[0] * HD, group[0] * HD + columns)
    return pl.pallas_call(
        functools.partial(score_kernel, len(pieces), cols),
        in_specs=[SCALAR, SCALAR, WHOLE] + [ANYWHERE] * (1 + len(pieces)),
        out_specs=[WHOLE] * 3,
        out_shape=[jax.ShapeDtypeStruct((heads, patch, patch), BF16), stat, stat],
        scratch_shapes=[
            pltpu.VMEM((patch, 2 * columns), BF16),
            pltpu.VMEM((width, 2 * columns), BF16),
            pltpu.VMEM((2, keys, columns), BF16),
            pltpu.SemaphoreType.DMA((len(pieces) + 1,)),
        ],
        compiler_params=params(20),
        cost_estimate=cost(
            4 * patch * columns * (width + keys), 4 * columns * (width + keys), patch * heads * keys
        ),
        name="score",
    )(sources, where, normed, in_hbm(stale), *pieces)


def attend(normed, pieces, sources, first, expo, base, share):
    patch, width = normed.shape
    columns = expo.shape[0] * HD
    return pl.pallas_call(
        functools.partial(attend_kernel, len(pieces), first),
        in_specs=[SCALAR, WHOLE, WHOLE, WHOLE, WHOLE] + [ANYWHERE] * len(pieces),
        out_specs=WHOLE,
        out_shape=jax.ShapeDtypeStruct((patch, columns), BF16),
        scratch_shapes=[
            pltpu.VMEM((patch, columns), BF16),
            pltpu.VMEM((width, columns), BF16),
            pltpu.SemaphoreType.DMA((len(pieces),)),
        ],
        compiler_params=params(10),
        cost_estimate=cost(2 * patch * columns * (width + patch), 2 * columns * width),
        name="attend",
    )(sources, normed, expo, base, share, *pieces)


def output_kernel(tp, chunks, inflow_ref, gate_ref, *rest):
    attended, matrices, out_ref = rest[: tp * chunks], rest[tp * chunks : -1], rest[-1]
    mixed = 0.0
    for index in range(tp):
        own = attended[index * chunks : (index + 1) * chunks]
        left = jnp.concatenate([piece[...] for piece in own], axis=1)
        mixed += turned(left, matrices[index][...])
    out_ref[...] = (inflow_ref[...].astype(F32) + gate_ref[...] * mixed).astype(BF16)


def output(inflow, gate, attended, matrices):
    tp, chunks = len(attended), len(attended[0])
    patch, share = inflow.shape
    inner = matrices[0].shape[1]
    arrays = [inflow, gate] + [piece for own in attended for piece in own] + matrices
    return pl.pallas_call(
        functools.partial(output_kernel, tp, chunks),
        grid=(1,),
        in_specs=[pl.BlockSpec(array.shape, lambda i: (0, 0)) for array in arrays],
        out_specs=pl.BlockSpec(inflow.shape, lambda i: (0, 0)),
        out_shape=jax.ShapeDtypeStruct(inflow.shape, BF16),
        compiler_params=params(20),
        cost_estimate=cost(2 * patch * share * inner * tp, 2 * inner * tp * (share + patch)),
        name="output",
    )(*arrays)


def after(block, earlier):
    return lax.optimization_barrier((block, earlier))[0]


def swapped(block, axis, distance):
    return lax.ppermute(block, axis, [(i, i ^ distance) for i in range(lax.axis_size(axis))])


def handed_on(block):
    sections = lax.axis_size("section")
    return lax.ppermute(block, "section", [(i, (i + 1) % sections) for i in range(sections)])


class Relay:
    def __init__(self, window):
        self.window, self.sent = window, []

    def swap(self, piece, distance, *earlier):
        for other in (*earlier, *self.sent[-self.window :][:1]):
            piece = after(piece, other)
        self.sent.append(swapped(piece, "section", distance))
        return self.sent[-1]


def place_kernel(count, slots_ref, *rest):
    pieces, (out_ref, sems) = rest[:count], rest[count:]
    copies = [
        pltpu.make_async_copy(piece, out_ref.at[slots_ref[index]], sems.at[index])
        for index, piece in enumerate(pieces)
    ]
    for copy in copies:
        copy.start()
    for copy in copies:
        copy.wait()


def placed(pieces, slots):
    return pl.pallas_call(
        functools.partial(place_kernel, len(pieces)),
        in_specs=[SCALAR] + [ANYWHERE] * len(pieces),
        out_specs=ANYWHERE,
        out_shape=jax.ShapeDtypeStruct((len(pieces),) + pieces[0].shape, BF16),
        scratch_shapes=[pltpu.SemaphoreType.DMA((len(pieces),))],
        compiler_params=params(4),
        cost_estimate=cost(0, 4 * len(pieces) * pieces[0].size),
        name="placed",
    )(slots, *[in_hbm(piece) for piece in pieces])


def local(block_weights, modulation, inflow, stale_cache, patch_index, assignment):
    sections, tp = lax.axis_size("section"), lax.axis_size("tp")
    here, rank = lax.axis_index("section"), lax.axis_index("tp")
    blocks, depth, kinds, inner = block_weights.shape
    lanes = inner // HD
    share = inflow.shape[2]

    section_ids = jnp.arange(sections, dtype=jnp.int32)
    sources = here ^ section_ids
    order = sorted(range(1, sections), key=lambda d: (d == 1, d % 2, d))
    turn = here ^ jnp.asarray(order + [0], jnp.int32)

    def block_of(section):
        return jnp.sum((assignment[None] == section[:, None]) * section_ids[None], axis=1)

    rows = block_weights.reshape(blocks, depth, kinds, lanes, HD)
    rows = rows.transpose(0, 1, 3, 2, 4).reshape(blocks, depth * lanes * kinds, HD)
    tokens = lax.all_gather(inflow[0], "tp", axis=1, tiled=True)

    before = block_of((turn + sections - 1) % sections)
    out_plan = [[(3, head) for head in range(lanes)]]
    soon = split_blocks(rows, before, 0, 3, out_plan, lanes, True)[0]
    soon += split_blocks(rows, before, 3, sections - 3, out_plan, lanes, True)[0]
    to_out = dict(zip(order + [0], soon))
    size = max(1, lanes // 2)
    groups = [tuple(range(first, first + size)) for first in range(0, lanes, size)]
    plan = []
    for group in groups:
        plan.append([(kind, head) for kind in (0, 1) for head in group])
        values = [(2, head) for head in group]
        if group == groups[-1]:
            plan.append(values)
        else:
            plan[-1] += values
    split = split_blocks(rows, block_of(turn), 0, sections, plan, lanes, False)
    split = [dict(zip(order + [0], made)) for made in split]

    relay = Relay(4)
    for distance in order:
        to_out[distance] = relay.swap(to_out[distance], distance)
    per = sections // tp
    slots = ((sources // per) ^ rank) * per + sources % per
    held = placed([to_out[d] for d in range(sections)], slots).reshape(tp, per * depth, inner)
    matrices = [held[0]]
    for distance in range(1, tp):
        matrices.append(swapped(after(held[distance], matrices[-1]), "tp", distance))
    normed = norm(tokens, modulation[0])
    gate = handed_on(modulation[0, 2])

    def relayed(stage, waits):
        pieces = [split[stage][0]] * sections
        for index, distance in enumerate(order):
            wait = waits.get(index, ())
            pieces[distance] = relay.swap(split[stage][distance], distance, *wait)
        return pieces

    attended = [[] for _ in range(tp)]

    def share_out(part):
        moved = handed_on(part)
        for distance in range(tp):
            attended[distance].append(swapped(moved, "tp", distance) if distance else moved)
        return moved

    last = sections - 2
    waits = {0: (gate,), last - 1: (matrices[1],), last: (normed,)}
    for stage, group in enumerate(groups[:-1]):
        pieces = relayed(stage, waits)
        stats = score(normed, pieces, sources, patch_index, stale_cache[0], group)
        own = attend(normed, pieces, sources, 2 * len(group) * HD, *stats)
        moved = share_out(own)
        waits = {2: (matrices[2],), min(4, last): (own,), last: (moved,)}
    pieces = relayed(len(plan) - 2, waits)
    stats = score(normed, pieces, sources, patch_index, stale_cache[0], groups[-1])
    value_pieces = relayed(len(plan) - 1, {last: (stats[0], matrices[-1])})
    ready = functools.reduce(after, [part for own in attended for part in own], stats[0])
    own = attend(normed, value_pieces, sources, 0, ready, *stats[1:])
    moved = share_out(own)
    carried = handed_on(after(inflow[0], moved))
    gate = lax.dynamic_slice_in_dim(gate, rank * share, share, 0)[None]
    return output(carried, gate, attended, matrices)[None]


def solution(mesh):
    spread = (
        P(None, "section", None, "tp"),
        P("section", None, None),
        P("section", None, "tp"),
        P("section", None, None, "tp"),
        P("section"),
        P(),
    )
    return jax.shard_map(
        local, mesh=mesh, in_specs=spread, out_specs=P("section", None, "tp"), check_vma=False
    )
```

```python
import functools

import jax
import jax.numpy as jnp
import numpy as np
from jax import lax
from jax.experimental import pallas as pl
from jax.experimental.pallas import tpu as pltpu
from jax.sharding import PartitionSpec as P

HD = 128
F32 = jnp.float32
BF16 = jnp.bfloat16
WHOLE = pl.BlockSpec(memory_space=pltpu.VMEM)
ANYWHERE = pl.BlockSpec(memory_space=pl.ANY)
SCALAR = pl.BlockSpec(memory_space=pltpu.SMEM)


def params(mebibytes):
    return pltpu.CompilerParams(vmem_limit_bytes=mebibytes * 1024 * 1024)


def in_hbm(array):
    return pltpu.with_memory_space_constraint(array, pltpu.HBM)


def cost(flops, size, exps=0):
    return pl.CostEstimate(flops=flops, bytes_accessed=size, transcendentals=exps)


def turned(left, right):
    return lax.dot_general(left, right, (((1,), (1,)), ((), ())), preferred_element_type=F32)


def pick_matrix(kinds, lanes, depth_step):
    period = 4 * lanes
    shape = (len(kinds) * lanes * depth_step, period * depth_step)
    row = lax.broadcasted_iota(jnp.int32, shape, 0)
    column = lax.broadcasted_iota(jnp.int32, shape, 1)
    source = row % depth_step * period + row // depth_step % lanes * 4 + kinds[0]
    source += row // (lanes * depth_step)
    return jnp.where(source == column, 1.0, 0.0).astype(BF16)


def split_kernel(lanes, plan, kinds, depth_step, order_ref, rows_ref, *rest):
    outs, pick = rest[:-1], rest[-1]
    depth = rows_ref.shape[1] // (4 * lanes)
    chunk = depth_step * 4 * lanes
    beside = 2 if depth % (2 * depth_step) == 0 else 1

    @pl.when(pl.program_id(0) == 0)
    def _():
        pick[...] = pick_matrix(kinds, lanes, depth_step)

    for first in range(0, depth, beside * depth_step):
        begin = first * 4 * lanes
        chunks = [
            rows_ref[0, begin + i * chunk : begin + (i + 1) * chunk, :] for i in range(beside)
        ]
        sorted_rows = jnp.dot(
            pick[...], jnp.concatenate(chunks, axis=1), preferred_element_type=F32
        ).astype(BF16)
        for i in range(beside):
            to = slice(first + i * depth_step, first + (i + 1) * depth_step)
            for out, columns in zip(outs, plan):
                for column, (kind, lane) in enumerate(columns):
                    at = (kinds.index(kind) * lanes + lane) * depth_step
                    out[0, to, column * HD : (column + 1) * HD] = sorted_rows[
                        at : at + depth_step, i * HD : (i + 1) * HD
                    ]


def split_blocks(rows, order, plan, lanes):
    depth = rows.shape[1] // (4 * lanes)
    depth_step = max(n for n in (16, 32, 64) if depth % n == 0 and n * 4 * lanes <= 256)
    kinds = sorted({kind for columns in plan for kind, _ in columns})
    blocks = order.shape[0]
    shapes = [(blocks, depth, len(columns) * HD) for columns in plan]
    return pl.pallas_call(
        functools.partial(split_kernel, lanes, plan, kinds, depth_step),
        grid_spec=pltpu.PrefetchScalarGridSpec(
            num_scalar_prefetch=1,
            grid=(blocks,),
            in_specs=[pl.BlockSpec((1,) + rows.shape[1:], lambda i, order: (order[i], 0, 0))],
            out_specs=[pl.BlockSpec((1,) + shape[1:], lambda i, order: (i, 0, 0)) for shape in shapes],
            scratch_shapes=[
                pltpu.VMEM((len(kinds) * lanes * depth_step, depth_step * 4 * lanes), BF16)
            ],
        ),
        out_shape=[jax.ShapeDtypeStruct(shape, BF16) for shape in shapes],
        compiler_params=params(16),
        cost_estimate=cost(0, 3 * blocks * rows.shape[1] * HD),
        name="split_blocks",
    )(order, in_hbm(rows))


def norm_kernel(tokens_ref, modulation_ref, out_ref):
    tokens = tokens_ref[...].astype(F32)
    center = jnp.mean(tokens, axis=1, keepdims=True)
    tokens = tokens - center
    spread = jnp.mean(tokens * tokens, axis=1, keepdims=True)
    normed = tokens * lax.rsqrt(spread + 1e-06)
    out_ref[...] = (normed * (1.0 + modulation_ref[0:1]) + modulation_ref[1:2]).astype(BF16)


def norm(tokens, modulation):
    patch, width = tokens.shape
    rows = 128
    return pl.pallas_call(
        norm_kernel,
        grid=(patch // rows,),
        in_specs=[
            pl.BlockSpec((rows, width), lambda i: (i, 0)),
            pl.BlockSpec((3, width), lambda i: (0, 0)),
        ],
        out_specs=pl.BlockSpec((rows, width), lambda i: (i, 0)),
        out_shape=jax.ShapeDtypeStruct((patch, width), BF16),
        compiler_params=params(14),
        cost_estimate=cost(10 * patch * width, 4 * patch * width),
        name="norm",
    )(in_hbm(tokens), modulation)


def attend_kernel(where_ref, normed_ref, matrix_ref, stale_ref, out_ref, own):
    patch = normed_ref.shape[0]
    parts = stale_ref.shape[1] // patch
    own[...] = jnp.dot(normed_ref[...], matrix_ref[...], preferred_element_type=F32).astype(BF16)
    starts = [
        pl.multiple_of(lax.rem(where_ref[0] + 1 + part, parts) * patch, patch)
        for part in range(parts - 1)
    ]
    scale = F32(np.log2(np.e) / np.sqrt(HD))
    keys = [stale_ref[0, pl.ds(start, patch), :] for start in starts] + [own[:, HD : 2 * HD]]
    values = [stale_ref[1, pl.ds(start, patch), :] for start in starts] + [own[:, 2 * HD :]]
    scores = [turned(own[:, :HD], key) for key in keys]
    top = jnp.max(functools.reduce(jnp.maximum, scores), axis=1, keepdims=True)
    total, summed = 0.0, 0.0
    for score, value in zip(scores, values):
        expo = jnp.exp2((score - top) * scale)
        total += expo
        summed += jnp.dot(expo.astype(BF16), value, preferred_element_type=F32)
    out_ref[...] = (summed / jnp.sum(total, axis=1, keepdims=True)).astype(BF16)


def attend(normed, matrix, where, stale, group):
    patch, width = normed.shape
    heads, keys = len(group), stale.shape[1]
    first = group[0]
    return pl.pallas_call(
        attend_kernel,
        grid_spec=pltpu.PrefetchScalarGridSpec(
            num_scalar_prefetch=1,
            grid=(heads,),
            in_specs=[
                pl.BlockSpec((patch, width), lambda h, where: (0, 0)),
                pl.BlockSpec((width, 3 * HD), lambda h, where: (0, h)),
                pl.BlockSpec((2, keys, HD), lambda h, where: (0, 0, first + h)),
            ],
            out_specs=pl.BlockSpec((patch, HD), lambda h, where: (0, h)),
            scratch_shapes=[pltpu.VMEM((patch, 3 * HD), BF16)],
        ),
        out_shape=jax.ShapeDtypeStruct((patch, heads * HD), BF16),
        compiler_params=params(32),
        cost_estimate=cost(
            2 * patch * heads * HD * (3 * width + 2 * keys), 2 * heads * HD * (3 * width + 2 * keys),
            patch * heads * keys,
        ),
        name="attend",
    )(where, normed, matrix, stale)


def output_kernel(tp, chunks, inflow_ref, gate_ref, *rest):
    attended, matrices, out_ref = rest[: tp * chunks], rest[tp * chunks : -1], rest[-1]
    mixed = 0.0
    for index in range(tp):
        own = attended[index * chunks : (index + 1) * chunks]
        left = jnp.concatenate([piece[...] for piece in own], axis=1)
        mixed += turned(left, matrices[index][...])
    out_ref[...] = (inflow_ref[...].astype(F32) + gate_ref[...] * mixed).astype(BF16)


def output(inflow, gate, attended, matrices):
    tp, chunks = len(attended), len(attended[0])
    patch, share = inflow.shape
    inner = matrices[0].shape[1]
    arrays = [inflow, gate] + [piece for own in attended for piece in own] + matrices
    return pl.pallas_call(
        functools.partial(output_kernel, tp, chunks),
        grid=(1,),
        in_specs=[pl.BlockSpec(array.shape, lambda i: (0, 0)) for array in arrays],
        out_specs=pl.BlockSpec(inflow.shape, lambda i: (0, 0)),
        out_shape=jax.ShapeDtypeStruct(inflow.shape, BF16),
        compiler_params=params(20),
        cost_estimate=cost(2 * patch * share * inner * tp, 2 * inner * tp * (share + patch)),
        name="output",
    )(*arrays)


def after(block, earlier):
    return lax.optimization_barrier((block, earlier))[0]


def swapped(block, axis, distance):
    return lax.ppermute(block, axis, [(i, i ^ distance) for i in range(lax.axis_size(axis))])


def handed_on(block):
    sections = lax.axis_size("section")
    return lax.ppermute(block, "section", [(i, (i + 1) % sections) for i in range(sections)])


def relayed(pieces):
    moved = lax.all_to_all(pieces, "section", split_axis=0, concat_axis=0, tiled=True)
    return moved.reshape(-1, moved.shape[2])


def local(block_weights, modulation, inflow, stale_cache, patch_index, assignment):
    sections, tp = lax.axis_size("section"), lax.axis_size("tp")
    rank = lax.axis_index("tp")
    blocks, depth, kinds, inner = block_weights.shape
    lanes = inner // HD
    share = inflow.shape[2]

    section_ids = jnp.arange(sections, dtype=jnp.int32)

    def block_of(section):
        return jnp.sum((assignment[None] == section[:, None]) * section_ids[None], axis=1)

    rows = block_weights.reshape(blocks, depth, kinds, lanes, HD)
    rows = rows.transpose(0, 1, 3, 2, 4).reshape(blocks, depth * lanes * kinds, HD)
    tokens = lax.all_gather(inflow[0], "tp", axis=1, tiled=True)

    out_plan = [[(3, head) for head in range(lanes)]]
    (to_out,) = split_blocks(rows, block_of((section_ids + sections - 1) % sections), out_plan, lanes)
    half = max(1, lanes // 2)
    groups = [tuple(range(half))] + [(head,) for head in range(half, lanes)]
    plan = [[(kind, head) for head in group for kind in range(3)] for group in groups]
    split = split_blocks(rows, block_of(section_ids), plan, lanes)

    to_out = relayed(to_out)
    normed = norm(tokens, modulation[0])
    matrices = []
    for distance in range(tp):
        held = lax.dynamic_slice_in_dim(to_out, (rank ^ distance) * share, share, 0)
        if distance > 2:
            held = after(held, matrices[distance - 2])
        matrices.append(swapped(held, "tp", distance) if distance else held)
    gate = handed_on(modulation[0, 2])

    waits = [[], [normed, gate, *matrices[1:3]], matrices[3:]]
    attended = [[] for _ in range(tp)]
    ready = normed
    for index, group in enumerate(groups):
        pieces = split[index]
        for earlier in waits[index] if index < len(waits) else []:
            pieces = after(pieces, earlier)
        matrix = relayed(pieces)
        own = attend(ready, matrix, patch_index, stale_cache[0], group)
        moved = handed_on(own)
        for distance in range(tp):
            attended[distance].append(swapped(moved, "tp", distance) if distance else moved)
        if index + 2 < len(groups):
            waits[index + 2] = [*waits[index + 2], *[own[-1] for own in attended]]
        elif index + 1 < len(groups):
            ready = functools.reduce(after, [own[-1] for own in attended], ready)
    carried = handed_on(after(inflow[0], moved))
    gate = lax.dynamic_slice_in_dim(gate, rank * share, share, 0)[None]
    return output(carried, gate, attended, matrices)[None]


def solution(mesh):
    spread = (
        P(None, "section", None, "tp"),
        P("section", None, None),
        P("section", None, "tp"),
        P("section", None, None, "tp"),
        P("section"),
        P(),
    )
    return jax.shard_map(
        local, mesh=mesh, in_specs=spread, out_specs=P("section", None, "tp"), check_vma=False
    )
```

```python
import functools

import jax
import jax.numpy as jnp
import numpy as np
from jax import lax
from jax.experimental import pallas as pl
from jax.experimental.pallas import tpu as pltpu
from jax.sharding import PartitionSpec as P

HD = 128
F32 = jnp.float32
BF16 = jnp.bfloat16
WHOLE = pl.BlockSpec(memory_space=pltpu.VMEM)
ANYWHERE = pl.BlockSpec(memory_space=pl.ANY)
SCALAR = pl.BlockSpec(memory_space=pltpu.SMEM)


def params(mebibytes):
    return pltpu.CompilerParams(vmem_limit_bytes=mebibytes * 1024 * 1024)


def in_hbm(array):
    return pltpu.with_memory_space_constraint(array, pltpu.HBM)


def cost(flops, size, exps=0):
    return pl.CostEstimate(flops=flops, bytes_accessed=size, transcendentals=exps)


def turned(left, right):
    return lax.dot_general(left, right, (((1,), (1,)), ((), ())), preferred_element_type=F32)


def pick_matrix(kinds, lanes, depth_step):
    period = 4 * lanes
    shape = (len(kinds) * lanes * depth_step, period * depth_step)
    row = lax.broadcasted_iota(jnp.int32, shape, 0)
    column = lax.broadcasted_iota(jnp.int32, shape, 1)
    source = row % depth_step * period + row // depth_step % lanes * 4 + kinds[0]
    source += row // (lanes * depth_step)
    return jnp.where(source == column, 1.0, 0.0).astype(BF16)


def split_kernel(lanes, plan, single, kinds, depth_step, order_ref, to_ref, rows_ref, *rest):
    outs, pick = rest[:-1], rest[-1]
    depth = rows_ref.shape[1] // (4 * lanes)
    chunk = depth_step * 4 * lanes
    beside = 2 if depth % (2 * depth_step) == 0 else 1

    @pl.when(pl.program_id(0) == 0)
    def _():
        pick[...] = pick_matrix(kinds, lanes, depth_step)

    def store(out, to, columns, values):
        out[to, columns] = values

    for first in range(0, depth, beside * depth_step):
        begin = first * 4 * lanes
        chunks = [
            rows_ref[0, begin + i * chunk : begin + (i + 1) * chunk, :] for i in range(beside)
        ]
        sorted_rows = jnp.dot(
            pick[...], jnp.concatenate(chunks, axis=1), preferred_element_type=F32
        ).astype(BF16)
        for i in range(beside):
            to = slice(first + i * depth_step, first + (i + 1) * depth_step)
            for out, columns in zip(outs, plan):
                for column, (kind, lane) in enumerate(columns):
                    at = (kinds.index(kind) * lanes + lane) * depth_step
                    values = sorted_rows[at : at + depth_step, i * HD : (i + 1) * HD]
                    spot = slice(column * HD, (column + 1) * HD)
                    if columns is not plan[-1] or not single:
                        out[0, to, spot] = values
                        continue
                    for block, own in enumerate(outs[len(plan) - 1 :]):
                        pl.when(pl.program_id(0) == block)(
                            functools.partial(store, own, to, spot, values)
                        )


def split_blocks(rows, order, to, plan, lanes, single=False):
    depth = rows.shape[1] // (4 * lanes)
    depth_step = max(n for n in (16, 32, 64) if depth % n == 0 and n * 4 * lanes <= 256)
    kinds = sorted({kind for columns in plan for kind, _ in columns})
    blocks = order.shape[0]
    shapes = [(blocks, depth, len(columns) * HD) for columns in plan]
    out_specs = [
        pl.BlockSpec((1,) + shape[1:], lambda i, order, to: (to[i], 0, 0)) for shape in shapes
    ]
    if single:
        alone = shapes.pop()[1:]
        shapes += [alone] * blocks
        out_specs[-1:] = [pl.BlockSpec(alone, lambda i, order, to: (0, 0))] * blocks
    return pl.pallas_call(
        functools.partial(split_kernel, lanes, plan, single, kinds, depth_step),
        grid_spec=pltpu.PrefetchScalarGridSpec(
            num_scalar_prefetch=2,
            grid=(blocks,),
            in_specs=[pl.BlockSpec((1,) + rows.shape[1:], lambda i, order, to: (order[i], 0, 0))],
            out_specs=out_specs,
            scratch_shapes=[
                pltpu.VMEM((len(kinds) * lanes * depth_step, depth_step * 4 * lanes), BF16)
            ],
        ),
        out_shape=[jax.ShapeDtypeStruct(shape, BF16) for shape in shapes],
        compiler_params=params(24),
        cost_estimate=cost(0, 3 * blocks * rows.shape[1] * HD),
        name="split_blocks",
    )(order, to, in_hbm(rows))


def norm_kernel(tokens_ref, modulation_ref, out_ref):
    tokens = tokens_ref[...].astype(F32)
    center = jnp.mean(tokens, axis=1, keepdims=True)
    tokens = tokens - center
    spread = jnp.mean(tokens * tokens, axis=1, keepdims=True)
    normed = tokens * lax.rsqrt(spread + 1e-06)
    out_ref[...] = (normed * (1.0 + modulation_ref[0:1]) + modulation_ref[1:2]).astype(BF16)


def norm(tokens, modulation):
    patch, width = tokens.shape
    rows = 128
    return pl.pallas_call(
        norm_kernel,
        grid=(patch // rows,),
        in_specs=[
            pl.BlockSpec((rows, width), lambda i: (i, 0)),
            pl.BlockSpec((3, width), lambda i: (0, 0)),
        ],
        out_specs=pl.BlockSpec((rows, width), lambda i: (i, 0)),
        out_shape=jax.ShapeDtypeStruct((patch, width), BF16),
        compiler_params=params(14),
        cost_estimate=cost(10 * patch * width, 4 * patch * width),
        name="norm",
    )(in_hbm(tokens), modulation)


def attend_kernel(where_ref, normed_ref, matrix_ref, stale_ref, out_ref, own):
    patch = normed_ref.shape[0]
    parts = stale_ref.shape[1] // patch
    own[...] = jnp.dot(normed_ref[...], matrix_ref[...], preferred_element_type=F32).astype(BF16)
    starts = [
        pl.multiple_of(lax.rem(where_ref[0] + 1 + part, parts) * patch, patch)
        for part in range(parts - 1)
    ]
    scale = F32(np.log2(np.e) / np.sqrt(HD))
    keys = [stale_ref[0, pl.ds(start, patch), :] for start in starts] + [own[:, HD : 2 * HD]]
    values = [stale_ref[1, pl.ds(start, patch), :] for start in starts] + [own[:, 2 * HD :]]
    scores = [turned(own[:, :HD], key) for key in keys]
    top = jnp.max(functools.reduce(jnp.maximum, scores), axis=1, keepdims=True)
    total, summed = 0.0, 0.0
    for score, value in zip(scores, values):
        expo = jnp.exp2((score - top) * scale)
        total += expo
        summed += jnp.dot(expo.astype(BF16), value, preferred_element_type=F32)
    out_ref[...] = (summed / jnp.sum(total, axis=1, keepdims=True)).astype(BF16)


def attend(normed, matrix, where, stale, group):
    patch, width = normed.shape
    heads, keys = len(group), stale.shape[1]
    first = group[0]
    return pl.pallas_call(
        attend_kernel,
        grid_spec=pltpu.PrefetchScalarGridSpec(
            num_scalar_prefetch=1,
            grid=(heads,),
            in_specs=[
                pl.BlockSpec((patch, width), lambda h, where: (0, 0)),
                pl.BlockSpec((width, 3 * HD), lambda h, where: (0, h)),
                pl.BlockSpec((2, keys, HD), lambda h, where: (0, 0, first + h)),
            ],
            out_specs=pl.BlockSpec((patch, HD), lambda h, where: (0, h)),
            scratch_shapes=[pltpu.VMEM((patch, 3 * HD), BF16)],
        ),
        out_shape=jax.ShapeDtypeStruct((patch, heads * HD), BF16),
        compiler_params=params(32),
        cost_estimate=cost(
            2 * patch * heads * HD * (3 * width + 2 * keys), 2 * heads * HD * (3 * width + 2 * keys),
            patch * heads * keys,
        ),
        name="attend",
    )(where, normed, matrix, stale)


def output_kernel(tp, chunks, inflow_ref, gate_ref, *rest):
    attended, matrices, out_ref = rest[: tp * chunks], rest[tp * chunks : -1], rest[-1]
    mixed = 0.0
    for index in range(tp):
        own = attended[index * chunks : (index + 1) * chunks]
        left = jnp.concatenate([piece[...] for piece in own], axis=1)
        mixed += turned(left, matrices[index][...])
    out_ref[...] = (inflow_ref[...].astype(F32) + gate_ref[...] * mixed).astype(BF16)


def output(inflow, gate, attended, matrices):
    tp, chunks = len(attended), len(attended[0])
    patch, share = inflow.shape
    inner = matrices[0].shape[1]
    arrays = [inflow, gate] + [piece for own in attended for piece in own] + matrices
    return pl.pallas_call(
        functools.partial(output_kernel, tp, chunks),
        grid=(1,),
        in_specs=[pl.BlockSpec(array.shape, lambda i: (0, 0)) for array in arrays],
        out_specs=pl.BlockSpec(inflow.shape, lambda i: (0, 0)),
        out_shape=jax.ShapeDtypeStruct(inflow.shape, BF16),
        compiler_params=params(20),
        cost_estimate=cost(2 * patch * share * inner * tp, 2 * inner * tp * (share + patch)),
        name="output",
    )(*arrays)


def after(block, earlier):
    return lax.optimization_barrier((block, earlier))[0]


def swapped(block, axis, distance):
    return lax.ppermute(block, axis, [(i, i ^ distance) for i in range(lax.axis_size(axis))])


def handed_on(block):
    sections = lax.axis_size("section")
    return lax.ppermute(block, "section", [(i, (i + 1) % sections) for i in range(sections)])


def relayed(pieces):
    moved = lax.all_to_all(pieces, "section", split_axis=0, concat_axis=0, tiled=True)
    return moved.reshape(-1, moved.shape[2])


def place_kernel(count, slots_ref, *rest):
    pieces, (out_ref, sems) = rest[:count], rest[count:]
    copies = [
        pltpu.make_async_copy(piece, out_ref.at[slots_ref[index]], sems.at[index])
        for index, piece in enumerate(pieces)
    ]
    for copy in copies:
        copy.start()
    for copy in copies:
        copy.wait()


def placed(pieces, slots):
    return pl.pallas_call(
        functools.partial(place_kernel, len(pieces)),
        in_specs=[SCALAR] + [ANYWHERE] * len(pieces),
        out_specs=ANYWHERE,
        out_shape=jax.ShapeDtypeStruct((len(pieces),) + pieces[0].shape, BF16),
        scratch_shapes=[pltpu.SemaphoreType.DMA((len(pieces),))],
        compiler_params=params(4),
        cost_estimate=cost(0, 4 * len(pieces) * pieces[0].size),
        name="placed",
    )(slots, *[in_hbm(piece) for piece in pieces])


def local(block_weights, modulation, inflow, stale_cache, patch_index, assignment):
    sections, tp = lax.axis_size("section"), lax.axis_size("tp")
    here, rank = lax.axis_index("section"), lax.axis_index("tp")
    blocks, depth, kinds, inner = block_weights.shape
    lanes = inner // HD
    share = inflow.shape[2]

    section_ids = jnp.arange(sections, dtype=jnp.int32)
    sources = here ^ section_ids

    def block_of(section):
        return jnp.sum((assignment[None] == section[:, None]) * section_ids[None], axis=1)

    rows = block_weights.reshape(blocks, depth, kinds, lanes, HD)
    rows = rows.transpose(0, 1, 3, 2, 4).reshape(blocks, depth * lanes * kinds, HD)
    tokens = lax.all_gather(inflow[0], "tp", axis=1, tiled=True)
    normed = norm(tokens, modulation[0])
    gate = handed_on(modulation[0, 2])

    out_plan = [[(3, head) for head in range(lanes)]]
    before = block_of((section_ids + sections - 1) % sections)
    (to_out,) = split_blocks(rows, before, section_ids, out_plan, lanes)
    half = max(1, lanes // 2)
    groups = [tuple(range(half))] + [(head,) for head in range(half, lanes)]
    plan = [[(kind, head) for head in group for kind in range(3)] for group in groups]
    alone = len(groups) > 1
    split = split_blocks(rows, after(block_of(sources), to_out), sources, plan, lanes, alone)

    pieces = list(split[len(groups) - 1 :]) if alone else []
    chain = []
    for distance in sorted(range(1, len(pieces)), key=lambda d: (d == 1, d % 2, d)):
        piece = pieces[distance]
        if len(chain) >= 3:
            piece = after(piece, chain[-3])
        chain.append(swapped(piece, "section", distance))
        pieces[distance] = chain[-1]

    to_out = relayed(to_out)
    matrices = []
    for distance in range(tp):
        held = lax.dynamic_slice_in_dim(to_out, (rank ^ distance) * share, share, 0)
        matrices.append(swapped(held, "tp", distance) if distance else held)

    attended = [[] for _ in range(tp)]

    def share_out(group, matrix, tokens):
        own = attend(tokens, matrix, patch_index, stale_cache[0], group)
        moved = handed_on(own)
        for distance in range(tp):
            attended[distance].append(swapped(moved, "tp", distance) if distance else moved)
        return moved

    def waiting(block, *earlier):
        return functools.reduce(after, earlier, block)

    first = relayed(waiting(split[0], normed, gate, *chain))
    if alone:
        last = relayed(waiting(split[1], *matrices[1:3]))
        matrix = placed(pieces, sources)
        share_out(groups[2], matrix.reshape(-1, matrix.shape[2]), normed)
        share_out(groups[0], first, normed)
        ready = waiting(normed, *matrices[3:], *[part for own in attended for part in own])
        moved = share_out(groups[1], last, ready)
    else:
        moved = share_out(groups[0], first, normed)
    heads_first = [own[1:2] + own[2:] + own[:1] if alone else own for own in attended]
    carried = handed_on(after(inflow[0], moved))
    gate = lax.dynamic_slice_in_dim(gate, rank * share, share, 0)[None]
    return output(carried, gate, heads_first, matrices)[None]


def solution(mesh):
    spread = (
        P(None, "section", None, "tp"),
        P("section", None, None),
        P("section", None, "tp"),
        P("section", None, None, "tp"),
        P("section"),
        P(),
    )
    return jax.shard_map(
        local, mesh=mesh, in_specs=spread, out_specs=P("section", None, "tp"), check_vma=False
    )
```

```python
import functools

import jax
import jax.numpy as jnp
import numpy as np
from jax import lax
from jax.experimental import pallas as pl
from jax.experimental.pallas import tpu as pltpu
from jax.sharding import PartitionSpec as P

HD = 128
F32 = jnp.float32
BF16 = jnp.bfloat16
WHOLE = pl.BlockSpec(memory_space=pltpu.VMEM)
ANYWHERE = pl.BlockSpec(memory_space=pl.ANY)
SCALAR = pl.BlockSpec(memory_space=pltpu.SMEM)


def params(mebibytes):
    return pltpu.CompilerParams(vmem_limit_bytes=mebibytes * 1024 * 1024)


def in_hbm(array):
    return pltpu.with_memory_space_constraint(array, pltpu.HBM)


def cost(flops, size, exps=0):
    return pl.CostEstimate(flops=flops, bytes_accessed=size, transcendentals=exps)


def turned(left, right):
    return lax.dot_general(left, right, (((1,), (1,)), ((), ())), preferred_element_type=F32)


def pick_matrix(kinds, lanes, depth_step):
    period = 4 * lanes
    shape = (len(kinds) * lanes * depth_step, period * depth_step)
    row = lax.broadcasted_iota(jnp.int32, shape, 0)
    column = lax.broadcasted_iota(jnp.int32, shape, 1)
    source = row % depth_step * period + row // depth_step % lanes * 4 + kinds[0]
    source += row // (lanes * depth_step)
    return jnp.where(source == column, 1.0, 0.0).astype(BF16)


def split_kernel(lanes, plan, single, kinds, depth_step, order_ref, to_ref, rows_ref, *rest):
    outs, pick, alone = rest[: len(plan) - single], rest[-2], rest[-1]
    singles = rest[len(outs) : -2]
    depth = rows_ref.shape[1] // (4 * lanes)
    chunk = depth_step * 4 * lanes
    beside = 2 if depth % (2 * depth_step) == 0 else 1

    @pl.when(pl.program_id(0) == 0)
    def _():
        pick[...] = pick_matrix(kinds, lanes, depth_step)

    targets = [out.at[0] for out in outs] + [alone] * single
    for first in range(0, depth, beside * depth_step):
        begin = first * 4 * lanes
        chunks = [
            rows_ref[0, begin + i * chunk : begin + (i + 1) * chunk, :] for i in range(beside)
        ]
        sorted_rows = jnp.dot(
            pick[...], jnp.concatenate(chunks, axis=1), preferred_element_type=F32
        ).astype(BF16)
        for i in range(beside):
            to = slice(first + i * depth_step, first + (i + 1) * depth_step)
            for out, columns in zip(targets, plan):
                for column, (kind, lane) in enumerate(columns):
                    at = (kinds.index(kind) * lanes + lane) * depth_step
                    out[to, column * HD : (column + 1) * HD] = sorted_rows[
                        at : at + depth_step, i * HD : (i + 1) * HD
                    ]

    def keep(own):
        own[...] = alone[...]

    for block, own in enumerate(singles):
        pl.when(pl.program_id(0) == block)(functools.partial(keep, own))


def split_blocks(rows, order, to, plan, lanes, single=False):
    depth = rows.shape[1] // (4 * lanes)
    depth_step = max(n for n in (16, 32, 64) if depth % n == 0 and n * 4 * lanes <= 256)
    kinds = sorted({kind for columns in plan for kind, _ in columns})
    blocks = order.shape[0]
    shapes = [(blocks, depth, len(columns) * HD) for columns in plan]
    out_specs = [
        pl.BlockSpec((1,) + shape[1:], lambda i, order, to: (to[i], 0, 0)) for shape in shapes
    ]
    if single:
        alone = shapes.pop()[1:]
        shapes += [alone] * blocks
        out_specs[-1:] = [pl.BlockSpec(alone, lambda i, order, to: (0, 0))] * blocks
    return pl.pallas_call(
        functools.partial(split_kernel, lanes, plan, single, kinds, depth_step),
        grid_spec=pltpu.PrefetchScalarGridSpec(
            num_scalar_prefetch=2,
            grid=(blocks,),
            in_specs=[pl.BlockSpec((1,) + rows.shape[1:], lambda i, order, to: (order[i], 0, 0))],
            out_specs=out_specs,
            scratch_shapes=[
                pltpu.VMEM((len(kinds) * lanes * depth_step, depth_step * 4 * lanes), BF16),
                pltpu.VMEM((depth, len(plan[-1]) * HD), BF16),
            ],
        ),
        out_shape=[jax.ShapeDtypeStruct(shape, BF16) for shape in shapes],
        compiler_params=params(32),
        cost_estimate=cost(0, 3 * blocks * rows.shape[1] * HD),
        name="split_blocks",
    )(order, to, in_hbm(rows))


def norm_kernel(tokens_ref, modulation_ref, out_ref):
    tokens = tokens_ref[...].astype(F32)
    center = jnp.mean(tokens, axis=1, keepdims=True)
    tokens = tokens - center
    spread = jnp.mean(tokens * tokens, axis=1, keepdims=True)
    normed = tokens * lax.rsqrt(spread + 1e-06)
    out_ref[...] = (normed * (1.0 + modulation_ref[0:1]) + modulation_ref[1:2]).astype(BF16)


def norm(tokens, modulation):
    patch, width = tokens.shape
    rows = 128
    return pl.pallas_call(
        norm_kernel,
        grid=(patch // rows,),
        in_specs=[
            pl.BlockSpec((rows, width), lambda i: (i, 0)),
            pl.BlockSpec((3, width), lambda i: (0, 0)),
        ],
        out_specs=pl.BlockSpec((rows, width), lambda i: (i, 0)),
        out_shape=jax.ShapeDtypeStruct((patch, width), BF16),
        compiler_params=params(14),
        cost_estimate=cost(10 * patch * width, 4 * patch * width),
        name="norm",
    )(in_hbm(tokens), modulation)


def attend_kernel(where_ref, normed_ref, matrix_ref, stale_ref, out_ref, own):
    patch = normed_ref.shape[0]
    parts = stale_ref.shape[1] // patch
    own[...] = jnp.dot(normed_ref[...], matrix_ref[...], preferred_element_type=F32).astype(BF16)
    starts = [
        pl.multiple_of(lax.rem(where_ref[0] + 1 + part, parts) * patch, patch)
        for part in range(parts - 1)
    ]
    scale = F32(np.log2(np.e) / np.sqrt(HD))
    keys = [stale_ref[0, pl.ds(start, patch), :] for start in starts] + [own[:, HD : 2 * HD]]
    values = [stale_ref[1, pl.ds(start, patch), :] for start in starts] + [own[:, 2 * HD :]]
    scores = [turned(own[:, :HD], key) for key in keys]
    top = jnp.max(functools.reduce(jnp.maximum, scores), axis=1, keepdims=True)
    total, summed = 0.0, 0.0
    for score, value in zip(scores, values):
        expo = jnp.exp2((score - top) * scale)
        total += expo
        summed += jnp.dot(expo.astype(BF16), value, preferred_element_type=F32)
    out_ref[...] = (summed / jnp.sum(total, axis=1, keepdims=True)).astype(BF16)


def attend(normed, matrix, where, stale, group):
    patch, width = normed.shape
    heads, keys = len(group), stale.shape[1]
    first = group[0]
    return pl.pallas_call(
        attend_kernel,
        grid_spec=pltpu.PrefetchScalarGridSpec(
            num_scalar_prefetch=1,
            grid=(heads,),
            in_specs=[
                pl.BlockSpec((patch, width), lambda h, where: (0, 0)),
                pl.BlockSpec((width, 3 * HD), lambda h, where: (0, h)),
                pl.BlockSpec((2, keys, HD), lambda h, where: (0, 0, first + h)),
            ],
            out_specs=pl.BlockSpec((patch, HD), lambda h, where: (0, h)),
            scratch_shapes=[pltpu.VMEM((patch, 3 * HD), BF16)],
        ),
        out_shape=jax.ShapeDtypeStruct((patch, heads * HD), BF16),
        compiler_params=params(32),
        cost_estimate=cost(
            2 * patch * heads * HD * (3 * width + 2 * keys), 2 * heads * HD * (3 * width + 2 * keys),
            patch * heads * keys,
        ),
        name="attend",
    )(where, normed, matrix, stale)


def output_kernel(tp, chunks, inflow_ref, gate_ref, *rest):
    attended, matrices, out_ref = rest[: tp * chunks], rest[tp * chunks : -1], rest[-1]
    mixed = 0.0
    for index in range(tp):
        own = attended[index * chunks : (index + 1) * chunks]
        left = jnp.concatenate([piece[...] for piece in own], axis=1)
        mixed += turned(left, matrices[index][...])
    out_ref[...] = (inflow_ref[...].astype(F32) + gate_ref[...] * mixed).astype(BF16)


def output(inflow, gate, attended, matrices):
    tp, chunks = len(attended), len(attended[0])
    patch, share = inflow.shape
    inner = matrices[0].shape[1]
    arrays = [inflow, gate] + [piece for own in attended for piece in own] + matrices
    return pl.pallas_call(
        functools.partial(output_kernel, tp, chunks),
        grid=(1,),
        in_specs=[pl.BlockSpec(array.shape, lambda i: (0, 0)) for array in arrays],
        out_specs=pl.BlockSpec(inflow.shape, lambda i: (0, 0)),
        out_shape=jax.ShapeDtypeStruct(inflow.shape, BF16),
        compiler_params=params(20),
        cost_estimate=cost(2 * patch * share * inner * tp, 2 * inner * tp * (share + patch)),
        name="output",
    )(*arrays)


def after(block, earlier):
    return lax.optimization_barrier((block, earlier))[0]


def swapped(block, axis, distance):
    return lax.ppermute(block, axis, [(i, i ^ distance) for i in range(lax.axis_size(axis))])


def handed_on(block):
    sections = lax.axis_size("section")
    return lax.ppermute(block, "section", [(i, (i + 1) % sections) for i in range(sections)])


def relayed(pieces):
    moved = lax.all_to_all(pieces, "section", split_axis=0, concat_axis=0, tiled=True)
    return moved.reshape(-1, moved.shape[2])


def place_kernel(count, slots_ref, *rest):
    pieces, (out_ref, sems) = rest[:count], rest[count:]
    copies = [
        pltpu.make_async_copy(piece, out_ref.at[slots_ref[index]], sems.at[index])
        for index, piece in enumerate(pieces)
    ]
    for copy in copies:
        copy.start()
    for copy in copies:
        copy.wait()


def placed(pieces, slots):
    return pl.pallas_call(
        functools.partial(place_kernel, len(pieces)),
        in_specs=[SCALAR] + [ANYWHERE] * len(pieces),
        out_specs=ANYWHERE,
        out_shape=jax.ShapeDtypeStruct((len(pieces),) + pieces[0].shape, BF16),
        scratch_shapes=[pltpu.SemaphoreType.DMA((len(pieces),))],
        compiler_params=params(4),
        cost_estimate=cost(0, 4 * len(pieces) * pieces[0].size),
        name="placed",
    )(slots, *[in_hbm(piece) for piece in pieces])


def local(block_weights, modulation, inflow, stale_cache, patch_index, assignment):
    sections, tp = lax.axis_size("section"), lax.axis_size("tp")
    here, rank = lax.axis_index("section"), lax.axis_index("tp")
    blocks, depth, kinds, inner = block_weights.shape
    lanes = inner // HD
    share = inflow.shape[2]

    section_ids = jnp.arange(sections, dtype=jnp.int32)
    sources = here ^ section_ids

    def block_of(section):
        return jnp.sum((assignment[None] == section[:, None]) * section_ids[None], axis=1)

    rows = block_weights.reshape(blocks, depth, kinds, lanes, HD)
    rows = rows.transpose(0, 1, 3, 2, 4).reshape(blocks, depth * lanes * kinds, HD)
    tokens = lax.all_gather(inflow[0], "tp", axis=1, tiled=True)
    normed = norm(tokens, modulation[0])
    gate = handed_on(modulation[0, 2])

    out_plan = [[(3, head) for head in range(lanes)]]
    before = block_of((section_ids + sections - 1) % sections)
    (to_out,) = split_blocks(rows, before, section_ids, out_plan, lanes)
    half = max(1, lanes // 2)
    groups = [(head,) for head in range(half, lanes)] + [tuple(range(half))]
    plan = [[(kind, head) for head in group for kind in range(3)] for group in groups]
    alone = len(groups) == 3
    order = after(block_of(sources), to_out)
    split = split_blocks(rows, order, sources, plan, lanes, alone)

    pieces = list(split[len(groups) - 1 :]) if alone else []
    chain = []
    for distance in sorted(range(1, len(pieces)), key=lambda d: (d == 1, d % 2, d)):
        piece = pieces[distance]
        if len(chain) >= 3:
            piece = after(piece, chain[-3])
        chain.append(swapped(piece, "section", distance))
        pieces[distance] = chain[-1]

    to_out = relayed(to_out)
    matrices = []
    for distance in range(tp):
        held = lax.dynamic_slice_in_dim(to_out, (rank ^ distance) * share, share, 0)
        matrices.append(swapped(held, "tp", distance) if distance else held)

    attended = [[] for _ in range(tp)]

    def share_out(group, matrix, ready, *earlier):
        own = attend(waiting(normed, *ready), matrix, patch_index, stale_cache[0], group)
        moved = waiting(handed_on(own), *earlier)
        parts = [swapped(moved, "tp", distance) if distance else moved for distance in range(tp)]
        for kept, part in zip(attended, parts):
            kept.append(part)
        return parts

    def waiting(block, *earlier):
        return functools.reduce(after, earlier, block)

    if alone:
        matrix = relayed(waiting(split[0], tokens, gate, *chain))
        last = relayed(waiting(split[1], *matrices[1:3]))
        placed_rows = placed(pieces, sources)
        parts = share_out(groups[2], placed_rows.reshape(-1, placed_rows.shape[2]), ())
        parts = share_out(groups[0], matrix, (*matrices[3:], *parts))
        parts = share_out(groups[1], last, (), *parts)
    else:
        for group, own in zip(groups, split):
            parts = share_out(group, relayed(own), ())
    carried = handed_on(after(inflow[0], parts[0]))
    gate = lax.dynamic_slice_in_dim(gate, rank * share, share, 0)[None]
    return output(carried, gate, attended, matrices)[None]


def solution(mesh):
    spread = (
        P(None, "section", None, "tp"),
        P("section", None, None),
        P("section", None, "tp"),
        P("section", None, None, "tp"),
        P("section"),
        P(),
    )
    return jax.shard_map(
        local, mesh=mesh, in_specs=spread, out_specs=P("section", None, "tp"), check_vma=False
    )
```

```python
import functools

import jax
import jax.numpy as jnp
import numpy as np
from jax import lax
from jax.experimental import pallas as pl
from jax.experimental.pallas import tpu as pltpu
from jax.sharding import PartitionSpec as P

HD = 128
F32 = jnp.float32
BF16 = jnp.bfloat16
WHOLE = pl.BlockSpec(memory_space=pltpu.VMEM)
ANYWHERE = pl.BlockSpec(memory_space=pl.ANY)
SCALAR = pl.BlockSpec(memory_space=pltpu.SMEM)


def params(mebibytes):
    return pltpu.CompilerParams(vmem_limit_bytes=mebibytes * 1024 * 1024)


def in_hbm(array):
    return pltpu.with_memory_space_constraint(array, pltpu.HBM)


def cost(flops, size, exps=0):
    return pl.CostEstimate(flops=flops, bytes_accessed=size, transcendentals=exps)


def turned(left, right):
    return lax.dot_general(left, right, (((1,), (1,)), ((), ())), preferred_element_type=F32)


def pick_matrix(kinds, lanes, depth_step):
    period = 4 * lanes
    shape = (len(kinds) * lanes * depth_step, period * depth_step)
    row = lax.broadcasted_iota(jnp.int32, shape, 0)
    column = lax.broadcasted_iota(jnp.int32, shape, 1)
    source = row % depth_step * period + row // depth_step % lanes * 4 + kinds[0]
    source += row // (lanes * depth_step)
    return jnp.where(source == column, 1.0, 0.0).astype(BF16)


def split_kernel(lanes, plan, single, kinds, depth_step, order_ref, to_ref, rows_ref, *rest):
    outs, pick, alone = rest[: len(plan) - single], rest[-2], rest[-1]
    singles = rest[len(outs) : -2]
    depth = rows_ref.shape[1] // (4 * lanes)
    chunk = depth_step * 4 * lanes
    beside = 2 if depth % (2 * depth_step) == 0 else 1

    @pl.when(pl.program_id(0) == 0)
    def _():
        pick[...] = pick_matrix(kinds, lanes, depth_step)

    targets = [out.at[0] for out in outs] + [alone] * single
    for first in range(0, depth, beside * depth_step):
        begin = first * 4 * lanes
        chunks = [
            rows_ref[0, begin + i * chunk : begin + (i + 1) * chunk, :] for i in range(beside)
        ]
        sorted_rows = jnp.dot(
            pick[...], jnp.concatenate(chunks, axis=1), preferred_element_type=F32
        ).astype(BF16)
        for i in range(beside):
            to = slice(first + i * depth_step, first + (i + 1) * depth_step)
            for out, columns in zip(targets, plan):
                for column, (kind, lane) in enumerate(columns):
                    at = (kinds.index(kind) * lanes + lane) * depth_step
                    out[to, column * HD : (column + 1) * HD] = sorted_rows[
                        at : at + depth_step, i * HD : (i + 1) * HD
                    ]

    def keep(own):
        own[...] = alone[...]

    for block, own in enumerate(singles):
        pl.when(pl.program_id(0) == block)(functools.partial(keep, own))


def split_blocks(rows, order, to, plan, lanes, single=False):
    depth = rows.shape[1] // (4 * lanes)
    depth_step = max(n for n in (16, 32, 64) if depth % n == 0 and n * 4 * lanes <= 256)
    kinds = sorted({kind for columns in plan for kind, _ in columns})
    blocks = order.shape[0]
    shapes = [(blocks, depth, len(columns) * HD) for columns in plan]
    out_specs = [
        pl.BlockSpec((1,) + shape[1:], lambda i, order, to: (to[i], 0, 0)) for shape in shapes
    ]
    if single:
        alone = shapes.pop()[1:]
        shapes += [alone] * blocks
        out_specs[-1:] = [pl.BlockSpec(alone, lambda i, order, to: (0, 0))] * blocks
    return pl.pallas_call(
        functools.partial(split_kernel, lanes, plan, single, kinds, depth_step),
        grid_spec=pltpu.PrefetchScalarGridSpec(
            num_scalar_prefetch=2,
            grid=(blocks,),
            in_specs=[pl.BlockSpec((1,) + rows.shape[1:], lambda i, order, to: (order[i], 0, 0))],
            out_specs=out_specs,
            scratch_shapes=[
                pltpu.VMEM((len(kinds) * lanes * depth_step, depth_step * 4 * lanes), BF16),
                pltpu.VMEM((depth, len(plan[-1]) * HD), BF16),
            ],
        ),
        out_shape=[jax.ShapeDtypeStruct(shape, BF16) for shape in shapes],
        compiler_params=params(32),
        cost_estimate=cost(0, 3 * blocks * rows.shape[1] * HD),
        name="split_blocks",
    )(order, to, in_hbm(rows))


def norm_kernel(tokens_ref, modulation_ref, out_ref):
    tokens = tokens_ref[...].astype(F32)
    center = jnp.mean(tokens, axis=1, keepdims=True)
    tokens = tokens - center
    spread = jnp.mean(tokens * tokens, axis=1, keepdims=True)
    normed = tokens * lax.rsqrt(spread + 1e-06)
    out_ref[...] = (normed * (1.0 + modulation_ref[0:1]) + modulation_ref[1:2]).astype(BF16)


def norm(tokens, modulation):
    patch, width = tokens.shape
    rows = 128
    return pl.pallas_call(
        norm_kernel,
        grid=(patch // rows,),
        in_specs=[
            pl.BlockSpec((rows, width), lambda i: (i, 0)),
            pl.BlockSpec((3, width), lambda i: (0, 0)),
        ],
        out_specs=pl.BlockSpec((rows, width), lambda i: (i, 0)),
        out_shape=jax.ShapeDtypeStruct((patch, width), BF16),
        compiler_params=params(14),
        cost_estimate=cost(10 * patch * width, 4 * patch * width),
        name="norm",
    )(in_hbm(tokens), modulation)


def attend_kernel(where_ref, normed_ref, matrix_ref, stale_ref, out_ref, own):
    patch = normed_ref.shape[0]
    parts = stale_ref.shape[1] // patch
    own[...] = jnp.dot(normed_ref[...], matrix_ref[...], preferred_element_type=F32).astype(BF16)
    starts = [
        pl.multiple_of(lax.rem(where_ref[0] + 1 + part, parts) * patch, patch)
        for part in range(parts - 1)
    ]
    scale = F32(np.log2(np.e) / np.sqrt(HD))
    keys = [stale_ref[0, pl.ds(start, patch), :] for start in starts] + [own[:, HD : 2 * HD]]
    values = [stale_ref[1, pl.ds(start, patch), :] for start in starts] + [own[:, 2 * HD :]]
    scores = [turned(own[:, :HD], key) for key in keys]
    top = jnp.max(functools.reduce(jnp.maximum, scores), axis=1, keepdims=True)
    total, summed = 0.0, 0.0
    for score, value in zip(scores, values):
        expo = jnp.exp2((score - top) * scale)
        total += expo
        summed += jnp.dot(expo.astype(BF16), value, preferred_element_type=F32)
    out_ref[...] = (summed / jnp.sum(total, axis=1, keepdims=True)).astype(BF16)


def attend(normed, matrix, where, stale, group):
    patch, width = normed.shape
    heads, keys = len(group), stale.shape[1]
    first = group[0]
    return pl.pallas_call(
        attend_kernel,
        grid_spec=pltpu.PrefetchScalarGridSpec(
            num_scalar_prefetch=1,
            grid=(heads,),
            in_specs=[
                pl.BlockSpec((patch, width), lambda h, where: (0, 0)),
                pl.BlockSpec((width, 3 * HD), lambda h, where: (0, h)),
                pl.BlockSpec((2, keys, HD), lambda h, where: (0, 0, first + h)),
            ],
            out_specs=pl.BlockSpec((patch, HD), lambda h, where: (0, h)),
            scratch_shapes=[pltpu.VMEM((patch, 3 * HD), BF16)],
        ),
        out_shape=jax.ShapeDtypeStruct((patch, heads * HD), BF16),
        compiler_params=params(32),
        cost_estimate=cost(
            2 * patch * heads * HD * (3 * width + 2 * keys), 2 * heads * HD * (3 * width + 2 * keys),
            patch * heads * keys,
        ),
        name="attend",
    )(where, normed, matrix, stale)


def output_kernel(tp, chunks, inflow_ref, gate_ref, *rest):
    attended, matrices, out_ref = rest[: tp * chunks], rest[tp * chunks : -1], rest[-1]
    mixed = 0.0
    for index in range(tp):
        own = attended[index * chunks : (index + 1) * chunks]
        left = jnp.concatenate([piece[...] for piece in own], axis=1)
        mixed += turned(left, matrices[index][...])
    out_ref[...] = (inflow_ref[...].astype(F32) + gate_ref[...] * mixed).astype(BF16)


def output(inflow, gate, attended, matrices):
    tp, chunks = len(attended), len(attended[0])
    patch, share = inflow.shape
    inner = matrices[0].shape[1]
    arrays = [inflow, gate] + [piece for own in attended for piece in own] + matrices
    return pl.pallas_call(
        functools.partial(output_kernel, tp, chunks),
        grid=(1,),
        in_specs=[pl.BlockSpec(array.shape, lambda i: (0, 0)) for array in arrays],
        out_specs=pl.BlockSpec(inflow.shape, lambda i: (0, 0)),
        out_shape=jax.ShapeDtypeStruct(inflow.shape, BF16),
        compiler_params=params(20),
        cost_estimate=cost(2 * patch * share * inner * tp, 2 * inner * tp * (share + patch)),
        name="output",
    )(*arrays)


def after(block, earlier):
    return lax.optimization_barrier((block, earlier))[0]


def swapped(block, axis, distance):
    return lax.ppermute(block, axis, [(i, i ^ distance) for i in range(lax.axis_size(axis))])


def handed_on(block):
    sections = lax.axis_size("section")
    return lax.ppermute(block, "section", [(i, (i + 1) % sections) for i in range(sections)])


def relayed(pieces):
    moved = lax.all_to_all(pieces, "section", split_axis=0, concat_axis=0, tiled=True)
    return moved.reshape(-1, moved.shape[2])


def place_kernel(count, slots_ref, *rest):
    pieces, (out_ref, sems) = rest[:count], rest[count:]
    copies = [
        pltpu.make_async_copy(piece, out_ref.at[slots_ref[index]], sems.at[index])
        for index, piece in enumerate(pieces)
    ]
    for copy in copies:
        copy.start()
    for copy in copies:
        copy.wait()


def placed(pieces, slots):
    return pl.pallas_call(
        functools.partial(place_kernel, len(pieces)),
        in_specs=[SCALAR] + [ANYWHERE] * len(pieces),
        out_specs=ANYWHERE,
        out_shape=jax.ShapeDtypeStruct((len(pieces),) + pieces[0].shape, BF16),
        scratch_shapes=[pltpu.SemaphoreType.DMA((len(pieces),))],
        compiler_params=params(4),
        cost_estimate=cost(0, 4 * len(pieces) * pieces[0].size),
        name="placed",
    )(slots, *[in_hbm(piece) for piece in pieces])


def local(block_weights, modulation, inflow, stale_cache, patch_index, assignment):
    sections, tp = lax.axis_size("section"), lax.axis_size("tp")
    here, rank = lax.axis_index("section"), lax.axis_index("tp")
    blocks, depth, kinds, inner = block_weights.shape
    lanes = inner // HD
    share = inflow.shape[2]

    section_ids = jnp.arange(sections, dtype=jnp.int32)
    sources = here ^ section_ids

    def block_of(section):
        return jnp.sum((assignment[None] == section[:, None]) * section_ids[None], axis=1)

    rows = block_weights.reshape(blocks, depth, kinds, lanes, HD)
    rows = rows.transpose(0, 1, 3, 2, 4).reshape(blocks, depth * lanes * kinds, HD)
    tokens = lax.all_gather(inflow[0], "tp", axis=1, tiled=True)
    normed = norm(tokens, modulation[0])
    gate = handed_on(modulation[0, 2])

    out_plan = [[(3, head) for head in range(lanes)]]
    before = block_of((section_ids + sections - 1) % sections)
    (to_out,) = split_blocks(rows, before, section_ids, out_plan, lanes)
    def waiting(block, *earlier):
        return functools.reduce(after, earlier, block)

    half = max(1, lanes // 2)
    groups = [tuple(range(half))] + [(head,) for head in range(half, lanes)][::-1]
    plan = [[(kind, head) for head in group for kind in range(3)] for group in groups]
    alone = len(groups) == 3
    order = after(block_of(sources), to_out)
    split = split_blocks(rows, order, sources, plan, lanes, alone)

    to_out = relayed(to_out)
    held = [
        lax.dynamic_slice_in_dim(to_out, (rank ^ distance) * share, share, 0)
        for distance in range(tp)
    ]
    matrices = held[:1] + [swapped(held[distance], "tp", distance) for distance in range(1, tp)]

    attended = [[] for _ in range(tp)]

    def share_out(own, *earlier):
        moved = waiting(handed_on(own), *earlier)
        parts = [swapped(moved, "tp", distance) if distance else moved for distance in range(tp)]
        for kept, part in zip(attended, parts):
            kept.append(part)
        return parts

    def attended_by(index, matrix, *earlier):
        ready = waiting(normed, *earlier)
        return attend(ready, matrix, patch_index, stale_cache[0], groups[index])

    first = relayed(split[0])
    if alone:
        pieces = list(split[2:])
        chain = []
        for distance in sorted(range(1, sections), key=lambda d: (d == 1, d % 2, d)):
            earlier = [chain[-3]] if len(chain) > 2 else matrices[1:2]
            if len(chain) == 1:
                earlier.append(tokens)
            chain.append(swapped(waiting(pieces[distance], *earlier), "section", distance))
            pieces[distance] = chain[-1]
        own = attended_by(0, first, gate)
        last = relayed(waiting(split[1], own, *chain, *matrices[1:]))
        done = share_out(own)
        middle = placed(pieces, sources)
        middle = middle.reshape(-1, middle.shape[2])
        parts = share_out(attended_by(2, middle, done[0]))
        parts = share_out(attended_by(1, last, *done, parts[0]), *parts)
    else:
        for index, pieces in enumerate(split):
            moved = first if index == 0 else relayed(pieces)
            parts = share_out(attended_by(index, moved))
    carried = handed_on(after(inflow[0], parts[0]))
    gate = lax.dynamic_slice_in_dim(gate, rank * share, share, 0)[None]
    return output(carried, gate, attended, matrices)[None]


def solution(mesh):
    spread = (
        P(None, "section", None, "tp"),
        P("section", None, None),
        P("section", None, "tp"),
        P("section", None, None, "tp"),
        P("section"),
        P(),
    )
    return jax.shard_map(
        local, mesh=mesh, in_specs=spread, out_specs=P("section", None, "tp"), check_vma=False
    )
```

```python
import functools

import jax
import jax.numpy as jnp
import numpy as np
from jax import lax
from jax.experimental import pallas as pl
from jax.experimental.pallas import tpu as pltpu
from jax.sharding import PartitionSpec as P

HD = 128
F32 = jnp.float32
BF16 = jnp.bfloat16
WHOLE = pl.BlockSpec(memory_space=pltpu.VMEM)
ANYWHERE = pl.BlockSpec(memory_space=pl.ANY)
SCALAR = pl.BlockSpec(memory_space=pltpu.SMEM)


def params(mebibytes):
    return pltpu.CompilerParams(vmem_limit_bytes=mebibytes * 1024 * 1024)


def in_hbm(array):
    return pltpu.with_memory_space_constraint(array, pltpu.HBM)


def cost(flops, size, exps=0):
    return pl.CostEstimate(flops=flops, bytes_accessed=size, transcendentals=exps)


def turned(left, right):
    return lax.dot_general(left, right, (((1,), (1,)), ((), ())), preferred_element_type=F32)


def pick_matrix(kinds, lanes, depth_step):
    period = 4 * lanes
    shape = (len(kinds) * lanes * depth_step, period * depth_step)
    row = lax.broadcasted_iota(jnp.int32, shape, 0)
    column = lax.broadcasted_iota(jnp.int32, shape, 1)
    source = row % depth_step * period + row // depth_step % lanes * 4 + kinds[0]
    source += row // (lanes * depth_step)
    return jnp.where(source == column, 1.0, 0.0).astype(BF16)


def split_kernel(lanes, plan, kinds, depth_step, order_ref, rows_ref, *rest):
    outs, pick = rest[:-1], rest[-1]
    depth = rows_ref.shape[1] // (4 * lanes)
    chunk = depth_step * 4 * lanes
    beside = 2 if depth % (2 * depth_step) == 0 else 1

    @pl.when(pl.program_id(0) == 0)
    def _():
        pick[...] = pick_matrix(kinds, lanes, depth_step)

    for first in range(0, depth, beside * depth_step):
        begin = first * 4 * lanes
        chunks = [
            rows_ref[0, begin + i * chunk : begin + (i + 1) * chunk, :] for i in range(beside)
        ]
        sorted_rows = jnp.dot(
            pick[...], jnp.concatenate(chunks, axis=1), preferred_element_type=F32
        ).astype(BF16)
        for i in range(beside):
            to = slice(first + i * depth_step, first + (i + 1) * depth_step)
            for out, columns in zip(outs, plan):
                for column, (kind, lane) in enumerate(columns):
                    at = (kinds.index(kind) * lanes + lane) * depth_step
                    out[0, to, column * HD : (column + 1) * HD] = sorted_rows[
                        at : at + depth_step, i * HD : (i + 1) * HD
                    ]


def split_blocks(rows, order, plan, lanes):
    depth = rows.shape[1] // (4 * lanes)
    depth_step = max(n for n in (16, 32, 64) if depth % n == 0 and n * 4 * lanes <= 256)
    kinds = sorted({kind for columns in plan for kind, _ in columns})
    blocks = order.shape[0]
    shapes = [(blocks, depth, len(columns) * HD) for columns in plan]
    return pl.pallas_call(
        functools.partial(split_kernel, lanes, plan, kinds, depth_step),
        grid_spec=pltpu.PrefetchScalarGridSpec(
            num_scalar_prefetch=1,
            grid=(blocks,),
            in_specs=[pl.BlockSpec((1,) + rows.shape[1:], lambda i, order: (order[i], 0, 0))],
            out_specs=[pl.BlockSpec((1,) + shape[1:], lambda i, order: (i, 0, 0)) for shape in shapes],
            scratch_shapes=[
                pltpu.VMEM((len(kinds) * lanes * depth_step, depth_step * 4 * lanes), BF16)
            ],
        ),
        out_shape=[jax.ShapeDtypeStruct(shape, BF16) for shape in shapes],
        compiler_params=params(16),
        cost_estimate=cost(0, 3 * blocks * rows.shape[1] * HD),
        name="split_blocks",
    )(order, in_hbm(rows))


def norm_kernel(tokens_ref, modulation_ref, out_ref):
    tokens = tokens_ref[...].astype(F32)
    center = jnp.mean(tokens, axis=1, keepdims=True)
    tokens = tokens - center
    spread = jnp.mean(tokens * tokens, axis=1, keepdims=True)
    normed = tokens * lax.rsqrt(spread + 1e-06)
    out_ref[...] = (normed * (1.0 + modulation_ref[0:1]) + modulation_ref[1:2]).astype(BF16)


def norm(tokens, modulation):
    patch, width = tokens.shape
    rows = 128
    return pl.pallas_call(
        norm_kernel,
        grid=(patch // rows,),
        in_specs=[
            pl.BlockSpec((rows, width), lambda i: (i, 0)),
            pl.BlockSpec((3, width), lambda i: (0, 0)),
        ],
        out_specs=pl.BlockSpec((rows, width), lambda i: (i, 0)),
        out_shape=jax.ShapeDtypeStruct((patch, width), BF16),
        compiler_params=params(14),
        cost_estimate=cost(10 * patch * width, 4 * patch * width),
        name="norm",
    )(in_hbm(tokens), modulation)


def attend_kernel(where_ref, normed_ref, matrix_ref, stale_ref, out_ref, own):
    patch = normed_ref.shape[0]
    parts = stale_ref.shape[1] // patch
    own[...] = jnp.dot(normed_ref[...], matrix_ref[...], preferred_element_type=F32).astype(BF16)
    starts = [
        pl.multiple_of(lax.rem(where_ref[0] + 1 + part, parts) * patch, patch)
        for part in range(parts - 1)
    ]
    scale = F32(np.log2(np.e) / np.sqrt(HD))
    keys = [stale_ref[0, pl.ds(start, patch), :] for start in starts] + [own[:, HD : 2 * HD]]
    values = [stale_ref[1, pl.ds(start, patch), :] for start in starts] + [own[:, 2 * HD :]]
    scores = [turned(own[:, :HD], key) for key in keys]
    top = jnp.max(functools.reduce(jnp.maximum, scores), axis=1, keepdims=True)
    total, summed = 0.0, 0.0
    for score, value in zip(scores, values):
        expo = jnp.exp2((score - top) * scale)
        total += expo
        summed += jnp.dot(expo.astype(BF16), value, preferred_element_type=F32)
    out_ref[...] = (summed / jnp.sum(total, axis=1, keepdims=True)).astype(BF16)


def attend(normed, matrix, where, stale, group, spot):
    patch, width = normed.shape
    heads, keys = len(group), stale.shape[1]
    first = group[0]
    return pl.pallas_call(
        attend_kernel,
        grid_spec=pltpu.PrefetchScalarGridSpec(
            num_scalar_prefetch=1,
            grid=(heads,),
            in_specs=[
                pl.BlockSpec((patch, width), lambda h, where: (0, 0)),
                pl.BlockSpec((width, 3 * HD), lambda h, where: (0, spot + h)),
                pl.BlockSpec((2, keys, HD), lambda h, where: (0, 0, first + h)),
            ],
            out_specs=pl.BlockSpec((patch, HD), lambda h, where: (0, h)),
            scratch_shapes=[pltpu.VMEM((patch, 3 * HD), BF16)],
        ),
        out_shape=jax.ShapeDtypeStruct((patch, heads * HD), BF16),
        compiler_params=params(32),
        cost_estimate=cost(
            2 * patch * heads * HD * (3 * width + 2 * keys), 2 * heads * HD * (3 * width + 2 * keys),
            patch * heads * keys,
        ),
        name="attend",
    )(where, normed, matrix, stale)


def output_kernel(tp, chunks, inflow_ref, gate_ref, *rest):
    attended, matrices, out_ref = rest[: tp * chunks], rest[tp * chunks : -1], rest[-1]
    mixed = 0.0
    for index in range(tp):
        own = attended[index * chunks : (index + 1) * chunks]
        left = jnp.concatenate([piece[...] for piece in own], axis=1)
        mixed += turned(left, matrices[index][...])
    out_ref[...] = (inflow_ref[...].astype(F32) + gate_ref[...] * mixed).astype(BF16)


def output(inflow, gate, attended, matrices):
    tp, chunks = len(attended), len(attended[0])
    patch, share = inflow.shape
    inner = matrices[0].shape[1]
    arrays = [inflow, gate] + [piece for own in attended for piece in own] + matrices
    return pl.pallas_call(
        functools.partial(output_kernel, tp, chunks),
        grid=(1,),
        in_specs=[pl.BlockSpec(array.shape, lambda i: (0, 0)) for array in arrays],
        out_specs=pl.BlockSpec(inflow.shape, lambda i: (0, 0)),
        out_shape=jax.ShapeDtypeStruct(inflow.shape, BF16),
        compiler_params=params(20),
        cost_estimate=cost(2 * patch * share * inner * tp, 2 * inner * tp * (share + patch)),
        name="output",
    )(*arrays)


def after(block, earlier):
    return lax.optimization_barrier((block, earlier))[0]


def swapped(block, axis, distance):
    return lax.ppermute(block, axis, [(i, i ^ distance) for i in range(lax.axis_size(axis))])


def handed_on(block):
    sections = lax.axis_size("section")
    return lax.ppermute(block, "section", [(i, (i + 1) % sections) for i in range(sections)])


def relayed(pieces):
    moved = lax.all_to_all(pieces, "section", split_axis=0, concat_axis=0, tiled=True)
    return moved.reshape(-1, moved.shape[2])


def local(block_weights, modulation, inflow, stale_cache, patch_index, assignment):
    sections, tp = lax.axis_size("section"), lax.axis_size("tp")
    rank = lax.axis_index("tp")
    blocks, depth, kinds, inner = block_weights.shape
    lanes = inner // HD
    share = inflow.shape[2]

    section_ids = jnp.arange(sections, dtype=jnp.int32)

    def block_of(section):
        return jnp.sum((assignment[None] == section[:, None]) * section_ids[None], axis=1)

    rows = block_weights.reshape(blocks, depth, kinds, lanes, HD)
    rows = rows.transpose(0, 1, 3, 2, 4).reshape(blocks, depth * lanes * kinds, HD)
    tokens = lax.all_gather(inflow[0], "tp", axis=1, tiled=True)

    out_plan = [[(3, head) for head in range(lanes)]]
    before = block_of((section_ids + sections - 1) % sections)
    (to_out,) = split_blocks(rows, before, out_plan, lanes)
    half = max(1, lanes // 2)
    groups = [tuple(range(first, first + half)) for first in range(0, lanes, half)]
    plan = [[(kind, head) for head in group for kind in range(3)] for group in groups]
    split = split_blocks(rows, after(block_of(section_ids), to_out), plan, lanes)

    def waiting(block, *earlier):
        return functools.reduce(after, earlier, block)

    to_out = relayed(to_out)
    normed = norm(tokens, modulation[0])
    gate = handed_on(modulation[0, 2])
    matrices = []
    for distance in range(tp):
        held = lax.dynamic_slice_in_dim(to_out, (rank ^ distance) * share, share, 0)
        matrices.append(swapped(held, "tp", distance) if distance else held)
    ready = waiting(normed, gate)

    attended = [[] for _ in range(tp)]

    def share_out(matrix, heads, spot, *earlier):
        own = attend(waiting(ready, *earlier), matrix, patch_index, stale_cache[0], heads, spot)
        moved = handed_on(own)
        parts = [swapped(moved, "tp", distance) if distance else moved for distance in range(tp)]
        parts.append(own)
        for kept, part in zip(attended, parts):
            kept.append(part)
        return parts

    parts = matrices[3:]
    for index, group in enumerate(groups):
        pieces = split[index]
        if index > 0:
            pieces = waiting(pieces, normed, *matrices[1:3])
        matrix = relayed(pieces)
        if index < len(groups) - 1:
            parts = share_out(matrix, group, 0, *parts)
            continue
        for spot, head in enumerate(group):
            parts = share_out(matrix, (head,), spot, *parts)
            moved, parts = parts[0], parts[-1:]
    carried = handed_on(after(inflow[0], moved))
    gate = lax.dynamic_slice_in_dim(gate, rank * share, share, 0)[None]
    return output(carried, gate, attended, matrices)[None]


def solution(mesh):
    spread = (
        P(None, "section", None, "tp"),
        P("section", None, None),
        P("section", None, "tp"),
        P("section", None, None, "tp"),
        P("section"),
        P(),
    )
    return jax.shard_map(
        local, mesh=mesh, in_specs=spread, out_specs=P("section", None, "tp"), check_vma=False
    )
```

```python
import functools

import jax
import jax.numpy as jnp
import numpy as np
from jax import lax
from jax.experimental import pallas as pl
from jax.experimental.pallas import tpu as pltpu
from jax.sharding import PartitionSpec as P

HD = 128
F32 = jnp.float32
BF16 = jnp.bfloat16
WHOLE = pl.BlockSpec(memory_space=pltpu.VMEM)
ANYWHERE = pl.BlockSpec(memory_space=pl.ANY)
SCALAR = pl.BlockSpec(memory_space=pltpu.SMEM)


def params(mebibytes):
    return pltpu.CompilerParams(vmem_limit_bytes=mebibytes * 1024 * 1024)


def in_hbm(array):
    return pltpu.with_memory_space_constraint(array, pltpu.HBM)


def cost(flops, size, exps=0):
    return pl.CostEstimate(flops=flops, bytes_accessed=size, transcendentals=exps)


def turned(left, right):
    return lax.dot_general(left, right, (((1,), (1,)), ((), ())), preferred_element_type=F32)


def pick_matrix(kinds, lanes, depth_step):
    period = 4 * lanes
    shape = (len(kinds) * lanes * depth_step, period * depth_step)
    row = lax.broadcasted_iota(jnp.int32, shape, 0)
    column = lax.broadcasted_iota(jnp.int32, shape, 1)
    source = row % depth_step * period + row // depth_step % lanes * 4 + kinds[0]
    source += row // (lanes * depth_step)
    return jnp.where(source == column, 1.0, 0.0).astype(BF16)


def split_kernel(lanes, plan, kinds, depth_step, order_ref, rows_ref, *rest):
    outs, pick = rest[:-1], rest[-1]
    depth = rows_ref.shape[1] // (4 * lanes)
    chunk = depth_step * 4 * lanes
    beside = 2 if depth % (2 * depth_step) == 0 else 1

    @pl.when(pl.program_id(0) == 0)
    def _():
        pick[...] = pick_matrix(kinds, lanes, depth_step)

    for first in range(0, depth, beside * depth_step):
        begin = first * 4 * lanes
        chunks = [
            rows_ref[0, begin + i * chunk : begin + (i + 1) * chunk, :] for i in range(beside)
        ]
        sorted_rows = jnp.dot(
            pick[...], jnp.concatenate(chunks, axis=1), preferred_element_type=F32
        ).astype(BF16)
        for i in range(beside):
            to = slice(first + i * depth_step, first + (i + 1) * depth_step)
            for out, columns in zip(outs, plan):
                for column, (kind, lane) in enumerate(columns):
                    at = (kinds.index(kind) * lanes + lane) * depth_step
                    out[0, to, column * HD : (column + 1) * HD] = sorted_rows[
                        at : at + depth_step, i * HD : (i + 1) * HD
                    ]


def split_blocks(rows, order, plan, lanes):
    depth = rows.shape[1] // (4 * lanes)
    depth_step = max(n for n in (16, 32, 64) if depth % n == 0 and n * 4 * lanes <= 256)
    kinds = sorted({kind for columns in plan for kind, _ in columns})
    blocks = order.shape[0]
    shapes = [(blocks, depth, len(columns) * HD) for columns in plan]
    return pl.pallas_call(
        functools.partial(split_kernel, lanes, plan, kinds, depth_step),
        grid_spec=pltpu.PrefetchScalarGridSpec(
            num_scalar_prefetch=1,
            grid=(blocks,),
            in_specs=[pl.BlockSpec((1,) + rows.shape[1:], lambda i, order: (order[i], 0, 0))],
            out_specs=[pl.BlockSpec((1,) + shape[1:], lambda i, order: (i, 0, 0)) for shape in shapes],
            scratch_shapes=[
                pltpu.VMEM((len(kinds) * lanes * depth_step, depth_step * 4 * lanes), BF16)
            ],
        ),
        out_shape=[jax.ShapeDtypeStruct(shape, BF16) for shape in shapes],
        compiler_params=params(16),
        cost_estimate=cost(0, 3 * blocks * rows.shape[1] * HD),
        name="split_blocks",
    )(order, in_hbm(rows))


def norm_kernel(tokens_ref, modulation_ref, out_ref):
    tokens = tokens_ref[...].astype(F32)
    center = jnp.mean(tokens, axis=1, keepdims=True)
    tokens = tokens - center
    spread = jnp.mean(tokens * tokens, axis=1, keepdims=True)
    normed = tokens * lax.rsqrt(spread + 1e-06)
    out_ref[...] = (normed * (1.0 + modulation_ref[0:1]) + modulation_ref[1:2]).astype(BF16)


def norm(tokens, modulation):
    patch, width = tokens.shape
    rows = 128
    return pl.pallas_call(
        norm_kernel,
        grid=(patch // rows,),
        in_specs=[
            pl.BlockSpec((rows, width), lambda i: (i, 0)),
            pl.BlockSpec((3, width), lambda i: (0, 0)),
        ],
        out_specs=pl.BlockSpec((rows, width), lambda i: (i, 0)),
        out_shape=jax.ShapeDtypeStruct((patch, width), BF16),
        compiler_params=params(14),
        cost_estimate=cost(10 * patch * width, 4 * patch * width),
        name="norm",
    )(in_hbm(tokens), modulation)


def attend_kernel(where_ref, normed_ref, matrix_ref, stale_ref, out_ref, own):
    patch = normed_ref.shape[0]
    parts = stale_ref.shape[1] // patch
    own[...] = jnp.dot(normed_ref[...], matrix_ref[...], preferred_element_type=F32).astype(BF16)
    starts = [
        pl.multiple_of(lax.rem(where_ref[0] + 1 + part, parts) * patch, patch)
        for part in range(parts - 1)
    ]
    scale = F32(np.log2(np.e) / np.sqrt(HD))
    keys = [stale_ref[0, pl.ds(start, patch), :] for start in starts] + [own[:, HD : 2 * HD]]
    values = [stale_ref[1, pl.ds(start, patch), :] for start in starts] + [own[:, 2 * HD :]]
    scores = [turned(own[:, :HD], key) for key in keys]
    top = jnp.max(functools.reduce(jnp.maximum, scores), axis=1, keepdims=True)
    total, summed = 0.0, 0.0
    for score, value in zip(scores, values):
        expo = jnp.exp2((score - top) * scale)
        total += expo
        summed += jnp.dot(expo.astype(BF16), value, preferred_element_type=F32)
    out_ref[...] = (summed / jnp.sum(total, axis=1, keepdims=True)).astype(BF16)


def attend(normed, matrix, where, stale, group, spot):
    patch, width = normed.shape
    heads, keys = len(group), stale.shape[1]
    first = group[0]
    return pl.pallas_call(
        attend_kernel,
        grid_spec=pltpu.PrefetchScalarGridSpec(
            num_scalar_prefetch=1,
            grid=(heads,),
            in_specs=[
                pl.BlockSpec((patch, width), lambda h, where: (0, 0)),
                pl.BlockSpec((width, 3 * HD), lambda h, where: (0, spot + h)),
                pl.BlockSpec((2, keys, HD), lambda h, where: (0, 0, first + h)),
            ],
            out_specs=pl.BlockSpec((patch, HD), lambda h, where: (0, h)),
            scratch_shapes=[pltpu.VMEM((patch, 3 * HD), BF16)],
        ),
        out_shape=jax.ShapeDtypeStruct((patch, heads * HD), BF16),
        compiler_params=params(32),
        cost_estimate=cost(
            2 * patch * heads * HD * (3 * width + 2 * keys), 2 * heads * HD * (3 * width + 2 * keys),
            patch * heads * keys,
        ),
        name="attend",
    )(where, normed, matrix, stale)


def output_kernel(tp, chunks, inflow_ref, gate_ref, *rest):
    attended, matrices, out_ref = rest[: tp * chunks], rest[tp * chunks : -1], rest[-1]
    mixed = 0.0
    for index in range(tp):
        own = attended[index * chunks : (index + 1) * chunks]
        left = jnp.concatenate([piece[...] for piece in own], axis=1)
        mixed += turned(left, matrices[index][...])
    out_ref[...] = (inflow_ref[...].astype(F32) + gate_ref[...] * mixed).astype(BF16)


def output(inflow, gate, attended, matrices):
    tp, chunks = len(attended), len(attended[0])
    patch, share = inflow.shape
    inner = matrices[0].shape[1]
    arrays = [inflow, gate] + [piece for own in attended for piece in own] + matrices
    return pl.pallas_call(
        functools.partial(output_kernel, tp, chunks),
        grid=(1,),
        in_specs=[pl.BlockSpec(array.shape, lambda i: (0, 0)) for array in arrays],
        out_specs=pl.BlockSpec(inflow.shape, lambda i: (0, 0)),
        out_shape=jax.ShapeDtypeStruct(inflow.shape, BF16),
        compiler_params=params(20),
        cost_estimate=cost(2 * patch * share * inner * tp, 2 * inner * tp * (share + patch)),
        name="output",
    )(*arrays)


def after(block, earlier):
    return lax.optimization_barrier((block, earlier))[0]


def swapped(block, axis, distance):
    return lax.ppermute(block, axis, [(i, i ^ distance) for i in range(lax.axis_size(axis))])


def handed_on(block):
    sections = lax.axis_size("section")
    return lax.ppermute(block, "section", [(i, (i + 1) % sections) for i in range(sections)])


def relayed(pieces):
    moved = lax.all_to_all(pieces, "section", split_axis=0, concat_axis=0, tiled=True)
    return moved.reshape(-1, moved.shape[2])


def local(block_weights, modulation, inflow, stale_cache, patch_index, assignment):
    sections, tp = lax.axis_size("section"), lax.axis_size("tp")
    rank = lax.axis_index("tp")
    blocks, depth, kinds, inner = block_weights.shape
    lanes = inner // HD
    share = inflow.shape[2]

    section_ids = jnp.arange(sections, dtype=jnp.int32)

    def block_of(section):
        return jnp.sum((assignment[None] == section[:, None]) * section_ids[None], axis=1)

    rows = block_weights.reshape(blocks, depth, kinds, lanes, HD)
    rows = rows.transpose(0, 1, 3, 2, 4).reshape(blocks, depth * lanes * kinds, HD)
    tokens = lax.all_gather(inflow[0], "tp", axis=1, tiled=True)

    order = block_of(section_ids)
    (to_out,) = split_blocks(rows, order, [[(3, head) for head in range(lanes)]], lanes)
    half = max(1, lanes // 2)
    groups = [tuple(range(first, first + half)) for first in range(0, lanes, half)]
    plan = [[(kind, head) for head in group for kind in range(3)] for group in groups]
    split = split_blocks(rows, after(order, to_out), plan, lanes)

    def waiting(block, *earlier):
        return functools.reduce(after, earlier, block)

    to_out = relayed(to_out)
    normed = norm(tokens, modulation[0])
    matrices = []
    for distance in range(tp):
        held = lax.dynamic_slice_in_dim(to_out, (rank ^ distance) * share, share, 0)
        matrices.append(swapped(held, "tp", distance) if distance else held)

    attended = [[] for _ in range(tp)]

    def share_out(matrix, heads, spot, *earlier):
        own = attend(waiting(normed, *earlier), matrix, patch_index, stale_cache[0], heads, spot)
        parts = [swapped(own, "tp", distance) if distance else own for distance in range(tp)]
        for kept, part in zip(attended, parts):
            kept.append(part)
        return parts

    parts = matrices[3:]
    for index, group in enumerate(groups):
        pieces = split[index]
        if index > 0:
            pieces = waiting(pieces, normed, *matrices[1:3])
        matrix = relayed(pieces)
        if index < len(groups) - 1:
            parts = share_out(matrix, group, 0, *parts)
            continue
        for spot, head in enumerate(group):
            parts = share_out(matrix, (head,), spot, *parts)[:1]
    gate = lax.dynamic_slice_in_dim(modulation[0, 2], rank * share, share, 0)[None]
    return handed_on(output(inflow[0], gate, attended, matrices))[None]


def solution(mesh):
    spread = (
        P(None, "section", None, "tp"),
        P("section", None, None),
        P("section", None, "tp"),
        P("section", None, None, "tp"),
        P("section"),
        P(),
    )
    return jax.shard_map(
        local, mesh=mesh, in_specs=spread, out_specs=P("section", None, "tp"), check_vma=False
    )
```

```python
import functools

import jax
import jax.numpy as jnp
import numpy as np
from jax import lax
from jax.experimental import pallas as pl
from jax.experimental.pallas import tpu as pltpu
from jax.sharding import PartitionSpec as P

HD = 128
F32 = jnp.float32
BF16 = jnp.bfloat16
WHOLE = pl.BlockSpec(memory_space=pltpu.VMEM)
ANYWHERE = pl.BlockSpec(memory_space=pl.ANY)
SCALAR = pl.BlockSpec(memory_space=pltpu.SMEM)


def params(mebibytes):
    return pltpu.CompilerParams(vmem_limit_bytes=mebibytes * 1024 * 1024)


def in_hbm(array):
    return pltpu.with_memory_space_constraint(array, pltpu.HBM)


def cost(flops, size, exps=0):
    return pl.CostEstimate(flops=flops, bytes_accessed=size, transcendentals=exps)


def turned(left, right):
    return lax.dot_general(left, right, (((1,), (1,)), ((), ())), preferred_element_type=F32)


def pick_matrix(kinds, lanes, depth_step):
    period = 4 * lanes
    shape = (len(kinds) * lanes * depth_step, period * depth_step)
    row = lax.broadcasted_iota(jnp.int32, shape, 0)
    column = lax.broadcasted_iota(jnp.int32, shape, 1)
    source = row % depth_step * period + row // depth_step % lanes * 4 + kinds[0]
    source += row // (lanes * depth_step)
    return jnp.where(source == column, 1.0, 0.0).astype(BF16)


def split_kernel(lanes, plan, kinds, depth_step, order_ref, rows_ref, *rest):
    outs, pick = rest[:-1], rest[-1]
    depth = rows_ref.shape[1] // (4 * lanes)
    chunk = depth_step * 4 * lanes
    beside = 2 if depth % (2 * depth_step) == 0 else 1

    @pl.when(pl.program_id(0) == 0)
    def _():
        pick[...] = pick_matrix(kinds, lanes, depth_step)

    for first in range(0, depth, beside * depth_step):
        begin = first * 4 * lanes
        chunks = [
            rows_ref[0, begin + i * chunk : begin + (i + 1) * chunk, :] for i in range(beside)
        ]
        sorted_rows = jnp.dot(
            pick[...], jnp.concatenate(chunks, axis=1), preferred_element_type=F32
        ).astype(BF16)
        for i in range(beside):
            to = slice(first + i * depth_step, first + (i + 1) * depth_step)
            for out, columns in zip(outs, plan):
                for column, (kind, lane) in enumerate(columns):
                    at = (kinds.index(kind) * lanes + lane) * depth_step
                    out[0, to, column * HD : (column + 1) * HD] = sorted_rows[
                        at : at + depth_step, i * HD : (i + 1) * HD
                    ]


def split_blocks(rows, order, plan, lanes):
    depth = rows.shape[1] // (4 * lanes)
    depth_step = max(n for n in (16, 32, 64) if depth % n == 0 and n * 4 * lanes <= 256)
    kinds = sorted({kind for columns in plan for kind, _ in columns})
    blocks = order.shape[0]
    shapes = [(blocks, depth, len(columns) * HD) for columns in plan]
    return pl.pallas_call(
        functools.partial(split_kernel, lanes, plan, kinds, depth_step),
        grid_spec=pltpu.PrefetchScalarGridSpec(
            num_scalar_prefetch=1,
            grid=(blocks,),
            in_specs=[pl.BlockSpec((1,) + rows.shape[1:], lambda i, order: (order[i], 0, 0))],
            out_specs=[pl.BlockSpec((1,) + shape[1:], lambda i, order: (i, 0, 0)) for shape in shapes],
            scratch_shapes=[
                pltpu.VMEM((len(kinds) * lanes * depth_step, depth_step * 4 * lanes), BF16)
            ],
        ),
        out_shape=[jax.ShapeDtypeStruct(shape, BF16) for shape in shapes],
        compiler_params=params(16),
        cost_estimate=cost(0, 3 * blocks * rows.shape[1] * HD),
        name="split_blocks",
    )(order, in_hbm(rows))


def norm_kernel(tokens_ref, modulation_ref, out_ref):
    tokens = tokens_ref[...].astype(F32)
    center = jnp.mean(tokens, axis=1, keepdims=True)
    tokens = tokens - center
    spread = jnp.mean(tokens * tokens, axis=1, keepdims=True)
    normed = tokens * lax.rsqrt(spread + 1e-06)
    out_ref[...] = (normed * (1.0 + modulation_ref[0:1]) + modulation_ref[1:2]).astype(BF16)


def norm(tokens, modulation):
    patch, width = tokens.shape
    rows = 128
    return pl.pallas_call(
        norm_kernel,
        grid=(patch // rows,),
        in_specs=[
            pl.BlockSpec((rows, width), lambda i: (i, 0)),
            pl.BlockSpec((3, width), lambda i: (0, 0)),
        ],
        out_specs=pl.BlockSpec((rows, width), lambda i: (i, 0)),
        out_shape=jax.ShapeDtypeStruct((patch, width), BF16),
        compiler_params=params(14),
        cost_estimate=cost(10 * patch * width, 4 * patch * width),
        name="norm",
    )(in_hbm(tokens), modulation)


def attend_kernel(where_ref, normed_ref, matrix_ref, stale_ref, out_ref, own):
    patch = normed_ref.shape[0]
    parts = stale_ref.shape[1] // patch
    own[...] = jnp.dot(normed_ref[...], matrix_ref[...], preferred_element_type=F32).astype(BF16)
    starts = [
        pl.multiple_of(lax.rem(where_ref[0] + 1 + part, parts) * patch, patch)
        for part in range(parts - 1)
    ]
    scale = F32(np.log2(np.e) / np.sqrt(HD))
    keys = [stale_ref[0, pl.ds(start, patch), :] for start in starts] + [own[:, HD : 2 * HD]]
    values = [stale_ref[1, pl.ds(start, patch), :] for start in starts] + [own[:, 2 * HD :]]
    scores = [turned(own[:, :HD], key) for key in keys]
    top = jnp.max(functools.reduce(jnp.maximum, scores), axis=1, keepdims=True)
    total, summed = 0.0, 0.0
    for score, value in zip(scores, values):
        expo = jnp.exp2((score - top) * scale)
        total += expo
        summed += jnp.dot(expo.astype(BF16), value, preferred_element_type=F32)
    out_ref[...] = (summed / jnp.sum(total, axis=1, keepdims=True)).astype(BF16)


def attend(normed, matrix, where, stale, group, spot):
    patch, width = normed.shape
    heads, keys = len(group), stale.shape[1]
    first = group[0]
    return pl.pallas_call(
        attend_kernel,
        grid_spec=pltpu.PrefetchScalarGridSpec(
            num_scalar_prefetch=1,
            grid=(heads,),
            in_specs=[
                pl.BlockSpec((patch, width), lambda h, where: (0, 0)),
                pl.BlockSpec((width, 3 * HD), lambda h, where: (0, spot + h)),
                pl.BlockSpec((2, keys, HD), lambda h, where: (0, 0, first + h)),
            ],
            out_specs=pl.BlockSpec((patch, HD), lambda h, where: (0, h)),
            scratch_shapes=[pltpu.VMEM((patch, 3 * HD), BF16)],
        ),
        out_shape=jax.ShapeDtypeStruct((patch, heads * HD), BF16),
        compiler_params=params(32),
        cost_estimate=cost(
            2 * patch * heads * HD * (3 * width + 2 * keys), 2 * heads * HD * (3 * width + 2 * keys),
            patch * heads * keys,
        ),
        name="attend",
    )(where, normed, matrix, stale)


def output_kernel(tp, whole, rank_ref, inflow_ref, gate_ref, *rest):
    shared, rest = rest[:whole], rest[whole:]
    swaps, matrices, out_ref = rest[:tp], rest[tp:-1], rest[-1]
    mixed = 0.0
    for distance in range(tp):
        own = [every[rank_ref[0] ^ distance] for every in shared] + [swaps[distance][...]]
        mixed += turned(jnp.concatenate(own, axis=1), matrices[distance][...])
    out_ref[...] = (inflow_ref[...].astype(F32) + gate_ref[...] * mixed).astype(BF16)


def output(rank, inflow, gate, shared, swaps, matrices):
    tp = len(matrices)
    patch, share = inflow.shape
    inner = matrices[0].shape[1]
    arrays = [inflow, gate, *shared, *swaps, *matrices]
    return pl.pallas_call(
        functools.partial(output_kernel, tp, len(shared)),
        grid_spec=pltpu.PrefetchScalarGridSpec(
            num_scalar_prefetch=1,
            grid=(1,),
            in_specs=[
                pl.BlockSpec(array.shape, lambda i, rank, zeros=(0,) * array.ndim: zeros)
                for array in arrays
            ],
            out_specs=pl.BlockSpec(inflow.shape, lambda i, rank: (0, 0)),
        ),
        out_shape=jax.ShapeDtypeStruct(inflow.shape, BF16),
        compiler_params=params(24),
        cost_estimate=cost(2 * patch * share * inner * tp, 2 * inner * tp * (share + patch)),
        name="output",
    )(rank[None], *arrays)


def after(block, earlier):
    return lax.optimization_barrier((block, earlier))[0]


def swapped(block, axis, distance):
    return lax.ppermute(block, axis, [(i, i ^ distance) for i in range(lax.axis_size(axis))])


def handed_on(block):
    sections = lax.axis_size("section")
    return lax.ppermute(block, "section", [(i, (i + 1) % sections) for i in range(sections)])


def relayed(pieces):
    moved = lax.all_to_all(pieces, "section", split_axis=0, concat_axis=0, tiled=True)
    return moved.reshape(-1, moved.shape[2])


def local(block_weights, modulation, inflow, stale_cache, patch_index, assignment):
    sections, tp = lax.axis_size("section"), lax.axis_size("tp")
    rank = lax.axis_index("tp")
    blocks, depth, kinds, inner = block_weights.shape
    lanes = inner // HD
    share = inflow.shape[2]

    section_ids = jnp.arange(sections, dtype=jnp.int32)

    def block_of(section):
        return jnp.sum((assignment[None] == section[:, None]) * section_ids[None], axis=1)

    rows = block_weights.reshape(blocks, depth, kinds, lanes, HD)
    rows = rows.transpose(0, 1, 3, 2, 4).reshape(blocks, depth * lanes * kinds, HD)
    tokens = lax.all_gather(inflow[0], "tp", axis=1, tiled=True)

    order = block_of(section_ids)
    (to_out,) = split_blocks(rows, order, [[(3, head) for head in range(lanes)]], lanes)
    groups = [tuple(range(max(1, lanes - 1)))] + [(lanes - 1,)] * (lanes > 1)
    plan = [[(kind, head) for head in group for kind in range(3)] for group in groups]
    split = split_blocks(rows, after(order, to_out), plan, lanes)

    def waiting(block, *earlier):
        return functools.reduce(after, earlier, block)

    to_out = relayed(to_out)
    normed = norm(tokens, modulation[0])
    matrices = []
    for distance in range(tp):
        held = lax.dynamic_slice_in_dim(to_out, (rank ^ distance) * share, share, 0)
        matrices.append(swapped(held, "tp", distance) if distance else held)

    def attended(matrix, head, spot, *earlier):
        ready = waiting(normed, *earlier)
        return attend(ready, matrix, patch_index, stale_cache[0], (head,), spot)

    matrix = relayed(split[0])
    shared, last = [], ()
    if len(groups) > 1:
        moved = relayed(waiting(split[1], normed, *matrices[1:]))
        for spot, head in enumerate(groups[0]):
            own = attended(matrix, head, spot, *last)
            shared.append(lax.all_gather(own, "tp"))
            last = (own,)
        matrix, last = moved, (own, shared[0])
    own = attended(matrix, lanes - 1, 0, *last)
    swaps = [swapped(own, "tp", distance) if distance else own for distance in range(tp)]
    gate = lax.dynamic_slice_in_dim(modulation[0, 2], rank * share, share, 0)[None]
    return handed_on(output(rank, inflow[0], gate, shared, swaps, matrices))[None]


def solution(mesh):
    spread = (
        P(None, "section", None, "tp"),
        P("section", None, None),
        P("section", None, "tp"),
        P("section", None, None, "tp"),
        P("section"),
        P(),
    )
    return jax.shard_map(
        local, mesh=mesh, in_specs=spread, out_specs=P("section", None, "tp"), check_vma=False
    )
```

```python
import functools

import jax
import jax.numpy as jnp
import numpy as np
from jax import lax
from jax.experimental import pallas as pl
from jax.experimental.pallas import tpu as pltpu
from jax.sharding import PartitionSpec as P

HD = 128
F32 = jnp.float32
BF16 = jnp.bfloat16
WHOLE = pl.BlockSpec(memory_space=pltpu.VMEM)
ANYWHERE = pl.BlockSpec(memory_space=pl.ANY)
SCALAR = pl.BlockSpec(memory_space=pltpu.SMEM)


def params(mebibytes):
    return pltpu.CompilerParams(vmem_limit_bytes=mebibytes * 1024 * 1024)


def in_hbm(array):
    return pltpu.with_memory_space_constraint(array, pltpu.HBM)


def cost(flops, size, exps=0):
    return pl.CostEstimate(flops=flops, bytes_accessed=size, transcendentals=exps)


def turned(left, right):
    return lax.dot_general(left, right, (((1,), (1,)), ((), ())), preferred_element_type=F32)


def pick_matrix(kinds, lanes, depth_step):
    period = 4 * lanes
    shape = (len(kinds) * lanes * depth_step, period * depth_step)
    row = lax.broadcasted_iota(jnp.int32, shape, 0)
    column = lax.broadcasted_iota(jnp.int32, shape, 1)
    source = row % depth_step * period + row // depth_step % lanes * 4 + kinds[0]
    source += row // (lanes * depth_step)
    return jnp.where(source == column, 1.0, 0.0).astype(BF16)


def split_kernel(lanes, plan, kinds, depth_step, order_ref, rows_ref, *rest):
    outs, pick = rest[:-1], rest[-1]
    depth = rows_ref.shape[1] // (4 * lanes)
    chunk = depth_step * 4 * lanes
    beside = 2 if depth % (2 * depth_step) == 0 else 1

    @pl.when(pl.program_id(0) == 0)
    def _():
        pick[...] = pick_matrix(kinds, lanes, depth_step)

    for first in range(0, depth, beside * depth_step):
        begin = first * 4 * lanes
        chunks = [
            rows_ref[0, begin + i * chunk : begin + (i + 1) * chunk, :] for i in range(beside)
        ]
        sorted_rows = jnp.dot(
            pick[...], jnp.concatenate(chunks, axis=1), preferred_element_type=F32
        ).astype(BF16)
        for i in range(beside):
            to = slice(first + i * depth_step, first + (i + 1) * depth_step)
            for out, columns in zip(outs, plan):
                for column, (kind, lane) in enumerate(columns):
                    at = (kinds.index(kind) * lanes + lane) * depth_step
                    out[0, to, column * HD : (column + 1) * HD] = sorted_rows[
                        at : at + depth_step, i * HD : (i + 1) * HD
                    ]


def split_blocks(rows, order, plan, lanes):
    depth = rows.shape[1] // (4 * lanes)
    depth_step = max(n for n in (16, 32, 64) if depth % n == 0 and n * 4 * lanes <= 256)
    kinds = sorted({kind for columns in plan for kind, _ in columns})
    blocks = order.shape[0]
    shapes = [(blocks, depth, len(columns) * HD) for columns in plan]
    return pl.pallas_call(
        functools.partial(split_kernel, lanes, plan, kinds, depth_step),
        grid_spec=pltpu.PrefetchScalarGridSpec(
            num_scalar_prefetch=1,
            grid=(blocks,),
            in_specs=[pl.BlockSpec((1,) + rows.shape[1:], lambda i, order: (order[i], 0, 0))],
            out_specs=[pl.BlockSpec((1,) + shape[1:], lambda i, order: (i, 0, 0)) for shape in shapes],
            scratch_shapes=[
                pltpu.VMEM((len(kinds) * lanes * depth_step, depth_step * 4 * lanes), BF16)
            ],
        ),
        out_shape=[jax.ShapeDtypeStruct(shape, BF16) for shape in shapes],
        compiler_params=params(16),
        cost_estimate=cost(0, 3 * blocks * rows.shape[1] * HD),
        name="split_blocks",
    )(order, in_hbm(rows))


def norm_kernel(tokens_ref, modulation_ref, out_ref):
    tokens = tokens_ref[...].astype(F32)
    center = jnp.mean(tokens, axis=1, keepdims=True)
    tokens = tokens - center
    spread = jnp.mean(tokens * tokens, axis=1, keepdims=True)
    normed = tokens * lax.rsqrt(spread + 1e-06)
    out_ref[...] = (normed * (1.0 + modulation_ref[0:1]) + modulation_ref[1:2]).astype(BF16)


def norm(tokens, modulation):
    patch, width = tokens.shape
    rows = 128
    return pl.pallas_call(
        norm_kernel,
        grid=(patch // rows,),
        in_specs=[
            pl.BlockSpec((rows, width), lambda i: (i, 0)),
            pl.BlockSpec((3, width), lambda i: (0, 0)),
        ],
        out_specs=pl.BlockSpec((rows, width), lambda i: (i, 0)),
        out_shape=jax.ShapeDtypeStruct((patch, width), BF16),
        compiler_params=params(14),
        cost_estimate=cost(10 * patch * width, 4 * patch * width),
        name="norm",
    )(in_hbm(tokens), modulation)


def attend_kernel(where_ref, normed_ref, matrix_ref, stale_ref, out_ref, own):
    patch = normed_ref.shape[0]
    parts = stale_ref.shape[1] // patch
    own[...] = jnp.dot(normed_ref[...], matrix_ref[...], preferred_element_type=F32).astype(BF16)
    starts = [
        pl.multiple_of(lax.rem(where_ref[0] + 1 + part, parts) * patch, patch)
        for part in range(parts - 1)
    ]
    scale = F32(np.log2(np.e) / np.sqrt(HD))
    keys = [stale_ref[0, pl.ds(start, patch), :] for start in starts] + [own[:, HD : 2 * HD]]
    values = [stale_ref[1, pl.ds(start, patch), :] for start in starts] + [own[:, 2 * HD :]]
    scores = [turned(own[:, :HD], key) for key in keys]
    top = jnp.max(functools.reduce(jnp.maximum, scores), axis=1, keepdims=True)
    total, summed = 0.0, 0.0
    for score, value in zip(scores, values):
        expo = jnp.exp2((score - top) * scale)
        total += expo
        summed += jnp.dot(expo.astype(BF16), value, preferred_element_type=F32)
    out_ref[...] = (summed / jnp.sum(total, axis=1, keepdims=True)).astype(BF16)


def attend(normed, matrix, where, stale, group, spot):
    patch, width = normed.shape
    heads, keys = len(group), stale.shape[1]
    first = group[0]
    return pl.pallas_call(
        attend_kernel,
        grid_spec=pltpu.PrefetchScalarGridSpec(
            num_scalar_prefetch=1,
            grid=(heads,),
            in_specs=[
                pl.BlockSpec((patch, width), lambda h, where: (0, 0)),
                pl.BlockSpec((width, 3 * HD), lambda h, where: (0, spot + h)),
                pl.BlockSpec((2, keys, HD), lambda h, where: (0, 0, first + h)),
            ],
            out_specs=pl.BlockSpec((patch, HD), lambda h, where: (0, h)),
            scratch_shapes=[pltpu.VMEM((patch, 3 * HD), BF16)],
        ),
        out_shape=jax.ShapeDtypeStruct((patch, heads * HD), BF16),
        compiler_params=params(32),
        cost_estimate=cost(
            2 * patch * heads * HD * (3 * width + 2 * keys), 2 * heads * HD * (3 * width + 2 * keys),
            patch * heads * keys,
        ),
        name="attend",
    )(where, normed, matrix, stale)


def output_kernel(tp, chunks, inflow_ref, gate_ref, *rest):
    attended, matrices, out_ref = rest[: tp * chunks], rest[tp * chunks : -1], rest[-1]
    mixed = 0.0
    for index in range(tp):
        own = attended[index * chunks : (index + 1) * chunks]
        left = jnp.concatenate([piece[...] for piece in own], axis=1)
        mixed += turned(left, matrices[index][...])
    out_ref[...] = (inflow_ref[...].astype(F32) + gate_ref[...] * mixed).astype(BF16)


def output(inflow, gate, attended, matrices):
    tp, chunks = len(attended), len(attended[0])
    patch, share = inflow.shape
    inner = matrices[0].shape[1]
    arrays = [inflow, gate] + [piece for own in attended for piece in own] + matrices
    return pl.pallas_call(
        functools.partial(output_kernel, tp, chunks),
        grid=(1,),
        in_specs=[pl.BlockSpec(array.shape, lambda i: (0, 0)) for array in arrays],
        out_specs=pl.BlockSpec(inflow.shape, lambda i: (0, 0)),
        out_shape=jax.ShapeDtypeStruct(inflow.shape, BF16),
        compiler_params=params(20),
        cost_estimate=cost(2 * patch * share * inner * tp, 2 * inner * tp * (share + patch)),
        name="output",
    )(*arrays)


def after(block, earlier):
    return lax.optimization_barrier((block, earlier))[0]


def swapped(block, axis, distance):
    return lax.ppermute(block, axis, [(i, i ^ distance) for i in range(lax.axis_size(axis))])


def handed_on(block):
    sections = lax.axis_size("section")
    return lax.ppermute(block, "section", [(i, (i + 1) % sections) for i in range(sections)])


def relayed(pieces):
    moved = lax.all_to_all(pieces, "section", split_axis=0, concat_axis=0, tiled=True)
    return moved.reshape(-1, moved.shape[2])


def local(block_weights, modulation, inflow, stale_cache, patch_index, assignment):
    sections, tp = lax.axis_size("section"), lax.axis_size("tp")
    rank = lax.axis_index("tp")
    blocks, depth, kinds, inner = block_weights.shape
    lanes = inner // HD
    share = inflow.shape[2]

    section_ids = jnp.arange(sections, dtype=jnp.int32)

    def block_of(section):
        return jnp.sum((assignment[None] == section[:, None]) * section_ids[None], axis=1)

    rows = block_weights.reshape(blocks, depth, kinds, lanes, HD)
    rows = rows.transpose(0, 1, 3, 2, 4).reshape(blocks, depth * lanes * kinds, HD)
    tokens = lax.all_gather(inflow[0], "tp", axis=1, tiled=True)

    order = block_of(section_ids)
    (to_out,) = split_blocks(rows, order, [[(3, head) for head in range(lanes)]], lanes)
    half = max(1, lanes // 2)
    groups = [tuple(range(half))] + [(head,) for head in range(half, lanes)]
    plan = [[(kind, head) for head in group for kind in range(3)] for group in groups]
    split = split_blocks(rows, after(order, to_out), plan, lanes)

    def waiting(block, *earlier):
        return functools.reduce(after, earlier, block)

    to_out = relayed(to_out)
    normed = norm(tokens, modulation[0])
    matrices = []
    for distance in range(tp):
        held = lax.dynamic_slice_in_dim(to_out, (rank ^ distance) * share, share, 0)
        matrices.append(swapped(held, "tp", distance) if distance else held)

    waits, parts = [(), (normed, *matrices[1:3]), tuple(matrices[3:])], []
    owns, final = [], len(groups) - 1
    for index, group in enumerate(groups):
        if index > 1:
            waits[index] += (owns[index - 2], moved)
        pieces = waiting(split[index], *(waits[index] if index < len(waits) else ()))
        moved = relayed(pieces)
        if index > 0:
            owns.append(attend(normed, matrix, patch_index, stale_cache[0], groups[index - 1], 0))
        matrix = moved
        if index < final:
            continue
        parts = [[swapped(own, "tp", distance) for distance in range(1, tp)] for own in owns]
        ready = waiting(normed, *[part for own in parts[:1] for part in own], *owns[1:])
        owns.append(attend(ready, matrix, patch_index, stale_cache[0], group, 0))
        parts.append([swapped(owns[-1], "tp", distance) for distance in range(1, tp)])
    attended = [owns] + [[own[distance] for own in parts] for distance in range(tp - 1)]
    gate = lax.dynamic_slice_in_dim(modulation[0, 2], rank * share, share, 0)[None]
    return handed_on(output(inflow[0], gate, attended, matrices))[None]


def solution(mesh):
    spread = (
        P(None, "section", None, "tp"),
        P("section", None, None),
        P("section", None, "tp"),
        P("section", None, None, "tp"),
        P("section"),
        P(),
    )
    return jax.shard_map(
        local, mesh=mesh, in_specs=spread, out_specs=P("section", None, "tp"), check_vma=False
    )
```

```python
import functools

import jax
import jax.numpy as jnp
import numpy as np
from jax import lax
from jax.experimental import pallas as pl
from jax.experimental.pallas import tpu as pltpu
from jax.sharding import PartitionSpec as P

HD = 128
F32 = jnp.float32
BF16 = jnp.bfloat16
WHOLE = pl.BlockSpec(memory_space=pltpu.VMEM)
ANYWHERE = pl.BlockSpec(memory_space=pl.ANY)
SCALAR = pl.BlockSpec(memory_space=pltpu.SMEM)


def params(mebibytes):
    return pltpu.CompilerParams(vmem_limit_bytes=mebibytes * 1024 * 1024)


def in_hbm(array):
    return pltpu.with_memory_space_constraint(array, pltpu.HBM)


def cost(flops, size, exps=0):
    return pl.CostEstimate(flops=flops, bytes_accessed=size, transcendentals=exps)


def turned(left, right):
    return lax.dot_general(left, right, (((1,), (1,)), ((), ())), preferred_element_type=F32)


def pick_matrix(kinds, lanes, depth_step):
    period = 4 * lanes
    shape = (len(kinds) * lanes * depth_step, period * depth_step)
    row = lax.broadcasted_iota(jnp.int32, shape, 0)
    column = lax.broadcasted_iota(jnp.int32, shape, 1)
    source = row % depth_step * period + row // depth_step % lanes * 4 + kinds[0]
    source += row // (lanes * depth_step)
    return jnp.where(source == column, 1.0, 0.0).astype(BF16)


def split_kernel(lanes, plan, kinds, depth_step, order_ref, rows_ref, *rest):
    outs, pick = rest[:-1], rest[-1]
    depth = rows_ref.shape[1] // (4 * lanes)
    chunk = depth_step * 4 * lanes
    beside = 2 if depth % (2 * depth_step) == 0 else 1

    @pl.when(pl.program_id(0) == 0)
    def _():
        pick[...] = pick_matrix(kinds, lanes, depth_step)

    for first in range(0, depth, beside * depth_step):
        begin = first * 4 * lanes
        chunks = [
            rows_ref[0, begin + i * chunk : begin + (i + 1) * chunk, :] for i in range(beside)
        ]
        sorted_rows = jnp.dot(
            pick[...], jnp.concatenate(chunks, axis=1), preferred_element_type=F32
        ).astype(BF16)
        for i in range(beside):
            to = slice(first + i * depth_step, first + (i + 1) * depth_step)
            for out, columns in zip(outs, plan):
                for column, (kind, lane) in enumerate(columns):
                    at = (kinds.index(kind) * lanes + lane) * depth_step
                    out[0, to, column * HD : (column + 1) * HD] = sorted_rows[
                        at : at + depth_step, i * HD : (i + 1) * HD
                    ]


def split_blocks(rows, order, plan, lanes):
    depth = rows.shape[1] // (4 * lanes)
    depth_step = max(n for n in (16, 32, 64) if depth % n == 0 and n * 4 * lanes <= 256)
    kinds = sorted({kind for columns in plan for kind, _ in columns})
    blocks = order.shape[0]
    shapes = [(blocks, depth, len(columns) * HD) for columns in plan]
    return pl.pallas_call(
        functools.partial(split_kernel, lanes, plan, kinds, depth_step),
        grid_spec=pltpu.PrefetchScalarGridSpec(
            num_scalar_prefetch=1,
            grid=(blocks,),
            in_specs=[pl.BlockSpec((1,) + rows.shape[1:], lambda i, order: (order[i], 0, 0))],
            out_specs=[pl.BlockSpec((1,) + shape[1:], lambda i, order: (i, 0, 0)) for shape in shapes],
            scratch_shapes=[
                pltpu.VMEM((len(kinds) * lanes * depth_step, depth_step * 4 * lanes), BF16)
            ],
        ),
        out_shape=[jax.ShapeDtypeStruct(shape, BF16) for shape in shapes],
        compiler_params=params(16),
        cost_estimate=cost(0, 3 * blocks * rows.shape[1] * HD),
        name="split_blocks",
    )(order, in_hbm(rows))


def norm_kernel(tokens_ref, modulation_ref, out_ref):
    tokens = tokens_ref[...].astype(F32)
    center = jnp.mean(tokens, axis=1, keepdims=True)
    tokens = tokens - center
    spread = jnp.mean(tokens * tokens, axis=1, keepdims=True)
    normed = tokens * lax.rsqrt(spread + 1e-06)
    out_ref[...] = (normed * (1.0 + modulation_ref[0:1]) + modulation_ref[1:2]).astype(BF16)


def norm(tokens, modulation):
    patch, width = tokens.shape
    rows = 128
    return pl.pallas_call(
        norm_kernel,
        grid=(patch // rows,),
        in_specs=[
            pl.BlockSpec((rows, width), lambda i: (i, 0)),
            pl.BlockSpec((3, width), lambda i: (0, 0)),
        ],
        out_specs=pl.BlockSpec((rows, width), lambda i: (i, 0)),
        out_shape=jax.ShapeDtypeStruct((patch, width), BF16),
        compiler_params=params(14),
        cost_estimate=cost(10 * patch * width, 4 * patch * width),
        name="norm",
    )(in_hbm(tokens), modulation)


def attend_kernel(where_ref, normed_ref, matrix_ref, stale_ref, out_ref, own):
    patch = normed_ref.shape[0]
    parts = stale_ref.shape[1] // patch
    own[...] = jnp.dot(normed_ref[...], matrix_ref[...], preferred_element_type=F32).astype(BF16)
    starts = [
        pl.multiple_of(lax.rem(where_ref[0] + 1 + part, parts) * patch, patch)
        for part in range(parts - 1)
    ]
    scale = F32(np.log2(np.e) / np.sqrt(HD))
    keys = [stale_ref[0, pl.ds(start, patch), :] for start in starts] + [own[:, HD : 2 * HD]]
    values = [stale_ref[1, pl.ds(start, patch), :] for start in starts] + [own[:, 2 * HD :]]
    scores = [turned(own[:, :HD], key) for key in keys]
    top = jnp.max(functools.reduce(jnp.maximum, scores), axis=1, keepdims=True)
    total, summed = 0.0, 0.0
    for score, value in zip(scores, values):
        expo = jnp.exp2((score - top) * scale)
        total += expo
        summed += jnp.dot(expo.astype(BF16), value, preferred_element_type=F32)
    out_ref[...] = (summed / jnp.sum(total, axis=1, keepdims=True)).astype(BF16)


def attend(normed, matrix, where, stale, group, spot):
    patch, width = normed.shape
    heads, keys = len(group), stale.shape[1]
    first = group[0]
    return pl.pallas_call(
        attend_kernel,
        grid_spec=pltpu.PrefetchScalarGridSpec(
            num_scalar_prefetch=1,
            grid=(heads,),
            in_specs=[
                pl.BlockSpec((patch, width), lambda h, where: (0, 0)),
                pl.BlockSpec((width, 3 * HD), lambda h, where: (0, spot + h)),
                pl.BlockSpec((2, keys, HD), lambda h, where: (0, 0, first + h)),
            ],
            out_specs=pl.BlockSpec((patch, HD), lambda h, where: (0, h)),
            scratch_shapes=[pltpu.VMEM((patch, 3 * HD), BF16)],
        ),
        out_shape=jax.ShapeDtypeStruct((patch, heads * HD), BF16),
        compiler_params=params(32),
        cost_estimate=cost(
            2 * patch * heads * HD * (3 * width + 2 * keys), 2 * heads * HD * (3 * width + 2 * keys),
            patch * heads * keys,
        ),
        name="attend",
    )(where, normed, matrix, in_hbm(stale))


def output_kernel(tp, chunks, inflow_ref, gate_ref, *rest):
    attended, matrices, out_ref = rest[: tp * chunks], rest[tp * chunks : -1], rest[-1]
    mixed = 0.0
    for index in range(tp):
        own = attended[index * chunks : (index + 1) * chunks]
        left = jnp.concatenate([piece[...] for piece in own], axis=1)
        mixed += turned(left, matrices[index][...])
    out_ref[...] = (inflow_ref[...].astype(F32) + gate_ref[...] * mixed).astype(BF16)


def output(inflow, gate, attended, matrices):
    tp, chunks = len(attended), len(attended[0])
    patch, share = inflow.shape
    inner = matrices[0].shape[1]
    arrays = [inflow, gate] + [piece for own in attended for piece in own] + matrices
    return pl.pallas_call(
        functools.partial(output_kernel, tp, chunks),
        grid=(1,),
        in_specs=[pl.BlockSpec(array.shape, lambda i: (0, 0)) for array in arrays],
        out_specs=pl.BlockSpec(inflow.shape, lambda i: (0, 0)),
        out_shape=jax.ShapeDtypeStruct(inflow.shape, BF16),
        compiler_params=params(20),
        cost_estimate=cost(2 * patch * share * inner * tp, 2 * inner * tp * (share + patch)),
        name="output",
    )(*arrays)


def after(block, earlier):
    return lax.optimization_barrier((block, earlier))[0]


def swapped(block, axis, distance):
    return lax.ppermute(block, axis, [(i, i ^ distance) for i in range(lax.axis_size(axis))])


def handed_on(block):
    sections = lax.axis_size("section")
    return lax.ppermute(block, "section", [(i, (i + 1) % sections) for i in range(sections)])


def relayed(pieces):
    moved = lax.all_to_all(pieces, "section", split_axis=0, concat_axis=0, tiled=True)
    return moved.reshape(-1, moved.shape[2])


def local(block_weights, modulation, inflow, stale_cache, patch_index, assignment):
    sections, tp = lax.axis_size("section"), lax.axis_size("tp")
    rank = lax.axis_index("tp")
    blocks, depth, kinds, inner = block_weights.shape
    lanes = inner // HD
    share = inflow.shape[2]

    section_ids = jnp.arange(sections, dtype=jnp.int32)

    def block_of(section):
        return jnp.sum((assignment[None] == section[:, None]) * section_ids[None], axis=1)

    rows = block_weights.reshape(blocks, depth, kinds, lanes, HD)
    rows = rows.transpose(0, 1, 3, 2, 4).reshape(blocks, depth * lanes * kinds, HD)
    tokens = lax.all_gather(inflow[0], "tp", axis=1, tiled=True)

    order = block_of(section_ids)
    (to_out,) = split_blocks(rows, order, [[(3, head) for head in range(lanes)]], lanes)
    half = max(1, lanes // 2)
    groups = [tuple(range(half))] + [(head,) for head in range(half, lanes)]
    plan = [[(kind, head) for head in group for kind in range(3)] for group in groups]
    split = split_blocks(rows, after(order, to_out), plan, lanes)

    def waiting(block, *earlier):
        return functools.reduce(after, earlier, block)

    to_out = relayed(to_out)
    normed = norm(tokens, modulation[0])
    matrices = []
    for distance in range(tp):
        held = lax.dynamic_slice_in_dim(to_out, (rank ^ distance) * share, share, 0)
        matrices.append(swapped(held, "tp", distance) if distance else held)

    waits, parts = [(), (normed, *matrices[1:3]), ()], []
    owns, final = [], len(groups) - 1
    for index, group in enumerate(groups):
        if index > 1:
            waits[index] += (owns[index - 2], moved)
        pieces = waiting(split[index], *(waits[index] if index < len(waits) else ()))
        moved = relayed(pieces)
        if index > 0:
            owns.append(attend(normed, matrix, patch_index, stale_cache[0], groups[index - 1], 0))
        matrix = moved
        if index < final:
            continue
        early = [waiting(own, *owns[1:]) for own in owns[:1]] + owns[1:]
        parts = [[swapped(own, "tp", distance) for distance in range(1, tp)] for own in early]
        first = [part for own in parts[:1] for part in own]
        ready = waiting(normed, *first[:1], *owns[1:], *matrices[3:])
        owns.append(attend(ready, matrix, patch_index, stale_cache[0], group, 0))
        ready = waiting(owns[-1], *first[1:])
        parts.append([swapped(ready, "tp", distance) for distance in range(1, tp)])
    attended = [owns] + [[own[distance] for own in parts] for distance in range(tp - 1)]
    gate = lax.dynamic_slice_in_dim(modulation[0, 2], rank * share, share, 0)[None]
    return handed_on(output(inflow[0], gate, attended, matrices))[None]


def solution(mesh):
    spread = (
        P(None, "section", None, "tp"),
        P("section", None, None),
        P("section", None, "tp"),
        P("section", None, None, "tp"),
        P("section"),
        P(),
    )
    return jax.shard_map(
        local, mesh=mesh, in_specs=spread, out_specs=P("section", None, "tp"), check_vma=False
    )
```

```python
import functools

import jax
import jax.numpy as jnp
import numpy as np
from jax import lax
from jax.experimental import pallas as pl
from jax.experimental.pallas import tpu as pltpu
from jax.sharding import PartitionSpec as P

HD = 128
F32 = jnp.float32
BF16 = jnp.bfloat16
WHOLE = pl.BlockSpec(memory_space=pltpu.VMEM)
ANYWHERE = pl.BlockSpec(memory_space=pl.ANY)
SCALAR = pl.BlockSpec(memory_space=pltpu.SMEM)


def params(mebibytes):
    return pltpu.CompilerParams(vmem_limit_bytes=mebibytes * 1024 * 1024)


def in_hbm(array):
    return pltpu.with_memory_space_constraint(array, pltpu.HBM)


def cost(flops, size, exps=0):
    return pl.CostEstimate(flops=flops, bytes_accessed=size, transcendentals=exps)


def turned(left, right):
    return lax.dot_general(left, right, (((1,), (1,)), ((), ())), preferred_element_type=F32)


def pick_matrix(kinds, lanes, depth_step):
    period = 4 * lanes
    shape = (len(kinds) * lanes * depth_step, period * depth_step)
    row = lax.broadcasted_iota(jnp.int32, shape, 0)
    column = lax.broadcasted_iota(jnp.int32, shape, 1)
    source = row % depth_step * period + row // depth_step % lanes * 4 + kinds[0]
    source += row // (lanes * depth_step)
    return jnp.where(source == column, 1.0, 0.0).astype(BF16)


def split_kernel(lanes, plan, kinds, depth_step, order_ref, rows_ref, *rest):
    outs, pick = rest[:-1], rest[-1]
    depth = rows_ref.shape[1] // (4 * lanes)
    chunk = depth_step * 4 * lanes
    beside = 2 if depth % (2 * depth_step) == 0 else 1

    @pl.when(pl.program_id(0) == 0)
    def _():
        pick[...] = pick_matrix(kinds, lanes, depth_step)

    for first in range(0, depth, beside * depth_step):
        begin = first * 4 * lanes
        chunks = [
            rows_ref[0, begin + i * chunk : begin + (i + 1) * chunk, :] for i in range(beside)
        ]
        sorted_rows = jnp.dot(
            pick[...], jnp.concatenate(chunks, axis=1), preferred_element_type=F32
        ).astype(BF16)
        for i in range(beside):
            to = slice(first + i * depth_step, first + (i + 1) * depth_step)
            for out, columns in zip(outs, plan):
                for column, (kind, lane) in enumerate(columns):
                    at = (kinds.index(kind) * lanes + lane) * depth_step
                    out[0, to, column * HD : (column + 1) * HD] = sorted_rows[
                        at : at + depth_step, i * HD : (i + 1) * HD
                    ]


def split_blocks(rows, order, plan, lanes):
    depth = rows.shape[1] // (4 * lanes)
    depth_step = max(n for n in (16, 32, 64) if depth % n == 0 and n * 4 * lanes <= 256)
    kinds = sorted({kind for columns in plan for kind, _ in columns})
    blocks = order.shape[0]
    shapes = [(blocks, depth, len(columns) * HD) for columns in plan]
    return pl.pallas_call(
        functools.partial(split_kernel, lanes, plan, kinds, depth_step),
        grid_spec=pltpu.PrefetchScalarGridSpec(
            num_scalar_prefetch=1,
            grid=(blocks,),
            in_specs=[pl.BlockSpec((1,) + rows.shape[1:], lambda i, order: (order[i], 0, 0))],
            out_specs=[pl.BlockSpec((1,) + shape[1:], lambda i, order: (i, 0, 0)) for shape in shapes],
            scratch_shapes=[
                pltpu.VMEM((len(kinds) * lanes * depth_step, depth_step * 4 * lanes), BF16)
            ],
        ),
        out_shape=[jax.ShapeDtypeStruct(shape, BF16) for shape in shapes],
        compiler_params=params(16),
        cost_estimate=cost(0, 3 * blocks * rows.shape[1] * HD),
        name="split_blocks",
    )(order, in_hbm(rows))


def norm_kernel(tokens_ref, modulation_ref, out_ref):
    tokens = tokens_ref[...].astype(F32)
    center = jnp.mean(tokens, axis=1, keepdims=True)
    tokens = tokens - center
    spread = jnp.mean(tokens * tokens, axis=1, keepdims=True)
    normed = tokens * lax.rsqrt(spread + 1e-06)
    out_ref[...] = (normed * (1.0 + modulation_ref[0:1]) + modulation_ref[1:2]).astype(BF16)


def norm(tokens, modulation):
    patch, width = tokens.shape
    rows = 128
    return pl.pallas_call(
        norm_kernel,
        grid=(patch // rows,),
        in_specs=[
            pl.BlockSpec((rows, width), lambda i: (i, 0)),
            pl.BlockSpec((3, width), lambda i: (0, 0)),
        ],
        out_specs=pl.BlockSpec((rows, width), lambda i: (i, 0)),
        out_shape=jax.ShapeDtypeStruct((patch, width), BF16),
        compiler_params=params(14),
        cost_estimate=cost(10 * patch * width, 4 * patch * width),
        name="norm",
    )(in_hbm(tokens), modulation)


def attend_kernel(where_ref, normed_ref, matrix_ref, stale_ref, out_ref, own):
    patch = normed_ref.shape[0]
    parts = stale_ref.shape[1] // patch
    own[...] = jnp.dot(normed_ref[...], matrix_ref[...], preferred_element_type=F32).astype(BF16)
    starts = [
        pl.multiple_of(lax.rem(where_ref[0] + 1 + part, parts) * patch, patch)
        for part in range(parts - 1)
    ]
    scale = F32(np.log2(np.e) / np.sqrt(HD))
    keys = [stale_ref[0, pl.ds(start, patch), :] for start in starts] + [own[:, HD : 2 * HD]]
    values = [stale_ref[1, pl.ds(start, patch), :] for start in starts] + [own[:, 2 * HD :]]
    scores = [turned(own[:, :HD], key) for key in keys]
    top = jnp.max(functools.reduce(jnp.maximum, scores), axis=1, keepdims=True)
    total, summed = 0.0, 0.0
    for score, value in zip(scores, values):
        expo = jnp.exp2((score - top) * scale)
        total += expo
        summed += jnp.dot(expo.astype(BF16), value, preferred_element_type=F32)
    out_ref[...] = (summed / jnp.sum(total, axis=1, keepdims=True)).astype(BF16)


def attend(normed, matrix, where, stale, group, spot):
    patch, width = normed.shape
    heads, keys = len(group), stale.shape[1]
    first = group[0]
    return pl.pallas_call(
        attend_kernel,
        grid_spec=pltpu.PrefetchScalarGridSpec(
            num_scalar_prefetch=1,
            grid=(heads,),
            in_specs=[
                pl.BlockSpec((patch, width), lambda h, where: (0, 0)),
                pl.BlockSpec((width, 3 * HD), lambda h, where: (0, spot + h)),
                pl.BlockSpec((2, keys, HD), lambda h, where: (0, 0, first + h)),
            ],
            out_specs=pl.BlockSpec((patch, HD), lambda h, where: (0, h)),
            scratch_shapes=[pltpu.VMEM((patch, 3 * HD), BF16)],
        ),
        out_shape=jax.ShapeDtypeStruct((patch, heads * HD), BF16),
        compiler_params=params(32),
        cost_estimate=cost(
            2 * patch * heads * HD * (3 * width + 2 * keys), 2 * heads * HD * (3 * width + 2 * keys),
            patch * heads * keys,
        ),
        name="attend",
    )(where, normed, matrix, in_hbm(stale))


def output_kernel(tp, chunks, inflow_ref, gate_ref, *rest):
    attended, matrices, out_ref = rest[: tp * chunks], rest[tp * chunks : -1], rest[-1]
    mixed = 0.0
    for index in range(tp):
        own = attended[index * chunks : (index + 1) * chunks]
        left = jnp.concatenate([piece[...] for piece in own], axis=1)
        mixed += turned(left, matrices[index][...])
    out_ref[...] = (inflow_ref[...].astype(F32) + gate_ref[...] * mixed).astype(BF16)


def output(inflow, gate, attended, matrices):
    tp, chunks = len(attended), len(attended[0])
    patch, share = inflow.shape
    inner = matrices[0].shape[1]
    arrays = [inflow, gate] + [piece for own in attended for piece in own] + matrices
    return pl.pallas_call(
        functools.partial(output_kernel, tp, chunks),
        grid=(1,),
        in_specs=[pl.BlockSpec(array.shape, lambda i: (0, 0)) for array in arrays],
        out_specs=pl.BlockSpec(inflow.shape, lambda i: (0, 0)),
        out_shape=jax.ShapeDtypeStruct(inflow.shape, BF16),
        compiler_params=params(20),
        cost_estimate=cost(2 * patch * share * inner * tp, 2 * inner * tp * (share + patch)),
        name="output",
    )(*arrays)


def after(block, earlier):
    return lax.optimization_barrier((block, earlier))[0]


def swapped(block, axis, distance):
    return lax.ppermute(block, axis, [(i, i ^ distance) for i in range(lax.axis_size(axis))])


def handed_on(block):
    sections = lax.axis_size("section")
    return lax.ppermute(block, "section", [(i, (i + 1) % sections) for i in range(sections)])


def relayed(pieces):
    moved = lax.all_to_all(pieces, "section", split_axis=0, concat_axis=0, tiled=True)
    return moved.reshape(-1, moved.shape[2])


def local(block_weights, modulation, inflow, stale_cache, patch_index, assignment):
    sections, tp = lax.axis_size("section"), lax.axis_size("tp")
    rank = lax.axis_index("tp")
    blocks, depth, kinds, inner = block_weights.shape
    lanes = inner // HD
    share = inflow.shape[2]

    section_ids = jnp.arange(sections, dtype=jnp.int32)

    def block_of(section):
        return jnp.sum((assignment[None] == section[:, None]) * section_ids[None], axis=1)

    rows = block_weights.reshape(blocks, depth, kinds, lanes, HD)
    rows = rows.transpose(0, 1, 3, 2, 4).reshape(blocks, depth * lanes * kinds, HD)
    tokens = lax.all_gather(inflow[0], "tp", axis=1, tiled=True)

    order = block_of(section_ids)
    (to_out,) = split_blocks(rows, order, [[(3, head) for head in range(lanes)]], lanes)
    half = max(1, lanes // 2)
    groups = [tuple(range(half))] + [(head,) for head in range(half, lanes)]
    plan = [[(kind, head) for head in group for kind in range(3)] for group in groups]
    split = split_blocks(rows, after(order, to_out), plan, lanes)

    def waiting(block, *earlier):
        return functools.reduce(after, earlier, block)

    to_out = relayed(to_out)
    normed = norm(tokens, modulation[0])
    matrices = []
    for distance in range(tp):
        held = lax.dynamic_slice_in_dim(to_out, (rank ^ distance) * share, share, 0)
        matrices.append(swapped(held, "tp", distance) if distance else held)

    waits, parts = [(), (normed, *matrices[1:3]), tuple(matrices[3:])], []
    owns, final = [], len(groups) - 1
    for index, group in enumerate(groups):
        if index > 1:
            waits[index] += (owns[index - 2], moved)
        pieces = waiting(split[index], *(waits[index] if index < len(waits) else ()))
        moved = relayed(pieces)
        if index > 0:
            owns.append(attend(normed, matrix, patch_index, stale_cache[0], groups[index - 1], 0))
        matrix = moved
        if index < final:
            continue
        early = [waiting(own, *owns[1:]) for own in owns[:1]] + owns[1:]
        parts = [[swapped(own, "tp", distance) for distance in range(1, tp)] for own in early]
        first = [part for own in parts[:1] for part in own]
        ready = waiting(normed, *first[:1], *owns[1:], *matrices[3:])
        owns.append(attend(ready, matrix, patch_index, stale_cache[0], group, 0))
        ready = waiting(owns[-1], *first[1:])
        parts.append([swapped(ready, "tp", distance) for distance in range(1, tp)])
    attended = [owns] + [[own[distance] for own in parts] for distance in range(tp - 1)]
    gate = lax.dynamic_slice_in_dim(modulation[0, 2], rank * share, share, 0)[None]
    return handed_on(output(inflow[0], gate, attended, matrices))[None]


def solution(mesh):
    spread = (
        P(None, "section", None, "tp"),
        P("section", None, None),
        P("section", None, "tp"),
        P("section", None, None, "tp"),
        P("section"),
        P(),
    )
    return jax.shard_map(
        local, mesh=mesh, in_specs=spread, out_specs=P("section", None, "tp"), check_vma=False
    )
```

```python
import functools

import jax
import jax.numpy as jnp
import numpy as np
from jax import lax
from jax.experimental import pallas as pl
from jax.experimental.pallas import tpu as pltpu
from jax.sharding import PartitionSpec as P

HD = 128
F32 = jnp.float32
BF16 = jnp.bfloat16
WHOLE = pl.BlockSpec(memory_space=pltpu.VMEM)
ANYWHERE = pl.BlockSpec(memory_space=pl.ANY)
SCALAR = pl.BlockSpec(memory_space=pltpu.SMEM)


def params(mebibytes):
    return pltpu.CompilerParams(vmem_limit_bytes=mebibytes * 1024 * 1024)


def in_hbm(array):
    return pltpu.with_memory_space_constraint(array, pltpu.HBM)


def cost(flops, size, exps=0):
    return pl.CostEstimate(flops=flops, bytes_accessed=size, transcendentals=exps)


def turned(left, right):
    return lax.dot_general(left, right, (((1,), (1,)), ((), ())), preferred_element_type=F32)


def pick_matrix(kinds, lanes, depth_step):
    period = 4 * lanes
    shape = (len(kinds) * lanes * depth_step, period * depth_step)
    row = lax.broadcasted_iota(jnp.int32, shape, 0)
    column = lax.broadcasted_iota(jnp.int32, shape, 1)
    source = row % depth_step * period + row // depth_step % lanes * 4 + kinds[0]
    source += row // (lanes * depth_step)
    return jnp.where(source == column, 1.0, 0.0).astype(BF16)


def split_kernel(lanes, plan, kinds, depth_step, order_ref, rows_ref, *rest):
    outs, pick = rest[:-1], rest[-1]
    depth = rows_ref.shape[1] // (4 * lanes)
    chunk = depth_step * 4 * lanes
    beside = 2 if depth % (2 * depth_step) == 0 else 1

    @pl.when(pl.program_id(0) == 0)
    def _():
        pick[...] = pick_matrix(kinds, lanes, depth_step)

    for first in range(0, depth, beside * depth_step):
        begin = first * 4 * lanes
        chunks = [
            rows_ref[0, begin + i * chunk : begin + (i + 1) * chunk, :] for i in range(beside)
        ]
        sorted_rows = jnp.dot(
            pick[...], jnp.concatenate(chunks, axis=1), preferred_element_type=F32
        ).astype(BF16)
        for i in range(beside):
            begin = first + i * depth_step
            for out, (start, stop, columns) in zip(outs, plan):
                if not start <= begin < stop:
                    continue
                to = slice(begin - start, begin - start + depth_step)
                for column, (kind, lane) in enumerate(columns):
                    at = (kinds.index(kind) * lanes + lane) * depth_step
                    out[0, to, column * HD : (column + 1) * HD] = sorted_rows[
                        at : at + depth_step, i * HD : (i + 1) * HD
                    ]


def split_blocks(rows, order, plan, lanes):
    depth = rows.shape[1] // (4 * lanes)
    depth_step = max(n for n in (16, 32, 64) if depth % n == 0 and n * 4 * lanes <= 256)
    kinds = sorted({kind for _, _, columns in plan for kind, _ in columns})
    blocks = order.shape[0]
    shapes = [(blocks, stop - start, len(columns) * HD) for start, stop, columns in plan]
    return pl.pallas_call(
        functools.partial(split_kernel, lanes, plan, kinds, depth_step),
        grid_spec=pltpu.PrefetchScalarGridSpec(
            num_scalar_prefetch=1,
            grid=(blocks,),
            in_specs=[pl.BlockSpec((1,) + rows.shape[1:], lambda i, order: (order[i], 0, 0))],
            out_specs=[pl.BlockSpec((1,) + shape[1:], lambda i, order: (i, 0, 0)) for shape in shapes],
            scratch_shapes=[
                pltpu.VMEM((len(kinds) * lanes * depth_step, depth_step * 4 * lanes), BF16)
            ],
        ),
        out_shape=[jax.ShapeDtypeStruct(shape, BF16) for shape in shapes],
        compiler_params=params(16),
        cost_estimate=cost(0, 3 * blocks * rows.shape[1] * HD),
        name="split_blocks",
    )(order, in_hbm(rows))


def norm_kernel(tokens_ref, modulation_ref, out_ref):
    tokens = tokens_ref[...].astype(F32)
    center = jnp.mean(tokens, axis=1, keepdims=True)
    tokens = tokens - center
    spread = jnp.mean(tokens * tokens, axis=1, keepdims=True)
    normed = tokens * lax.rsqrt(spread + 1e-06)
    out_ref[...] = (normed * (1.0 + modulation_ref[0:1]) + modulation_ref[1:2]).astype(BF16)


def norm(tokens, modulation):
    patch, width = tokens.shape
    rows = 128
    return pl.pallas_call(
        norm_kernel,
        grid=(patch // rows,),
        in_specs=[
            pl.BlockSpec((rows, width), lambda i: (i, 0)),
            pl.BlockSpec((3, width), lambda i: (0, 0)),
        ],
        out_specs=pl.BlockSpec((rows, width), lambda i: (i, 0)),
        out_shape=jax.ShapeDtypeStruct((patch, width), BF16),
        compiler_params=params(14),
        cost_estimate=cost(10 * patch * width, 4 * patch * width),
        name="norm",
    )(in_hbm(tokens), modulation)


def attend_kernel(where_ref, normed_ref, matrix_ref, stale_ref, out_ref, own):
    patch = normed_ref.shape[0]
    parts = stale_ref.shape[1] // patch
    own[...] = jnp.dot(normed_ref[...], matrix_ref[...], preferred_element_type=F32).astype(BF16)
    starts = [
        pl.multiple_of(lax.rem(where_ref[0] + 1 + part, parts) * patch, patch)
        for part in range(parts - 1)
    ]
    scale = F32(np.log2(np.e) / np.sqrt(HD))
    keys = [stale_ref[0, pl.ds(start, patch), :] for start in starts] + [own[:, HD : 2 * HD]]
    values = [stale_ref[1, pl.ds(start, patch), :] for start in starts] + [own[:, 2 * HD :]]
    scores = [turned(own[:, :HD], key) for key in keys]
    top = jnp.max(functools.reduce(jnp.maximum, scores), axis=1, keepdims=True)
    total, summed = 0.0, 0.0
    for score, value in zip(scores, values):
        expo = jnp.exp2((score - top) * scale)
        total += expo
        summed += jnp.dot(expo.astype(BF16), value, preferred_element_type=F32)
    out_ref[...] = (summed / jnp.sum(total, axis=1, keepdims=True)).astype(BF16)


def attend(normed, matrix, where, stale, group, spot):
    patch, width = normed.shape
    heads, keys = len(group), stale.shape[1]
    first = group[0]
    return pl.pallas_call(
        attend_kernel,
        grid_spec=pltpu.PrefetchScalarGridSpec(
            num_scalar_prefetch=1,
            grid=(heads,),
            in_specs=[
                pl.BlockSpec((patch, width), lambda h, where: (0, 0)),
                pl.BlockSpec((width, 3 * HD), lambda h, where: (0, spot + h)),
                pl.BlockSpec((2, keys, HD), lambda h, where: (0, 0, first + h)),
            ],
            out_specs=pl.BlockSpec((patch, HD), lambda h, where: (0, h)),
            scratch_shapes=[pltpu.VMEM((patch, 3 * HD), BF16)],
        ),
        out_shape=jax.ShapeDtypeStruct((patch, heads * HD), BF16),
        compiler_params=params(32),
        cost_estimate=cost(
            2 * patch * heads * HD * (3 * width + 2 * keys), 2 * heads * HD * (3 * width + 2 * keys),
            patch * heads * keys,
        ),
        name="attend",
    )(where, normed, matrix, in_hbm(stale))


def output_kernel(attended_ref, matrix_ref, out_ref):
    out_ref[...] = turned(attended_ref[...], matrix_ref[...]).astype(BF16)


def output(attended, matrix):
    patch, inner = attended.shape
    rows = matrix.shape[0]
    step = 512 if rows % 512 == 0 else rows
    return pl.pallas_call(
        output_kernel,
        grid=(rows // step,),
        in_specs=[
            pl.BlockSpec((patch, inner), lambda i: (0, 0)),
            pl.BlockSpec((step, inner), lambda i: (i, 0)),
        ],
        out_specs=pl.BlockSpec((patch, step), lambda i: (0, i)),
        out_shape=jax.ShapeDtypeStruct((patch, rows), BF16),
        compiler_params=params(24),
        cost_estimate=cost(2 * patch * rows * inner, 2 * rows * (inner + patch)),
        name="output",
    )(attended, matrix)


def after(block, earlier):
    return lax.optimization_barrier((block, earlier))[0]


def handed_on(block):
    sections = lax.axis_size("section")
    return lax.ppermute(block, "section", [(i, (i + 1) % sections) for i in range(sections)])


def relayed(pieces):
    moved = lax.all_to_all(pieces, "section", split_axis=0, concat_axis=0, tiled=True)
    return moved.reshape(-1, moved.shape[2])


def local(block_weights, modulation, inflow, stale_cache, patch_index, assignment):
    sections, tp = lax.axis_size("section"), lax.axis_size("tp")
    rank = lax.axis_index("tp")
    blocks, depth, kinds, inner = block_weights.shape
    lanes = inner // HD
    share = inflow.shape[2]

    section_ids = jnp.arange(sections, dtype=jnp.int32)

    def block_of(section):
        return jnp.sum((assignment[None] == section[:, None]) * section_ids[None], axis=1)

    rows = block_weights.reshape(blocks, depth, kinds, lanes, HD)
    rows = rows.transpose(0, 1, 3, 2, 4).reshape(blocks, depth * lanes * kinds, HD)
    tokens = lax.all_gather(inflow[0], "tp", axis=1, tiled=True)

    def waiting(block, *earlier):
        return functools.reduce(after, earlier, block)

    order = block_of(section_ids)
    every = [(kind, head) for head in range(lanes) for kind in range(3)]
    (pieces,) = split_blocks(rows, order, [(0, depth, every)], lanes)
    part = depth * 2 // 3 // 16 * 16
    out_columns = [(3, head) for head in range(lanes)]
    out_plan = [(0, part, out_columns), (part, depth, out_columns)]
    first, second = split_blocks(rows, after(order, pieces), out_plan, lanes)

    matrix = relayed(pieces)
    normed = norm(tokens, modulation[0])
    to_out = relayed(after(first, matrix))
    own = attend(normed, matrix, patch_index, stale_cache[0], tuple(range(lanes)), 0)
    rest = relayed(waiting(second, to_out, own))

    per = sections // tp
    gate = lax.dynamic_slice_in_dim(modulation[0, 2], rank * share, share, 0)

    def result(matrix, start, stop):
        columns = [slice(r * depth + start, r * depth + stop) for r in range(per)]
        mixed = lax.psum_scatter(output(own, matrix), "tp", scatter_dimension=1, tiled=True)
        patch = jnp.concatenate([inflow[0][:, cols] for cols in columns], axis=1)
        gates = jnp.concatenate([gate[cols] for cols in columns])
        made = handed_on((patch.astype(F32) + gates * mixed.astype(F32)).astype(BF16))
        return jnp.split(made, per, axis=1)

    results = zip(result(to_out, 0, part), result(rest, part, depth))
    return jnp.concatenate([piece for both in results for piece in both], axis=1)[None]


def solution(mesh):
    spread = (
        P(None, "section", None, "tp"),
        P("section", None, None),
        P("section", None, "tp"),
        P("section", None, None, "tp"),
        P("section"),
        P(),
    )
    return jax.shard_map(
        local, mesh=mesh, in_specs=spread, out_specs=P("section", None, "tp"), check_vma=False
    )
```

```python
import functools

import jax
import jax.numpy as jnp
import numpy as np
from jax import lax
from jax.experimental import pallas as pl
from jax.experimental.pallas import tpu as pltpu
from jax.sharding import PartitionSpec as P

HD = 128
F32 = jnp.float32
BF16 = jnp.bfloat16
WHOLE = pl.BlockSpec(memory_space=pltpu.VMEM)
ANYWHERE = pl.BlockSpec(memory_space=pl.ANY)
SCALAR = pl.BlockSpec(memory_space=pltpu.SMEM)


def params(mebibytes):
    return pltpu.CompilerParams(vmem_limit_bytes=mebibytes * 1024 * 1024)


def in_hbm(array):
    return pltpu.with_memory_space_constraint(array, pltpu.HBM)


def cost(flops, size, exps=0):
    return pl.CostEstimate(flops=flops, bytes_accessed=size, transcendentals=exps)


def turned(left, right):
    return lax.dot_general(left, right, (((1,), (1,)), ((), ())), preferred_element_type=F32)


def pick_matrix(kinds, lanes, depth_step):
    period = 4 * lanes
    shape = (len(kinds) * lanes * depth_step, period * depth_step)
    row = lax.broadcasted_iota(jnp.int32, shape, 0)
    column = lax.broadcasted_iota(jnp.int32, shape, 1)
    source = row % depth_step * period + row // depth_step % lanes * 4 + kinds[0]
    source += row // (lanes * depth_step)
    return jnp.where(source == column, 1.0, 0.0).astype(BF16)


def split_kernel(lanes, plan, kinds, depth_step, order_ref, rows_ref, *rest):
    outs, pick = rest[:-1], rest[-1]
    depth = rows_ref.shape[1] // (4 * lanes)
    chunk = depth_step * 4 * lanes
    beside = 2 if depth % (2 * depth_step) == 0 else 1

    @pl.when(pl.program_id(0) == 0)
    def _():
        pick[...] = pick_matrix(kinds, lanes, depth_step)

    for first in range(0, depth, beside * depth_step):
        begin = first * 4 * lanes
        chunks = [
            rows_ref[0, begin + i * chunk : begin + (i + 1) * chunk, :] for i in range(beside)
        ]
        sorted_rows = jnp.dot(
            pick[...], jnp.concatenate(chunks, axis=1), preferred_element_type=F32
        ).astype(BF16)
        for i in range(beside):
            begin = first + i * depth_step
            for out, (start, stop, columns) in zip(outs, plan):
                if not start <= begin < stop:
                    continue
                to = slice(begin - start, begin - start + depth_step)
                for column, (kind, lane) in enumerate(columns):
                    at = (kinds.index(kind) * lanes + lane) * depth_step
                    out[0, to, column * HD : (column + 1) * HD] = sorted_rows[
                        at : at + depth_step, i * HD : (i + 1) * HD
                    ]


def split_blocks(rows, order, plan, lanes):
    depth = rows.shape[1] // (4 * lanes)
    depth_step = max(n for n in (16, 32, 64) if depth % n == 0 and n * 4 * lanes <= 256)
    kinds = sorted({kind for _, _, columns in plan for kind, _ in columns})
    blocks = order.shape[0]
    shapes = [(blocks, stop - start, len(columns) * HD) for start, stop, columns in plan]
    return pl.pallas_call(
        functools.partial(split_kernel, lanes, plan, kinds, depth_step),
        grid_spec=pltpu.PrefetchScalarGridSpec(
            num_scalar_prefetch=1,
            grid=(blocks,),
            in_specs=[pl.BlockSpec((1,) + rows.shape[1:], lambda i, order: (order[i], 0, 0))],
            out_specs=[pl.BlockSpec((1,) + shape[1:], lambda i, order: (i, 0, 0)) for shape in shapes],
            scratch_shapes=[
                pltpu.VMEM((len(kinds) * lanes * depth_step, depth_step * 4 * lanes), BF16)
            ],
        ),
        out_shape=[pltpu.HBM(shape, BF16) for shape in shapes],
        compiler_params=params(16),
        cost_estimate=cost(0, 3 * blocks * rows.shape[1] * HD),
        name="split_blocks",
    )(order, in_hbm(rows))


def norm_kernel(tokens_ref, modulation_ref, out_ref):
    tokens = tokens_ref[...].astype(F32)
    center = jnp.mean(tokens, axis=1, keepdims=True)
    tokens = tokens - center
    spread = jnp.mean(tokens * tokens, axis=1, keepdims=True)
    normed = tokens * lax.rsqrt(spread + 1e-06)
    out_ref[...] = (normed * (1.0 + modulation_ref[0:1]) + modulation_ref[1:2]).astype(BF16)


def norm(tokens, modulation):
    patch, width = tokens.shape
    rows = 128
    return pl.pallas_call(
        norm_kernel,
        grid=(patch // rows,),
        in_specs=[
            pl.BlockSpec((rows, width), lambda i: (i, 0)),
            pl.BlockSpec((3, width), lambda i: (0, 0)),
        ],
        out_specs=pl.BlockSpec((rows, width), lambda i: (i, 0)),
        out_shape=jax.ShapeDtypeStruct((patch, width), BF16),
        compiler_params=params(14),
        cost_estimate=cost(10 * patch * width, 4 * patch * width),
        name="norm",
    )(in_hbm(tokens), modulation)


def attend_kernel(where_ref, normed_ref, matrix_ref, stale_ref, out_ref, own):
    patch = normed_ref.shape[0]
    parts = stale_ref.shape[1] // patch
    own[...] = jnp.dot(normed_ref[...], matrix_ref[...], preferred_element_type=F32).astype(BF16)
    starts = [
        pl.multiple_of(lax.rem(where_ref[0] + 1 + part, parts) * patch, patch)
        for part in range(parts - 1)
    ]
    scale = F32(np.log2(np.e) / np.sqrt(HD))
    keys = [stale_ref[0, pl.ds(start, patch), :] for start in starts] + [own[:, HD : 2 * HD]]
    values = [stale_ref[1, pl.ds(start, patch), :] for start in starts] + [own[:, 2 * HD :]]
    scores = [turned(own[:, :HD], key) for key in keys]
    top = jnp.max(functools.reduce(jnp.maximum, scores), axis=1, keepdims=True)
    total, summed = 0.0, 0.0
    for score, value in zip(scores, values):
        expo = jnp.exp2((score - top) * scale)
        total += expo
        summed += jnp.dot(expo.astype(BF16), value, preferred_element_type=F32)
    out_ref[...] = (summed / jnp.sum(total, axis=1, keepdims=True)).astype(BF16)


def attend(normed, matrix, where, stale, group, spot):
    patch, width = normed.shape
    heads, keys = len(group), stale.shape[1]
    first = group[0]
    return pl.pallas_call(
        attend_kernel,
        grid_spec=pltpu.PrefetchScalarGridSpec(
            num_scalar_prefetch=1,
            grid=(heads,),
            in_specs=[
                pl.BlockSpec((patch, width), lambda h, where: (0, 0)),
                pl.BlockSpec((width, 3 * HD), lambda h, where: (0, spot + h)),
                pl.BlockSpec((2, keys, HD), lambda h, where: (0, 0, first + h)),
            ],
            out_specs=pl.BlockSpec((patch, HD), lambda h, where: (0, h)),
            scratch_shapes=[pltpu.VMEM((patch, 3 * HD), BF16)],
        ),
        out_shape=jax.ShapeDtypeStruct((patch, heads * HD), BF16),
        compiler_params=params(32),
        cost_estimate=cost(
            2 * patch * heads * HD * (3 * width + 2 * keys), 2 * heads * HD * (3 * width + 2 * keys),
            patch * heads * keys,
        ),
        name="attend",
    )(where, normed, matrix, in_hbm(stale))


def output_kernel(attended_ref, matrix_ref, out_ref):
    out_ref[...] = turned(attended_ref[...], matrix_ref[...]).astype(BF16)


def output(attended, matrix):
    patch, inner = attended.shape
    rows = matrix.shape[0]
    step = 512 if rows % 512 == 0 else rows
    return pl.pallas_call(
        output_kernel,
        grid=(rows // step,),
        in_specs=[
            pl.BlockSpec((patch, inner), lambda i: (0, 0)),
            pl.BlockSpec((step, inner), lambda i: (i, 0)),
        ],
        out_specs=pl.BlockSpec((patch, step), lambda i: (0, i)),
        out_shape=jax.ShapeDtypeStruct((patch, rows), BF16),
        compiler_params=params(24),
        cost_estimate=cost(2 * patch * rows * inner, 2 * rows * (inner + patch)),
        name="output",
    )(attended, matrix)


def after(block, earlier):
    return lax.optimization_barrier((block, earlier))[0]


def handed_on(block):
    sections = lax.axis_size("section")
    return lax.ppermute(block, "section", [(i, (i + 1) % sections) for i in range(sections)])


def relayed(pieces):
    moved = lax.all_to_all(pieces, "section", split_axis=0, concat_axis=0, tiled=True)
    return moved.reshape(-1, moved.shape[2])


def local(block_weights, modulation, inflow, stale_cache, patch_index, assignment):
    sections, tp = lax.axis_size("section"), lax.axis_size("tp")
    rank = lax.axis_index("tp")
    blocks, depth, kinds, inner = block_weights.shape
    lanes = inner // HD
    share = inflow.shape[2]

    section_ids = jnp.arange(sections, dtype=jnp.int32)

    def block_of(section):
        return jnp.sum((assignment[None] == section[:, None]) * section_ids[None], axis=1)

    rows = block_weights.reshape(blocks, depth, kinds, lanes, HD)
    rows = rows.transpose(0, 1, 3, 2, 4).reshape(blocks, depth * lanes * kinds, HD)
    tokens = lax.all_gather(inflow[0], "tp", axis=1, tiled=True)

    def waiting(block, *earlier):
        return functools.reduce(after, earlier, block)

    order = block_of(section_ids)
    every = [(kind, head) for head in range(lanes) for kind in range(3)]
    (pieces,) = split_blocks(rows, order, [(0, depth, every)], lanes)
    part = depth // 3 // 16 * 16
    out_columns = [(3, head) for head in range(lanes)]
    out_plan = [(0, part, out_columns), (part, depth, out_columns)]
    first, second = split_blocks(rows, after(order, pieces), out_plan, lanes)

    matrix = relayed(pieces)
    normed = norm(tokens, modulation[0])
    to_out = relayed(waiting(first, matrix, normed))
    own = attend(normed, matrix, patch_index, stale_cache[0], tuple(range(lanes)), 0)
    rest = relayed(waiting(second, to_out, own))

    per = sections // tp
    gate = lax.dynamic_slice_in_dim(modulation[0, 2], rank * share, share, 0)

    def result(matrix, start, stop):
        columns = [slice(r * depth + start, r * depth + stop) for r in range(per)]
        mixed = lax.psum_scatter(output(own, matrix), "tp", scatter_dimension=1, tiled=True)
        patch = jnp.concatenate([inflow[0][:, cols] for cols in columns], axis=1)
        gates = jnp.concatenate([gate[cols] for cols in columns])
        made = handed_on((patch.astype(F32) + gates * mixed.astype(F32)).astype(BF16))
        return jnp.split(made, per, axis=1)

    results = zip(result(to_out, 0, part), result(rest, part, depth))
    return jnp.concatenate([piece for both in results for piece in both], axis=1)[None]


def solution(mesh):
    spread = (
        P(None, "section", None, "tp"),
        P("section", None, None),
        P("section", None, "tp"),
        P("section", None, None, "tp"),
        P("section"),
        P(),
    )
    return jax.shard_map(
        local, mesh=mesh, in_specs=spread, out_specs=P("section", None, "tp"), check_vma=False
    )
```

```python
import functools

import jax
import jax.numpy as jnp
import numpy as np
from jax import lax
from jax.experimental import pallas as pl
from jax.experimental.pallas import tpu as pltpu
from jax.sharding import PartitionSpec as P

HD = 128
F32 = jnp.float32
BF16 = jnp.bfloat16
WHOLE = pl.BlockSpec(memory_space=pltpu.VMEM)
ANYWHERE = pl.BlockSpec(memory_space=pl.ANY)
SCALAR = pl.BlockSpec(memory_space=pltpu.SMEM)


def params(mebibytes):
    return pltpu.CompilerParams(vmem_limit_bytes=mebibytes * 1024 * 1024)


def in_hbm(array):
    return pltpu.with_memory_space_constraint(array, pltpu.HBM)


def cost(flops, size, exps=0):
    return pl.CostEstimate(flops=flops, bytes_accessed=size, transcendentals=exps)


def turned(left, right):
    return lax.dot_general(left, right, (((1,), (1,)), ((), ())), preferred_element_type=F32)


def pick_matrix(kinds, lanes, depth_step):
    period = 4 * lanes
    shape = (len(kinds) * lanes * depth_step, period * depth_step)
    row = lax.broadcasted_iota(jnp.int32, shape, 0)
    column = lax.broadcasted_iota(jnp.int32, shape, 1)
    source = row % depth_step * period + row // depth_step % lanes * 4 + kinds[0]
    source += row // (lanes * depth_step)
    return jnp.where(source == column, 1.0, 0.0).astype(BF16)


def split_kernel(lanes, plan, kinds, depth_step, order_ref, rows_ref, *rest):
    outs, pick = rest[:-1], rest[-1]
    depth = rows_ref.shape[1] // (4 * lanes)
    chunk = depth_step * 4 * lanes
    beside = 2 if depth % (2 * depth_step) == 0 else 1

    @pl.when(pl.program_id(0) == 0)
    def _():
        pick[...] = pick_matrix(kinds, lanes, depth_step)

    for first in range(0, depth, beside * depth_step):
        begin = first * 4 * lanes
        chunks = [
            rows_ref[0, begin + i * chunk : begin + (i + 1) * chunk, :] for i in range(beside)
        ]
        sorted_rows = jnp.dot(
            pick[...], jnp.concatenate(chunks, axis=1), preferred_element_type=F32
        ).astype(BF16)
        for i in range(beside):
            begin = first + i * depth_step
            for out, (start, stop, columns) in zip(outs, plan):
                if not start <= begin < stop:
                    continue
                to = slice(begin - start, begin - start + depth_step)
                for column, (kind, lane) in enumerate(columns):
                    at = (kinds.index(kind) * lanes + lane) * depth_step
                    out[0, to, column * HD : (column + 1) * HD] = sorted_rows[
                        at : at + depth_step, i * HD : (i + 1) * HD
                    ]


def split_blocks(rows, order, plan, lanes):
    depth = rows.shape[1] // (4 * lanes)
    ends = [depth] + [stop for _, stop, _ in plan]
    depth_step = max(
        n for n in (16, 32, 64) if n * 4 * lanes <= 256 and all(end % n == 0 for end in ends)
    )
    kinds = sorted({kind for _, _, columns in plan for kind, _ in columns})
    blocks = order.shape[0]
    shapes = [(blocks, stop - start, len(columns) * HD) for start, stop, columns in plan]
    return pl.pallas_call(
        functools.partial(split_kernel, lanes, plan, kinds, depth_step),
        grid_spec=pltpu.PrefetchScalarGridSpec(
            num_scalar_prefetch=1,
            grid=(blocks,),
            in_specs=[pl.BlockSpec((1,) + rows.shape[1:], lambda i, order: (order[i], 0, 0))],
            out_specs=[pl.BlockSpec((1,) + shape[1:], lambda i, order: (i, 0, 0)) for shape in shapes],
            scratch_shapes=[
                pltpu.VMEM((len(kinds) * lanes * depth_step, depth_step * 4 * lanes), BF16)
            ],
        ),
        out_shape=[jax.ShapeDtypeStruct(shape, BF16) for shape in shapes],
        compiler_params=params(16),
        cost_estimate=cost(0, 3 * blocks * rows.shape[1] * HD),
        name="split_blocks",
    )(order, in_hbm(rows))


def norm_kernel(tokens_ref, modulation_ref, out_ref):
    tokens = tokens_ref[...].astype(F32)
    center = jnp.mean(tokens, axis=1, keepdims=True)
    tokens = tokens - center
    spread = jnp.mean(tokens * tokens, axis=1, keepdims=True)
    normed = tokens * lax.rsqrt(spread + 1e-06)
    out_ref[...] = (normed * (1.0 + modulation_ref[0:1]) + modulation_ref[1:2]).astype(BF16)


def norm(tokens, modulation):
    patch, width = tokens.shape
    rows = 128
    return pl.pallas_call(
        norm_kernel,
        grid=(patch // rows,),
        in_specs=[
            pl.BlockSpec((rows, width), lambda i: (i, 0)),
            pl.BlockSpec((3, width), lambda i: (0, 0)),
        ],
        out_specs=pl.BlockSpec((rows, width), lambda i: (i, 0)),
        out_shape=jax.ShapeDtypeStruct((patch, width), BF16),
        compiler_params=params(14),
        cost_estimate=cost(10 * patch * width, 4 * patch * width),
        name="norm",
    )(in_hbm(tokens), modulation)


def attend_kernel(where_ref, normed_ref, matrix_ref, stale_ref, out_ref, own):
    patch = normed_ref.shape[0]
    parts = stale_ref.shape[1] // patch
    own[...] = jnp.dot(normed_ref[...], matrix_ref[...], preferred_element_type=F32).astype(BF16)
    starts = [
        pl.multiple_of(lax.rem(where_ref[0] + 1 + part, parts) * patch, patch)
        for part in range(parts - 1)
    ]
    scale = F32(np.log2(np.e) / np.sqrt(HD))
    keys = [stale_ref[0, pl.ds(start, patch), :] for start in starts] + [own[:, HD : 2 * HD]]
    values = [stale_ref[1, pl.ds(start, patch), :] for start in starts] + [own[:, 2 * HD :]]
    scores = [turned(own[:, :HD], key) for key in keys]
    top = jnp.max(functools.reduce(jnp.maximum, scores), axis=1, keepdims=True)
    total, summed = 0.0, 0.0
    for score, value in zip(scores, values):
        expo = jnp.exp2((score - top) * scale)
        total += expo
        summed += jnp.dot(expo.astype(BF16), value, preferred_element_type=F32)
    out_ref[...] = (summed / jnp.sum(total, axis=1, keepdims=True)).astype(BF16)


def attend(normed, matrix, where, stale, group, spot):
    patch, width = normed.shape
    heads, keys = len(group), stale.shape[1]
    first = group[0]
    return pl.pallas_call(
        attend_kernel,
        grid_spec=pltpu.PrefetchScalarGridSpec(
            num_scalar_prefetch=1,
            grid=(heads,),
            in_specs=[
                pl.BlockSpec((patch, width), lambda h, where: (0, 0)),
                pl.BlockSpec((width, 3 * HD), lambda h, where: (0, spot + h)),
                pl.BlockSpec((2, keys, HD), lambda h, where: (0, 0, first + h)),
            ],
            out_specs=pl.BlockSpec((patch, HD), lambda h, where: (0, h)),
            scratch_shapes=[pltpu.VMEM((patch, 3 * HD), BF16)],
        ),
        out_shape=jax.ShapeDtypeStruct((patch, heads * HD), BF16),
        compiler_params=params(32),
        cost_estimate=cost(
            2 * patch * heads * HD * (3 * width + 2 * keys), 2 * heads * HD * (3 * width + 2 * keys),
            patch * heads * keys,
        ),
        name="attend",
    )(where, in_hbm(normed), matrix, in_hbm(stale))


def output_kernel(attended_ref, matrix_ref, out_ref):
    out_ref[...] = turned(attended_ref[...], matrix_ref[...]).astype(BF16)


def output(attended, matrix):
    patch, inner = attended.shape
    rows = matrix.shape[0]
    step = 512 if rows % 512 == 0 else rows
    return pl.pallas_call(
        output_kernel,
        grid=(rows // step,),
        in_specs=[
            pl.BlockSpec((patch, inner), lambda i: (0, 0)),
            pl.BlockSpec((step, inner), lambda i: (i, 0)),
        ],
        out_specs=pl.BlockSpec((patch, step), lambda i: (0, i)),
        out_shape=jax.ShapeDtypeStruct((patch, rows), BF16),
        compiler_params=params(24),
        cost_estimate=cost(2 * patch * rows * inner, 2 * rows * (inner + patch)),
        name="output",
    )(attended, matrix)


def after(block, earlier):
    return lax.optimization_barrier((block, earlier))[0]


def handed_on(block):
    sections = lax.axis_size("section")
    return lax.ppermute(block, "section", [(i, (i + 1) % sections) for i in range(sections)])


def relayed(pieces):
    moved = lax.all_to_all(pieces, "section", split_axis=0, concat_axis=0, tiled=True)
    return moved.reshape(-1, moved.shape[2])


def local(block_weights, modulation, inflow, stale_cache, patch_index, assignment):
    sections, tp = lax.axis_size("section"), lax.axis_size("tp")
    rank = lax.axis_index("tp")
    blocks, depth, kinds, inner = block_weights.shape
    lanes = inner // HD
    share = inflow.shape[2]

    section_ids = jnp.arange(sections, dtype=jnp.int32)

    def block_of(section):
        return jnp.sum((assignment[None] == section[:, None]) * section_ids[None], axis=1)

    rows = block_weights.reshape(blocks, depth, kinds, lanes, HD)
    rows = rows.transpose(0, 1, 3, 2, 4).reshape(blocks, depth * lanes * kinds, HD)
    tokens = lax.all_gather(inflow[0], "tp", axis=1, tiled=True)

    def waiting(block, *earlier):
        return functools.reduce(after, earlier, block)

    order = block_of(section_ids)
    every = [(kind, head) for head in range(lanes) for kind in range(3)]
    (pieces,) = split_blocks(rows, order, [(0, depth, every)], lanes)
    part = depth * 2 // 3 // 16 * 16
    out_columns = [(3, head) for head in range(lanes)]
    out_plan = [(0, part, out_columns), (part, depth, out_columns)]
    first, second = split_blocks(rows, after(order, pieces), out_plan, lanes)

    matrix = relayed(pieces)
    normed = norm(tokens, modulation[0])
    to_out = relayed(waiting(first, matrix, normed))
    own = attend(normed, matrix, patch_index, stale_cache[0], tuple(range(lanes)), 0)
    product = output(own, to_out)
    rest = relayed(waiting(second, product))

    per = sections // tp
    gate = lax.dynamic_slice_in_dim(modulation[0, 2], rank * share, share, 0)

    def result(partial, start, stop):
        columns = [slice(r * depth + start, r * depth + stop) for r in range(per)]
        mixed = lax.psum_scatter(partial, "tp", scatter_dimension=1, tiled=True)
        patch = jnp.concatenate([inflow[0][:, cols] for cols in columns], axis=1)
        gates = jnp.concatenate([gate[cols] for cols in columns])
        made = handed_on((patch.astype(F32) + gates * mixed.astype(F32)).astype(BF16))
        return jnp.split(made, per, axis=1)

    results = zip(result(product, 0, part), result(output(own, rest), part, depth))
    return jnp.concatenate([piece for both in results for piece in both], axis=1)[None]


def solution(mesh):
    spread = (
        P(None, "section", None, "tp"),
        P("section", None, None),
        P("section", None, "tp"),
        P("section", None, None, "tp"),
        P("section"),
        P(),
    )
    return jax.shard_map(
        local, mesh=mesh, in_specs=spread, out_specs=P("section", None, "tp"), check_vma=False
    )
```

```python
import functools

import jax
import jax.numpy as jnp
import numpy as np
from jax import lax
from jax.experimental import pallas as pl
from jax.experimental.pallas import tpu as pltpu
from jax.sharding import PartitionSpec as P

HD = 128
F32 = jnp.float32
BF16 = jnp.bfloat16
WHOLE = pl.BlockSpec(memory_space=pltpu.VMEM)
ANYWHERE = pl.BlockSpec(memory_space=pl.ANY)
SCALAR = pl.BlockSpec(memory_space=pltpu.SMEM)


def params(mebibytes):
    return pltpu.CompilerParams(vmem_limit_bytes=mebibytes * 1024 * 1024)


def in_hbm(array):
    return pltpu.with_memory_space_constraint(array, pltpu.HBM)


def cost(flops, size, exps=0):
    return pl.CostEstimate(flops=flops, bytes_accessed=size, transcendentals=exps)


def turned(left, right):
    return lax.dot_general(left, right, (((1,), (1,)), ((), ())), preferred_element_type=F32)


def pick_matrix(kinds, lanes, depth_step):
    period = 4 * lanes
    shape = (len(kinds) * lanes * depth_step, period * depth_step)
    row = lax.broadcasted_iota(jnp.int32, shape, 0)
    column = lax.broadcasted_iota(jnp.int32, shape, 1)
    source = row % depth_step * period + row // depth_step % lanes * 4 + kinds[0]
    source += row // (lanes * depth_step)
    return jnp.where(source == column, 1.0, 0.0).astype(BF16)


def split_kernel(lanes, plan, kinds, depth_step, order_ref, rows_ref, *rest):
    outs, pick = rest[:-1], rest[-1]
    depth = rows_ref.shape[1] // (4 * lanes)
    chunk = depth_step * 4 * lanes
    beside = 2 if depth % (2 * depth_step) == 0 else 1

    @pl.when(pl.program_id(0) == 0)
    def _():
        pick[...] = pick_matrix(kinds, lanes, depth_step)

    for first in range(0, depth, beside * depth_step):
        begin = first * 4 * lanes
        chunks = [
            rows_ref[0, begin + i * chunk : begin + (i + 1) * chunk, :] for i in range(beside)
        ]
        sorted_rows = jnp.dot(
            pick[...], jnp.concatenate(chunks, axis=1), preferred_element_type=F32
        ).astype(BF16)
        for i in range(beside):
            begin = first + i * depth_step
            for out, (start, stop, columns) in zip(outs, plan):
                if not start <= begin < stop:
                    continue
                to = slice(begin - start, begin - start + depth_step)
                for column, (kind, lane) in enumerate(columns):
                    at = (kinds.index(kind) * lanes + lane) * depth_step
                    out[0, to, column * HD : (column + 1) * HD] = sorted_rows[
                        at : at + depth_step, i * HD : (i + 1) * HD
                    ]


def split_blocks(rows, order, plan, lanes):
    depth = rows.shape[1] // (4 * lanes)
    ends = [depth] + [stop for _, stop, _ in plan]
    depth_step = max(
        n for n in (16, 32, 64) if n * 4 * lanes <= 256 and all(end % n == 0 for end in ends)
    )
    kinds = sorted({kind for _, _, columns in plan for kind, _ in columns})
    blocks = order.shape[0]
    shapes = [(blocks, stop - start, len(columns) * HD) for start, stop, columns in plan]
    return pl.pallas_call(
        functools.partial(split_kernel, lanes, plan, kinds, depth_step),
        grid_spec=pltpu.PrefetchScalarGridSpec(
            num_scalar_prefetch=1,
            grid=(blocks,),
            in_specs=[pl.BlockSpec((1,) + rows.shape[1:], lambda i, order: (order[i], 0, 0))],
            out_specs=[pl.BlockSpec((1,) + shape[1:], lambda i, order: (i, 0, 0)) for shape in shapes],
            scratch_shapes=[
                pltpu.VMEM((len(kinds) * lanes * depth_step, depth_step * 4 * lanes), BF16)
            ],
        ),
        out_shape=[jax.ShapeDtypeStruct(shape, BF16) for shape in shapes],
        compiler_params=params(16),
        cost_estimate=cost(0, 3 * blocks * rows.shape[1] * HD),
        name="split_blocks",
    )(order, in_hbm(rows))


def norm_kernel(tokens_ref, modulation_ref, out_ref):
    tokens = tokens_ref[...].astype(F32)
    center = jnp.mean(tokens, axis=1, keepdims=True)
    tokens = tokens - center
    spread = jnp.mean(tokens * tokens, axis=1, keepdims=True)
    normed = tokens * lax.rsqrt(spread + 1e-06)
    out_ref[...] = (normed * (1.0 + modulation_ref[0:1]) + modulation_ref[1:2]).astype(BF16)


def norm(tokens, modulation):
    patch, width = tokens.shape
    rows = 128
    return pl.pallas_call(
        norm_kernel,
        grid=(patch // rows,),
        in_specs=[
            pl.BlockSpec((rows, width), lambda i: (i, 0)),
            pl.BlockSpec((3, width), lambda i: (0, 0)),
        ],
        out_specs=pl.BlockSpec((rows, width), lambda i: (i, 0)),
        out_shape=jax.ShapeDtypeStruct((patch, width), BF16),
        compiler_params=params(14),
        cost_estimate=cost(10 * patch * width, 4 * patch * width),
        name="norm",
    )(in_hbm(tokens), modulation)


def attend_kernel(where_ref, normed_ref, matrix_ref, stale_ref, out_ref, own):
    patch = normed_ref.shape[0]
    parts = stale_ref.shape[1] // patch
    own[...] = jnp.dot(normed_ref[...], matrix_ref[...], preferred_element_type=F32).astype(BF16)
    starts = [
        pl.multiple_of(lax.rem(where_ref[0] + 1 + part, parts) * patch, patch)
        for part in range(parts - 1)
    ]
    scale = F32(np.log2(np.e) / np.sqrt(HD))
    keys = [stale_ref[0, pl.ds(start, patch), :] for start in starts] + [own[:, HD : 2 * HD]]
    values = [stale_ref[1, pl.ds(start, patch), :] for start in starts] + [own[:, 2 * HD :]]
    scores = [turned(own[:, :HD], key) for key in keys]
    top = jnp.max(functools.reduce(jnp.maximum, scores), axis=1, keepdims=True)
    total, summed = 0.0, 0.0
    for score, value in zip(scores, values):
        expo = jnp.exp2((score - top) * scale)
        total += expo
        summed += jnp.dot(expo.astype(BF16), value, preferred_element_type=F32)
    out_ref[...] = (summed / jnp.sum(total, axis=1, keepdims=True)).astype(BF16)


def attend(normed, matrix, where, stale, group, spot):
    patch, width = normed.shape
    heads, keys = len(group), stale.shape[1]
    first = group[0]
    return pl.pallas_call(
        attend_kernel,
        grid_spec=pltpu.PrefetchScalarGridSpec(
            num_scalar_prefetch=1,
            grid=(heads,),
            in_specs=[
                pl.BlockSpec((patch, width), lambda h, where: (0, 0)),
                pl.BlockSpec((width, 3 * HD), lambda h, where: (0, spot + h)),
                pl.BlockSpec((2, keys, HD), lambda h, where: (0, 0, first + h)),
            ],
            out_specs=pl.BlockSpec((patch, HD), lambda h, where: (0, h)),
            scratch_shapes=[pltpu.VMEM((patch, 3 * HD), BF16)],
        ),
        out_shape=jax.ShapeDtypeStruct((patch, heads * HD), BF16),
        compiler_params=params(32),
        cost_estimate=cost(
            2 * patch * heads * HD * (3 * width + 2 * keys), 2 * heads * HD * (3 * width + 2 * keys),
            patch * heads * keys,
        ),
        name="attend",
    )(where, in_hbm(normed), matrix, in_hbm(stale))


def output_kernel(attended_ref, matrix_ref, out_ref):
    out_ref[...] = turned(attended_ref[...], matrix_ref[...]).astype(BF16)


def output(attended, matrix):
    patch, inner = attended.shape
    rows = matrix.shape[0]
    step = 512 if rows % 512 == 0 else rows
    return pl.pallas_call(
        output_kernel,
        grid=(rows // step,),
        in_specs=[
            pl.BlockSpec((patch, inner), lambda i: (0, 0)),
            pl.BlockSpec((step, inner), lambda i: (i, 0)),
        ],
        out_specs=pl.BlockSpec((patch, step), lambda i: (0, i)),
        out_shape=jax.ShapeDtypeStruct((patch, rows), BF16),
        compiler_params=params(24),
        cost_estimate=cost(2 * patch * rows * inner, 2 * rows * (inner + patch)),
        name="output",
    )(attended, matrix)


def after(block, earlier):
    return lax.optimization_barrier((block, earlier))[0]


def swapped(block, axis, distance):
    return lax.ppermute(block, axis, [(i, i ^ distance) for i in range(lax.axis_size(axis))])


def handed_on(block):
    sections = lax.axis_size("section")
    return lax.ppermute(block, "section", [(i, (i + 1) % sections) for i in range(sections)])


def relayed(pieces):
    moved = lax.all_to_all(pieces, "section", split_axis=0, concat_axis=0, tiled=True)
    return moved.reshape(-1, moved.shape[2])


def local(block_weights, modulation, inflow, stale_cache, patch_index, assignment):
    sections, tp = lax.axis_size("section"), lax.axis_size("tp")
    rank = lax.axis_index("tp")
    blocks, depth, kinds, inner = block_weights.shape
    lanes = inner // HD
    share = inflow.shape[2]

    section_ids = jnp.arange(sections, dtype=jnp.int32)

    def block_of(section):
        return jnp.sum((assignment[None] == section[:, None]) * section_ids[None], axis=1)

    rows = block_weights.reshape(blocks, depth, kinds, lanes, HD)
    rows = rows.transpose(0, 1, 3, 2, 4).reshape(blocks, depth * lanes * kinds, HD)
    tokens = lax.all_gather(inflow[0], "tp", axis=1, tiled=True)

    def waiting(block, *earlier):
        return functools.reduce(after, earlier, block)

    order = block_of(section_ids)
    every = [(kind, head) for head in range(lanes) for kind in range(3)]
    (pieces,) = split_blocks(rows, order, [(0, depth, every)], lanes)
    part = depth * 2 // 3 // 16 * 16
    out_columns = [(3, head) for head in range(lanes)]
    out_plan = [(0, part, out_columns), (part, depth, out_columns)]
    first, second = split_blocks(rows, after(order, pieces), out_plan, lanes)

    matrix = relayed(pieces)
    normed = norm(tokens, modulation[0])
    to_out = relayed(waiting(first, matrix, normed))
    own = attend(normed, matrix, patch_index, stale_cache[0], tuple(range(lanes)), 0)
    product = output(own, to_out)
    rest = relayed(waiting(second, product))

    per = sections // tp
    gate = lax.dynamic_slice_in_dim(modulation[0, 2], rank * share, share, 0)

    mixed = lax.psum_scatter(product, "tp", scatter_dimension=1, tiled=True)
    product = output(own, rest)
    share = product.shape[1] // tp
    wanted = [
        lax.dynamic_slice_in_dim(product, (rank ^ distance) * share, share, 1)
        for distance in range(tp)
    ]
    wanted[1:] = [swapped(wanted[distance], "tp", distance) for distance in range(1, tp)]
    mixed = waiting(mixed, *wanted[1:])
    mixed_rest = sum(chunk.astype(F32) for chunk in wanted)

    def result(mixed, start, stop):
        columns = [slice(r * depth + start, r * depth + stop) for r in range(per)]
        patch = jnp.concatenate([inflow[0][:, cols] for cols in columns], axis=1)
        gates = jnp.concatenate([gate[cols] for cols in columns])
        made = handed_on((patch.astype(F32) + gates * mixed.astype(F32)).astype(BF16))
        return jnp.split(made, per, axis=1)

    results = zip(result(mixed, 0, part), result(mixed_rest, part, depth))
    return jnp.concatenate([piece for both in results for piece in both], axis=1)[None]


def solution(mesh):
    spread = (
        P(None, "section", None, "tp"),
        P("section", None, None),
        P("section", None, "tp"),
        P("section", None, None, "tp"),
        P("section"),
        P(),
    )
    return jax.shard_map(
        local, mesh=mesh, in_specs=spread, out_specs=P("section", None, "tp"), check_vma=False
    )
```

```python
import functools

import jax
import jax.numpy as jnp
import numpy as np
from jax import lax
from jax.experimental import pallas as pl
from jax.experimental.pallas import tpu as pltpu
from jax.sharding import PartitionSpec as P

HD = 128
F32 = jnp.float32
BF16 = jnp.bfloat16
WHOLE = pl.BlockSpec(memory_space=pltpu.VMEM)
ANYWHERE = pl.BlockSpec(memory_space=pl.ANY)
SCALAR = pl.BlockSpec(memory_space=pltpu.SMEM)


def params(mebibytes):
    return pltpu.CompilerParams(vmem_limit_bytes=mebibytes * 1024 * 1024)


def in_hbm(array):
    return pltpu.with_memory_space_constraint(array, pltpu.HBM)


def cost(flops, size, exps=0):
    return pl.CostEstimate(flops=flops, bytes_accessed=size, transcendentals=exps)


def turned(left, right):
    return lax.dot_general(left, right, (((1,), (1,)), ((), ())), preferred_element_type=F32)


def pick_matrix(kinds, lanes, depth_step):
    period = 4 * lanes
    shape = (len(kinds) * lanes * depth_step, period * depth_step)
    row = lax.broadcasted_iota(jnp.int32, shape, 0)
    column = lax.broadcasted_iota(jnp.int32, shape, 1)
    source = row % depth_step * period + row // depth_step % lanes * 4 + kinds[0]
    source += row // (lanes * depth_step)
    return jnp.where(source == column, 1.0, 0.0).astype(BF16)


def split_kernel(lanes, plan, kinds, depth_step, order_ref, rows_ref, *rest):
    outs, pick = rest[:-1], rest[-1]
    depth = rows_ref.shape[1] // (4 * lanes)
    chunk = depth_step * 4 * lanes
    beside = 2 if depth % (2 * depth_step) == 0 else 1

    @pl.when(pl.program_id(0) == 0)
    def _():
        pick[...] = pick_matrix(kinds, lanes, depth_step)

    for first in range(0, depth, beside * depth_step):
        begin = first * 4 * lanes
        chunks = [
            rows_ref[0, begin + i * chunk : begin + (i + 1) * chunk, :] for i in range(beside)
        ]
        sorted_rows = jnp.dot(
            pick[...], jnp.concatenate(chunks, axis=1), preferred_element_type=F32
        ).astype(BF16)
        for i in range(beside):
            begin = first + i * depth_step
            for out, (start, stop, columns) in zip(outs, plan):
                if not start <= begin < stop:
                    continue
                to = slice(begin - start, begin - start + depth_step)
                for column, (kind, lane) in enumerate(columns):
                    at = (kinds.index(kind) * lanes + lane) * depth_step
                    out[0, to, column * HD : (column + 1) * HD] = sorted_rows[
                        at : at + depth_step, i * HD : (i + 1) * HD
                    ]


def split_blocks(rows, order, plan, lanes):
    depth = rows.shape[1] // (4 * lanes)
    ends = [depth] + [stop for _, stop, _ in plan]
    depth_step = max(
        n for n in (16, 32, 64) if n * 4 * lanes <= 256 and all(end % n == 0 for end in ends)
    )
    kinds = sorted({kind for _, _, columns in plan for kind, _ in columns})
    blocks = order.shape[0]
    shapes = [(blocks, stop - start, len(columns) * HD) for start, stop, columns in plan]
    return pl.pallas_call(
        functools.partial(split_kernel, lanes, plan, kinds, depth_step),
        grid_spec=pltpu.PrefetchScalarGridSpec(
            num_scalar_prefetch=1,
            grid=(blocks,),
            in_specs=[pl.BlockSpec((1,) + rows.shape[1:], lambda i, order: (order[i], 0, 0))],
            out_specs=[pl.BlockSpec((1,) + shape[1:], lambda i, order: (i, 0, 0)) for shape in shapes],
            scratch_shapes=[
                pltpu.VMEM((len(kinds) * lanes * depth_step, depth_step * 4 * lanes), BF16)
            ],
        ),
        out_shape=[jax.ShapeDtypeStruct(shape, BF16) for shape in shapes],
        compiler_params=params(16),
        cost_estimate=cost(0, 3 * blocks * rows.shape[1] * HD),
        name="split_blocks",
    )(order, in_hbm(rows))


def norm_kernel(tokens_ref, modulation_ref, out_ref):
    tokens = tokens_ref[...].astype(F32)
    center = jnp.mean(tokens, axis=1, keepdims=True)
    tokens = tokens - center
    spread = jnp.mean(tokens * tokens, axis=1, keepdims=True)
    normed = tokens * lax.rsqrt(spread + 1e-06)
    out_ref[...] = (normed * (1.0 + modulation_ref[0:1]) + modulation_ref[1:2]).astype(BF16)


def norm(tokens, modulation):
    patch, width = tokens.shape
    rows = 128
    return pl.pallas_call(
        norm_kernel,
        grid=(patch // rows,),
        in_specs=[
            pl.BlockSpec((rows, width), lambda i: (i, 0)),
            pl.BlockSpec((3, width), lambda i: (0, 0)),
        ],
        out_specs=pl.BlockSpec((rows, width), lambda i: (i, 0)),
        out_shape=jax.ShapeDtypeStruct((patch, width), BF16),
        compiler_params=params(14),
        cost_estimate=cost(10 * patch * width, 4 * patch * width),
        name="norm",
    )(in_hbm(tokens), modulation)


def attend_kernel(where_ref, normed_ref, matrix_ref, stale_ref, out_ref, own):
    patch = normed_ref.shape[0]
    parts = stale_ref.shape[1] // patch
    own[...] = jnp.dot(normed_ref[...], matrix_ref[...], preferred_element_type=F32).astype(BF16)
    starts = [
        pl.multiple_of(lax.rem(where_ref[0] + 1 + part, parts) * patch, patch)
        for part in range(parts - 1)
    ]
    scale = F32(np.log2(np.e) / np.sqrt(HD))
    keys = [stale_ref[0, pl.ds(start, patch), :] for start in starts] + [own[:, HD : 2 * HD]]
    values = [stale_ref[1, pl.ds(start, patch), :] for start in starts] + [own[:, 2 * HD :]]
    scores = [turned(own[:, :HD], key) for key in keys]
    top = jnp.max(functools.reduce(jnp.maximum, scores), axis=1, keepdims=True)
    total, summed = 0.0, 0.0
    for score, value in zip(scores, values):
        expo = jnp.exp2((score - top) * scale)
        total += expo
        summed += jnp.dot(expo.astype(BF16), value, preferred_element_type=F32)
    out_ref[...] = (summed / jnp.sum(total, axis=1, keepdims=True)).astype(BF16)


def attend(normed, matrix, where, stale, group, spot):
    patch, width = normed.shape
    heads, keys = len(group), stale.shape[1]
    first = group[0]
    return pl.pallas_call(
        attend_kernel,
        grid_spec=pltpu.PrefetchScalarGridSpec(
            num_scalar_prefetch=1,
            grid=(heads,),
            in_specs=[
                pl.BlockSpec((patch, width), lambda h, where: (0, 0)),
                pl.BlockSpec((width, 3 * HD), lambda h, where: (0, spot + h)),
                pl.BlockSpec((2, keys, HD), lambda h, where: (0, 0, first + h)),
            ],
            out_specs=pl.BlockSpec((patch, HD), lambda h, where: (0, h)),
            scratch_shapes=[pltpu.VMEM((patch, 3 * HD), BF16)],
        ),
        out_shape=jax.ShapeDtypeStruct((patch, heads * HD), BF16),
        compiler_params=params(32),
        cost_estimate=cost(
            2 * patch * heads * HD * (3 * width + 2 * keys), 2 * heads * HD * (3 * width + 2 * keys),
            patch * heads * keys,
        ),
        name="attend",
    )(where, in_hbm(normed), matrix, in_hbm(stale))


def output_kernel(attended_ref, matrix_ref, out_ref):
    out_ref[...] = turned(attended_ref[...], matrix_ref[...]).astype(BF16)


def output(attended, matrix):
    patch, inner = attended.shape
    rows = matrix.shape[0]
    step = 512 if rows % 512 == 0 else rows
    return pl.pallas_call(
        output_kernel,
        grid=(rows // step,),
        in_specs=[
            pl.BlockSpec((patch, inner), lambda i: (0, 0)),
            pl.BlockSpec((step, inner), lambda i: (i, 0)),
        ],
        out_specs=pl.BlockSpec((patch, step), lambda i: (0, i)),
        out_shape=jax.ShapeDtypeStruct((patch, rows), BF16),
        compiler_params=params(24),
        cost_estimate=cost(2 * patch * rows * inner, 2 * rows * (inner + patch)),
        name="output",
    )(attended, matrix)


def after(block, earlier):
    return lax.optimization_barrier((block, earlier))[0]


def swapped(block, axis, distance):
    return lax.ppermute(block, axis, [(i, i ^ distance) for i in range(lax.axis_size(axis))])


def handed_on(block):
    sections = lax.axis_size("section")
    return lax.ppermute(block, "section", [(i, (i + 1) % sections) for i in range(sections)])


def relayed(pieces):
    moved = lax.all_to_all(pieces, "section", split_axis=0, concat_axis=0, tiled=True)
    return moved.reshape(-1, moved.shape[2])


def local(block_weights, modulation, inflow, stale_cache, patch_index, assignment):
    sections, tp = lax.axis_size("section"), lax.axis_size("tp")
    rank = lax.axis_index("tp")
    blocks, depth, kinds, inner = block_weights.shape
    lanes = inner // HD
    share = inflow.shape[2]

    section_ids = jnp.arange(sections, dtype=jnp.int32)

    def block_of(section):
        return jnp.sum((assignment[None] == section[:, None]) * section_ids[None], axis=1)

    rows = block_weights.reshape(blocks, depth, kinds, lanes, HD)
    rows = rows.transpose(0, 1, 3, 2, 4).reshape(blocks, depth * lanes * kinds, HD)
    tokens = lax.all_gather(inflow[0], "tp", axis=1, tiled=True)

    def waiting(block, *earlier):
        return functools.reduce(after, earlier, block)

    order = block_of(section_ids)
    every = [(kind, head) for head in range(lanes) for kind in range(3)]
    (pieces,) = split_blocks(rows, order, [(0, depth, every)], lanes)
    part = depth * 2 // 3 // 16 * 16
    out_columns = [(3, head) for head in range(lanes)]
    out_plan = [(0, part, out_columns), (part, depth, out_columns)]
    first, second = split_blocks(rows, after(order, pieces), out_plan, lanes)

    matrix = relayed(pieces)
    normed = norm(tokens, modulation[0])
    to_out = relayed(waiting(first, matrix, normed))
    own = attend(normed, matrix, patch_index, stale_cache[0], tuple(range(lanes)), 0)
    product = output(own, to_out)
    rest = relayed(waiting(second, product))

    per = sections // tp
    gate = lax.dynamic_slice_in_dim(modulation[0, 2], rank * share, share, 0)

    mixed = lax.psum_scatter(product, "tp", scatter_dimension=1, tiled=True)
    product = output(own, rest)
    share = product.shape[1] // tp
    wanted = [
        lax.dynamic_slice_in_dim(product, (rank ^ distance) * share, share, 1)
        for distance in range(tp)
    ]
    wanted[1:] = [swapped(wanted[distance], "tp", distance) for distance in range(1, tp)]
    mixed_rest = sum(chunk.astype(F32) for chunk in wanted)

    def result(mixed, start, stop):
        columns = [slice(r * depth + start, r * depth + stop) for r in range(per)]
        patch = jnp.concatenate([inflow[0][:, cols] for cols in columns], axis=1)
        gates = jnp.concatenate([gate[cols] for cols in columns])
        made = handed_on((patch.astype(F32) + gates * mixed.astype(F32)).astype(BF16))
        return made

    second = result(mixed_rest, part, depth)
    first = result(waiting(mixed, second), 0, part)
    results = zip(jnp.split(first, per, axis=1), jnp.split(second, per, axis=1))
    return jnp.concatenate([piece for both in results for piece in both], axis=1)[None]


def solution(mesh):
    spread = (
        P(None, "section", None, "tp"),
        P("section", None, None),
        P("section", None, "tp"),
        P("section", None, None, "tp"),
        P("section"),
        P(),
    )
    return jax.shard_map(
        local, mesh=mesh, in_specs=spread, out_specs=P("section", None, "tp"), check_vma=False
    )
```

```python
import functools

import jax
import jax.numpy as jnp
import numpy as np
from jax import lax
from jax.experimental import pallas as pl
from jax.experimental.pallas import tpu as pltpu
from jax.sharding import PartitionSpec as P

HD = 128
F32 = jnp.float32
BF16 = jnp.bfloat16
WHOLE = pl.BlockSpec(memory_space=pltpu.VMEM)
ANYWHERE = pl.BlockSpec(memory_space=pl.ANY)
SCALAR = pl.BlockSpec(memory_space=pltpu.SMEM)


def params(mebibytes):
    return pltpu.CompilerParams(vmem_limit_bytes=mebibytes * 1024 * 1024)


def in_hbm(array):
    return pltpu.with_memory_space_constraint(array, pltpu.HBM)


def cost(flops, size, exps=0):
    return pl.CostEstimate(flops=flops, bytes_accessed=size, transcendentals=exps)


def turned(left, right):
    return lax.dot_general(left, right, (((1,), (1,)), ((), ())), preferred_element_type=F32)


def pick_matrix(kinds, lanes, depth_step):
    period = 4 * lanes
    shape = (len(kinds) * lanes * depth_step, period * depth_step)
    row = lax.broadcasted_iota(jnp.int32, shape, 0)
    column = lax.broadcasted_iota(jnp.int32, shape, 1)
    source = row % depth_step * period + row // depth_step % lanes * 4 + kinds[0]
    source += row // (lanes * depth_step)
    return jnp.where(source == column, 1.0, 0.0).astype(BF16)


def split_kernel(lanes, plan, kinds, depth_step, order_ref, rows_ref, *rest):
    outs, pick = rest[:-1], rest[-1]
    depth = rows_ref.shape[1] // (4 * lanes)
    chunk = depth_step * 4 * lanes
    beside = 2 if depth % (2 * depth_step) == 0 else 1

    @pl.when(pl.program_id(0) == 0)
    def _():
        pick[...] = pick_matrix(kinds, lanes, depth_step)

    for first in range(0, depth, beside * depth_step):
        begin = first * 4 * lanes
        chunks = [
            rows_ref[0, begin + i * chunk : begin + (i + 1) * chunk, :] for i in range(beside)
        ]
        sorted_rows = jnp.dot(
            pick[...], jnp.concatenate(chunks, axis=1), preferred_element_type=F32
        ).astype(BF16)
        for i in range(beside):
            begin = first + i * depth_step
            for out, (start, stop, columns) in zip(outs, plan):
                if not start <= begin < stop:
                    continue
                to = slice(begin - start, begin - start + depth_step)
                for column, (kind, lane) in enumerate(columns):
                    at = (kinds.index(kind) * lanes + lane) * depth_step
                    out[0, to, column * HD : (column + 1) * HD] = sorted_rows[
                        at : at + depth_step, i * HD : (i + 1) * HD
                    ]


def split_blocks(rows, order, plan, lanes):
    depth = rows.shape[1] // (4 * lanes)
    ends = [depth] + [stop for _, stop, _ in plan]
    depth_step = max(
        n for n in (16, 32, 64) if n * 4 * lanes <= 256 and all(end % n == 0 for end in ends)
    )
    kinds = sorted({kind for _, _, columns in plan for kind, _ in columns})
    blocks = order.shape[0]
    shapes = [(blocks, stop - start, len(columns) * HD) for start, stop, columns in plan]
    return pl.pallas_call(
        functools.partial(split_kernel, lanes, plan, kinds, depth_step),
        grid_spec=pltpu.PrefetchScalarGridSpec(
            num_scalar_prefetch=1,
            grid=(blocks,),
            in_specs=[pl.BlockSpec((1,) + rows.shape[1:], lambda i, order: (order[i], 0, 0))],
            out_specs=[pl.BlockSpec((1,) + shape[1:], lambda i, order: (i, 0, 0)) for shape in shapes],
            scratch_shapes=[
                pltpu.VMEM((len(kinds) * lanes * depth_step, depth_step * 4 * lanes), BF16)
            ],
        ),
        out_shape=[jax.ShapeDtypeStruct(shape, BF16) for shape in shapes],
        compiler_params=params(16),
        cost_estimate=cost(0, 3 * blocks * rows.shape[1] * HD),
        name="split_blocks",
    )(order, in_hbm(rows))


def norm_kernel(tokens_ref, modulation_ref, out_ref):
    tokens = tokens_ref[...].astype(F32)
    center = jnp.mean(tokens, axis=1, keepdims=True)
    tokens = tokens - center
    spread = jnp.mean(tokens * tokens, axis=1, keepdims=True)
    normed = tokens * lax.rsqrt(spread + 1e-06)
    out_ref[...] = (normed * (1.0 + modulation_ref[0:1]) + modulation_ref[1:2]).astype(BF16)


def norm(tokens, modulation):
    patch, width = tokens.shape
    rows = 128
    return pl.pallas_call(
        norm_kernel,
        grid=(patch // rows,),
        in_specs=[
            pl.BlockSpec((rows, width), lambda i: (i, 0)),
            pl.BlockSpec((3, width), lambda i: (0, 0)),
        ],
        out_specs=pl.BlockSpec((rows, width), lambda i: (i, 0)),
        out_shape=jax.ShapeDtypeStruct((patch, width), BF16),
        compiler_params=params(14),
        cost_estimate=cost(10 * patch * width, 4 * patch * width),
        name="norm",
    )(in_hbm(tokens), modulation)


def attend_kernel(where_ref, normed_ref, matrix_ref, stale_ref, out_ref, own):
    patch = normed_ref.shape[0]
    parts = stale_ref.shape[1] // patch
    own[...] = jnp.dot(normed_ref[...], matrix_ref[...], preferred_element_type=F32).astype(BF16)
    starts = [
        pl.multiple_of(lax.rem(where_ref[0] + 1 + part, parts) * patch, patch)
        for part in range(parts - 1)
    ]
    scale = F32(np.log2(np.e) / np.sqrt(HD))
    keys = [stale_ref[0, pl.ds(start, patch), :] for start in starts] + [own[:, HD : 2 * HD]]
    values = [stale_ref[1, pl.ds(start, patch), :] for start in starts] + [own[:, 2 * HD :]]
    scores = [turned(own[:, :HD], key) for key in keys]
    top = jnp.max(functools.reduce(jnp.maximum, scores), axis=1, keepdims=True)
    total, summed = 0.0, 0.0
    for score, value in zip(scores, values):
        expo = jnp.exp2((score - top) * scale)
        total += expo
        summed += jnp.dot(expo.astype(BF16), value, preferred_element_type=F32)
    out_ref[...] = (summed / jnp.sum(total, axis=1, keepdims=True)).astype(BF16)


def attend(normed, matrix, where, stale, group, spot):
    patch, width = normed.shape
    heads, keys = len(group), stale.shape[1]
    first = group[0]
    return pl.pallas_call(
        attend_kernel,
        grid_spec=pltpu.PrefetchScalarGridSpec(
            num_scalar_prefetch=1,
            grid=(heads,),
            in_specs=[
                pl.BlockSpec((patch, width), lambda h, where: (0, 0)),
                pl.BlockSpec((width, 3 * HD), lambda h, where: (0, spot + h)),
                pl.BlockSpec((2, keys, HD), lambda h, where: (0, 0, first + h)),
            ],
            out_specs=pl.BlockSpec((patch, HD), lambda h, where: (0, h)),
            scratch_shapes=[pltpu.VMEM((patch, 3 * HD), BF16)],
        ),
        out_shape=jax.ShapeDtypeStruct((patch, heads * HD), BF16),
        compiler_params=params(32),
        cost_estimate=cost(
            2 * patch * heads * HD * (3 * width + 2 * keys), 2 * heads * HD * (3 * width + 2 * keys),
            patch * heads * keys,
        ),
        name="attend",
    )(where, in_hbm(normed), matrix, in_hbm(stale))


def output_kernel(attended_ref, matrix_ref, out_ref):
    out_ref[...] = turned(attended_ref[...], matrix_ref[...]).astype(BF16)


def output(attended, matrix):
    patch, inner = attended.shape
    rows = matrix.shape[0]
    step = 256 if rows % 256 == 0 else rows
    return pl.pallas_call(
        output_kernel,
        grid=(rows // step,),
        in_specs=[
            pl.BlockSpec((patch, inner), lambda i: (0, 0)),
            pl.BlockSpec((step, inner), lambda i: (i, 0)),
        ],
        out_specs=pl.BlockSpec((patch, step), lambda i: (0, i)),
        out_shape=jax.ShapeDtypeStruct((patch, rows), BF16),
        compiler_params=params(24),
        cost_estimate=cost(2 * patch * rows * inner, 2 * rows * (inner + patch)),
        name="output",
    )(attended, matrix)


def after(block, earlier):
    return lax.optimization_barrier((block, earlier))[0]


def swapped(block, axis, distance):
    return lax.ppermute(block, axis, [(i, i ^ distance) for i in range(lax.axis_size(axis))])


def handed_on(block):
    sections = lax.axis_size("section")
    return lax.ppermute(block, "section", [(i, (i + 1) % sections) for i in range(sections)])


def relayed(pieces):
    moved = lax.all_to_all(pieces, "section", split_axis=0, concat_axis=0, tiled=True)
    return moved.reshape(-1, moved.shape[2])


def local(block_weights, modulation, inflow, stale_cache, patch_index, assignment):
    sections, tp = lax.axis_size("section"), lax.axis_size("tp")
    rank = lax.axis_index("tp")
    blocks, depth, kinds, inner = block_weights.shape
    lanes = inner // HD
    share = inflow.shape[2]

    section_ids = jnp.arange(sections, dtype=jnp.int32)

    def block_of(section):
        return jnp.sum((assignment[None] == section[:, None]) * section_ids[None], axis=1)

    rows = block_weights.reshape(blocks, depth, kinds, lanes, HD)
    rows = rows.transpose(0, 1, 3, 2, 4).reshape(blocks, depth * lanes * kinds, HD)
    tokens = lax.all_gather(inflow[0], "tp", axis=1, tiled=True)

    def waiting(block, *earlier):
        return functools.reduce(after, earlier, block)

    order = block_of(section_ids)
    every = [(kind, head) for head in range(lanes) for kind in range(3)]
    (pieces,) = split_blocks(rows, order, [(0, depth, every)], lanes)
    part = depth * 2 // 3 // 16 * 16
    out_columns = [(3, head) for head in range(lanes)]
    out_plan = [(0, part, out_columns), (part, depth, out_columns)]
    first, second = split_blocks(rows, after(order, pieces), out_plan, lanes)

    matrix = relayed(pieces)
    normed = norm(tokens, modulation[0])
    to_out = relayed(waiting(first, matrix, normed))
    own = attend(normed, matrix, patch_index, stale_cache[0], tuple(range(lanes)), 0)
    product = output(own, to_out)
    rest = relayed(waiting(second, product))

    per = sections // tp
    gate = lax.dynamic_slice_in_dim(modulation[0, 2], rank * share, share, 0)

    mixed = lax.psum_scatter(product, "tp", scatter_dimension=1, tiled=True)
    product = output(own, rest)
    share = product.shape[1] // tp
    wanted = [
        lax.dynamic_slice_in_dim(product, (rank ^ distance) * share, share, 1)
        for distance in range(tp)
    ]
    wanted[1:] = [swapped(wanted[distance], "tp", distance) for distance in range(1, tp)]
    mixed = waiting(mixed, *wanted[1:])
    mixed_rest = sum(chunk.astype(F32) for chunk in wanted)

    def result(mixed, start, stop):
        columns = [slice(r * depth + start, r * depth + stop) for r in range(per)]
        patch = jnp.concatenate([inflow[0][:, cols] for cols in columns], axis=1)
        gates = jnp.concatenate([gate[cols] for cols in columns])
        made = handed_on((patch.astype(F32) + gates * mixed.astype(F32)).astype(BF16))
        return jnp.split(made, per, axis=1)

    results = zip(result(mixed, 0, part), result(mixed_rest, part, depth))
    return jnp.concatenate([piece for both in results for piece in both], axis=1)[None]


def solution(mesh):
    spread = (
        P(None, "section", None, "tp"),
        P("section", None, None),
        P("section", None, "tp"),
        P("section", None, None, "tp"),
        P("section"),
        P(),
    )
    return jax.shard_map(
        local, mesh=mesh, in_specs=spread, out_specs=P("section", None, "tp"), check_vma=False
    )
```
